256 devices in a mesh: seq: 128 (over y, x, z), pair: 2 (over core).
Axes of the slice: x: 4, y: 4, z: 8, core: 2. Of those that a mesh axis runs over, the one named last changes fastest.
Arguments:
- tokens_in: bfloat16 [32768, 1024], P(('seq', 'pair')), may hold values from -24 to 24
- queries: bfloat16 [32768, 1024], P(('seq', 'pair')), may hold values from -500 to 500
- key_value: bfloat16 [32768, 128], P(('seq', 'pair')), may hold values from -6 to 6
- out_grad: bfloat16 [32768, 1024], P(('seq', 'pair')), may hold values from -1.25 to 1.25
- cluster_of: int32 [32768, 16], P(('seq', 'pair')), may hold values from 0 to 1023, as said below
- slot_of: int32 [32768, 16], P(('seq', 'pair')), may hold values from 0 to 1023, as said below
Outputs:
- weight_grad: float32 [1024, 1024], P(('seq', 'pair'))
The draws below stay inside these ranges and needn't reach their ends.
Inputs may be any that keep to these rules, and one draw needn't show every extreme that they name: `cluster_of`: cluster c belongs to owner group c // 8. Of the 2048 rows of one aligned block of 128 tokens, at most 32 name clusters of one owner group; in every draw some owner group receives exactly 32 rows from every block of even index and some from every block of odd index. No two rows share a cluster and a slot. Rows of the k-th aligned block of 128 tokens take slots of half k % 2, that is slot_of // 512 == k % 2. Half of all slots have a member in all; single clusters hold more or fewer.
All inputs are finite; a program needn't handle non-finite values.
Results may differ from the reference program's by a relative error of at most 0.0041.
Values may be sent and summed in bfloat16 or wider, within the bound.
A program may use at most 64 MiB of HBM per device.

```python
import jax
import jax.numpy as jnp
from jax import lax

D = 1024
H = 16
HD = 64
CAP = 1024
TOK_DEV = 128
HALF = 512
CL_DEV = 8
GROUPS = 128
BOUND = 32
TOKENS = 32768
CLUSTERS = 1024


def assign_rows(key):
    base_key = jax.random.fold_in(key, 17)
    split_keys = jax.random.split(base_key, 5)
    row_count = TOK_DEV * H
    device_count = 2 * GROUPS
    cell_count = GROUPS * BOUND
    starred = jax.random.randint(split_keys[0], (2,), 0, GROUPS)
    levels = jax.random.randint(split_keys[1], (2, GROUPS), 0, 4) * 256
    biases = levels + 4096 * (jnp.arange(GROUPS)[None, :] == starred[:, None]).astype(jnp.int32)
    noises = jax.random.randint(split_keys[2], (device_count, GROUPS, BOUND), 0, 256)
    parity = jnp.arange(device_count) % 2
    ranking = (biases[parity][:, :, None] + noises).reshape(device_count, cell_count)
    ranking = ranking * cell_count + jnp.arange(cell_count)[None, :]
    chosen = lax.top_k(ranking, row_count)[1]
    row_keys = jax.random.split(split_keys[3], device_count)
    shuffle = jax.vmap(lambda each: jax.random.permutation(each, row_count))(row_keys)
    chosen = jnp.take_along_axis(chosen, shuffle, axis=1)
    owners = chosen // BOUND
    within = chosen % BOUND
    sources = jnp.arange(device_count) // 2
    slot_keys = jax.random.split(split_keys[4], GROUPS * 2)
    tables = jax.vmap(lambda each: jax.random.permutation(each, cell_count))(slot_keys).reshape(GROUPS, 2, cell_count)
    local_slot = tables[owners, parity[:, None], sources[:, None] * BOUND + within]
    clusters = owners * CL_DEV + local_slot // HALF
    slots = parity[:, None] * HALF + local_slot % HALF
    return (clusters.reshape(TOKENS, H).astype(jnp.int32), slots.reshape(TOKENS, H).astype(jnp.int32))


def draw_cluster_of(key, part):
    return assign_rows(key)[0]


def draw_slot_of(key, part):
    return assign_rows(key)[1]


def draw_queries(key, part):
    base = jax.random.normal(jax.random.fold_in(key, 3), (TOKENS, H, HD), jnp.float32)
    values = jnp.clip(base, -6.0, 6.0)
    return values.reshape(TOKENS, H * HD).astype(jnp.bfloat16)


def with_spikes(entries, key, source, target, blocks, factor):
    owner, partner = [(jnp.arange(entries.shape[axis_at]) // (entries.shape[axis_at] // blocks)).reshape([-1 if axis == axis_at else 1 for axis in range(entries.ndim)]) for axis_at in (source, target)]
    chosen = jax.random.permutation(key, blocks)[partner]
    strong = (owner == chosen) | (owner == (partner + blocks // 2) % blocks)
    return jnp.where(strong, factor * entries, entries)


def block_levels(rng, shape, shards, smallest, top_value):
    def one(dim, shards_of):
        draws = jax.random.uniform(jax.random.fold_in(jax.random.fold_in(rng, 6), dim), (shards_of,), jnp.float32, smallest / len(shards), top_value / len(shards))
        return jnp.repeat(jnp.exp(draws), shape[dim] // shards_of).reshape((-1,) + (1,) * (len(shape) - dim - 1))

    factor_of = one(*shards[0])
    for cut in shards[1:]:
        factor_of = factor_of * one(*cut)
    return factor_of


def gaussian(own_key, extent, scale, limit, cuts=(), kind=jnp.bfloat16):
    drawn = scale * jax.random.normal(own_key, extent, jnp.float32)
    if cuts:
        drawn = drawn * block_levels(own_key, extent, cuts, -0.22, 0.18)
    return jnp.clip(drawn, -limit, limit).astype(kind)


def gaussian_with(stream_key, dims, width, bound, shards, heavy, held_as=jnp.bfloat16):
    drawn = width * jax.random.normal(stream_key, dims, jnp.float32)
    if shards:
        drawn = drawn * block_levels(stream_key, dims, shards, -0.22, 0.18)
    return jnp.clip(with_spikes(drawn, jax.random.fold_in(stream_key, 3), *heavy), -bound, bound).astype(held_as)


def setup_inputs(seed: int = 0) -> dict:
    key_of = jax.random.split(jax.random.key(seed), 7)
    tokens_in = gaussian_with(key_of[0], (TOKENS, D), 1.0, 24.0, ((0, 256),), (0, 1, 256, 6.0))
    queries = draw_queries(jax.random.fold_in(key_of[6], 71), 0)
    key_value = gaussian(key_of[2], (TOKENS, 2 * HD), 1.0, 6.0, ((0, 256),))
    out_grad = gaussian(key_of[3], (TOKENS, H * HD), (16.0 / TOKENS ** 0.5), 1.25, ((0, 256),))
    cluster_of = draw_cluster_of(jax.random.fold_in(key_of[6], 71), 0)
    slot_of = draw_slot_of(jax.random.fold_in(key_of[6], 71), 0)
    return {"tokens_in": tokens_in, "queries": queries, "key_value": key_value, "out_grad": out_grad, "cluster_of": cluster_of, "slot_of": slot_of}


def cluster_grad(query_part, key_part, live_keys):
    score_scale = HD ** (-0.5)
    query_rows = query_part[:, :HD]
    grad_rows = query_part[:, HD:]
    key_rows = key_part[:, :HD]
    value_rows = key_part[:, HD:]
    scores = jnp.dot(query_rows, key_rows.T, preferred_element_type=jnp.float32) * score_scale
    scores = jnp.where(live_keys[None, :] > 0, scores, jnp.float32(-1e+30))
    row_max = lax.optimization_barrier(jnp.max(scores, axis=1, keepdims=True))
    weights = jnp.exp(scores - row_max)
    probs = weights / lax.optimization_barrier(jnp.sum(weights, axis=1, keepdims=True))
    prob_grad = jnp.dot(grad_rows, value_rows.T, preferred_element_type=jnp.float32)
    row_dot = lax.optimization_barrier(jnp.sum(probs * prob_grad, axis=1, keepdims=True))
    score_grad = (probs * (prob_grad - row_dot) * score_scale).astype(jnp.bfloat16)
    return jnp.dot(score_grad, key_rows, preferred_element_type=jnp.float32).astype(jnp.bfloat16)

def reference(tokens_in, queries, key_value, out_grad, cluster_of, slot_of):
    row_count = TOKENS * H
    flat_place = (cluster_of * CAP + slot_of).reshape(row_count).astype(jnp.int32)
    members = jnp.full((CLUSTERS * CAP,), -1, jnp.int32).at[flat_place].set(jnp.arange(row_count, dtype=jnp.int32))
    paired_rows = jnp.concatenate([queries.reshape(row_count, HD), out_grad.reshape(row_count, HD)], axis=1)

    def one_cluster(cluster):
        member_rows = lax.dynamic_slice_in_dim(members, (cluster * CAP).astype(jnp.int32), CAP)
        present = member_rows >= 0
        safe_rows = jnp.where(present, member_rows, 0)
        query_part = jnp.where(present[:, None], paired_rows[safe_rows], jnp.zeros((), paired_rows.dtype))
        key_part = jnp.where(present[:, None], key_value[safe_rows // H], jnp.zeros((), key_value.dtype))
        return cluster_grad(query_part, key_part, present.astype(jnp.float32))
    cluster_grads = lax.map(one_cluster, jnp.arange(CLUSTERS, dtype=jnp.int32))
    query_grad = cluster_grads.reshape(CLUSTERS * CAP, HD)[flat_place].reshape(TOKENS, H * HD)
    return jnp.dot(tokens_in.T, query_grad, preferred_element_type=jnp.float32)
```

```python
import functools

import jax
import jax.numpy as jnp
from jax import lax
from jax.experimental import pallas as pl
from jax.experimental.pallas import tpu as pltpu
from jax.sharding import PartitionSpec as P

H = 16
HD = 64
HALF = 512
CL_DEV = 8
TOK = 128
ROWS = TOK * H
SLOTS = CL_DEV * HALF
GROUPS = 128
BOUND = 32
PLANE = 16
DEPTH = 8
CHUNKS = 8
PER = GROUPS // CHUNKS
MESH = pl.DeviceIdType.MESH
F32 = jnp.float32
BF16 = jnp.bfloat16
VMEM = pl.BlockSpec(memory_space=pltpu.VMEM)


def params(collective=None):
    if collective is None:
        return pltpu.CompilerParams(vmem_limit_bytes=56 * 2**20)
    return pltpu.CompilerParams(
        vmem_limit_bytes=56 * 2**20, collective_id=collective, has_side_effects=True
    )


def iota(shape, dim):
    return lax.broadcasted_iota(jnp.int32, shape, dim)


def one_hot(mask):
    return jnp.where(mask, 1.0, 0.0).astype(BF16)


def dot(a, b):
    return jnp.dot(a, b, preferred_element_type=F32)


def dot_t(a, b):
    return lax.dot_general(a, b, (((1,), (1,)), ((), ())), preferred_element_type=F32)


def t_dot(a, b):
    return lax.dot_general(a, b, (((0,), (0,)), ((), ())), preferred_element_type=F32)


def pack_kernel(idx_ref, q_ref, g_ref, kv_ref, out_ref, lab_ref, cell_ref, rows_ref, pick_ref):
    cluster = idx_ref[0:1, :]
    slot = idx_ref[1:2, :]
    owner = lax.shift_right_logical(cluster, 3)
    local = (cluster & (CL_DEV - 1)) * HALF + (slot & (HALF - 1))
    pick_ref[...] = jnp.where(iota((GROUPS, ROWS), 0) == owner, 1.0, 0.0)
    before = one_hot(iota((TOK, TOK), 0) < iota((TOK, TOK), 1))
    base = jnp.zeros((GROUPS, 1), F32)
    ranks = []
    for h in range(H):
        pick = pick_ref[:, h * TOK : (h + 1) * TOK]
        count = dot(pick.astype(BF16), before) + base
        ranks.append(jnp.sum(pick * count, axis=0, keepdims=True))
        base = base + jnp.sum(pick, axis=1, keepdims=True)
    rank = jnp.concatenate(ranks, axis=1).astype(jnp.int32)
    cell = owner * BOUND + rank
    cell_ref[0:1, :] = cell
    at_rank = one_hot(iota((TOK, ROWS), 0) == rank)
    pick = pick_ref[...]
    high = dot_t((pick * lax.shift_right_logical(local, 6).astype(F32)).astype(BF16), at_rank)
    low = dot_t((pick * (local & 63).astype(F32)).astype(BF16), at_rank)
    live = dot_t(pick.astype(BF16), at_rank)
    label = jnp.where(live > 0.5, high * 64.0 + low, -1.0).astype(jnp.int32)
    for o in range(GROUPS):
        lab_ref[o] = label[o : o + 1, :]
    for h in range(H):
        cut = slice(h * HD, (h + 1) * HD)
        rows_ref[h * TOK : (h + 1) * TOK, :] = jnp.concatenate(
            [q_ref[:, cut], g_ref[:, cut], kv_ref[...]], axis=1
        )

    def step(c, carry):
        hot = one_hot(iota((256, ROWS), 0) == cell - c * 256)
        out_ref[pl.ds(c * 8, 8)] = dot(hot, rows_ref[...]).astype(BF16).reshape(8, BOUND, 4 * HD)
        return carry

    lax.fori_loop(0, GROUPS * BOUND // 256, step, 0)


def pack(idx, queries, out_grad, key_value):
    return pl.pallas_call(
        pack_kernel,
        out_shape=(
            jax.ShapeDtypeStruct((GROUPS, BOUND, 4 * HD), BF16),
            jax.ShapeDtypeStruct((GROUPS, 1, 128), jnp.int32),
            jax.ShapeDtypeStruct((1, ROWS), jnp.int32),
        ),
        in_specs=[VMEM] * 4,
        out_specs=(VMEM,) * 3,
        scratch_shapes=[pltpu.VMEM((ROWS, 4 * HD), BF16), pltpu.VMEM((GROUPS, ROWS), F32)],
        compiler_params=params(),
    )(idx, queries, out_grad, key_value)


def greet_all(seq, pair):
    barrier = pltpu.get_barrier_semaphore()

    def hello(i, carry):
        pl.semaphore_signal(
            barrier, inc=1, device_id=(lax.rem(seq + i, GROUPS), pair), device_id_type=MESH
        )
        return carry

    lax.fori_loop(1, GROUPS, hello, 0)
    return barrier


def forward_kernel(
    out_ref, lab_ref, qg_ref, kv_ref, live_ref, lane_ref, rows_ref, labs_ref, total_ref,
    send_sem, lsend_sem, recv_sem, lrecv_sem, own_sem,
):
    seq, pair = lax.axis_index("seq"), lax.axis_index("pair")
    barrier = greet_all(seq, pair)
    own = pltpu.make_async_copy(out_ref.at[seq], rows_ref.at[0], own_sem.at[0])
    own.start()
    own_lab = pltpu.make_async_copy(lab_ref.at[seq], labs_ref.at[0], own_sem.at[1])
    own_lab.start()
    pl.semaphore_wait(barrier, GROUPS - 1)

    def send(i, carry):
        to = lax.rem(seq + i, GROUPS)
        pltpu.make_async_remote_copy(
            src_ref=lab_ref.at[to], dst_ref=labs_ref.at[i], send_sem=lsend_sem, recv_sem=lrecv_sem,
            device_id=(to, pair), device_id_type=MESH,
        ).start()
        pltpu.make_async_remote_copy(
            src_ref=out_ref.at[to], dst_ref=rows_ref.at[i], send_sem=send_sem,
            recv_sem=recv_sem.at[i // PER], device_id=(to, pair), device_id_type=MESH,
        ).start()
        return carry

    lax.fori_loop(1, GROUPS, send, 0)
    own.wait()
    own_lab.wait()
    rest = pl.ds(1, GROUPS - 1)
    labels_done = pltpu.make_async_remote_copy(
        src_ref=lab_ref.at[rest], dst_ref=labs_ref.at[rest], send_sem=lsend_sem, recv_sem=lrecv_sem,
        device_id=(seq, pair), device_id_type=MESH,
    )
    labels_done.wait_recv()
    live = jnp.zeros((SLOTS // 128, 128), F32)
    for k in range(CHUNKS):
        lane = jnp.concatenate(
            [labs_ref[i, :, 0:BOUND] for i in range(k * PER, (k + 1) * PER)], axis=1
        )
        lane_ref[k : k + 1, :] = lane
        width = PER * BOUND
        live = live + dot_t(
            one_hot(iota((SLOTS // 128, width), 0) == lax.shift_right_arithmetic(lane, 7)),
            one_hot(iota((128, width), 0) == (lane & 127)),
        )
        part = pl.ds(max(1, k * PER), PER - (k == 0))
        pltpu.make_async_remote_copy(
            src_ref=out_ref.at[part], dst_ref=rows_ref.at[part], send_sem=send_sem,
            recv_sem=recv_sem.at[k], device_id=(seq, pair), device_id_type=MESH,
        ).wait_recv()
        rows = rows_ref[k * PER : (k + 1) * PER].reshape(width, 4 * HD)

        def add(b, carry, k=k, lane=lane, rows=rows):
            hot = one_hot(iota((HALF, width), 0) == lane - b * HALF)
            term = dot(hot, rows)
            if k == 0:
                total_ref[b] = term
            elif k < CHUNKS - 1:
                total_ref[b] += term
            else:
                done = (total_ref[b] + term).astype(BF16)
                qg_ref[b] = done[:, : 2 * HD]
                kv_ref[b] = done[:, 2 * HD :]
            return carry

        lax.fori_loop(0, CL_DEV, add, 0)
    for c in range(CL_DEV):
        live_ref[c] = live[4 * c : 4 * c + 4, :]
    labels_done.wait_send()
    pltpu.make_async_remote_copy(
        src_ref=out_ref.at[rest], dst_ref=rows_ref.at[rest], send_sem=send_sem,
        recv_sem=recv_sem.at[0], device_id=(seq, pair), device_id_type=MESH,
    ).wait_send()


def forward(outgoing, labels):
    return pl.pallas_call(
        forward_kernel,
        out_shape=(
            jax.ShapeDtypeStruct((CL_DEV, HALF, 2 * HD), BF16),
            jax.ShapeDtypeStruct((CL_DEV, HALF, 2 * HD), BF16),
            jax.ShapeDtypeStruct((CL_DEV, 4, 128), F32),
            jax.ShapeDtypeStruct((CHUNKS, PER * BOUND), jnp.int32),
        ),
        in_specs=[VMEM] * 2,
        out_specs=(VMEM,) * 4,
        scratch_shapes=[
            pltpu.VMEM((GROUPS, BOUND, 4 * HD), BF16),
            pltpu.VMEM((GROUPS, 1, 128), jnp.int32),
            pltpu.VMEM((CL_DEV, HALF, 4 * HD), F32),
            pltpu.SemaphoreType.DMA,
            pltpu.SemaphoreType.DMA,
            pltpu.SemaphoreType.DMA((CHUNKS,)),
            pltpu.SemaphoreType.DMA,
            pltpu.SemaphoreType.DMA((2,)),
        ],
        compiler_params=params(0),
    )(outgoing, labels)


def attend_kernel(
    qg_ref, kv_ref, live_ref, lane_ref, back_ref, kv2_ref, live2_ref, s_ref, d_ref, w_ref, grads_ref,
    send_sem, recv_sem,
):
    seq, pair = lax.axis_index("seq"), lax.axis_index("pair")
    other = (seq, 1 - pair)
    barrier = pltpu.get_barrier_semaphore()
    pl.semaphore_signal(barrier, inc=1, device_id=other, device_id_type=MESH)
    pl.semaphore_wait(barrier, 1)

    def copy_of(c):
        return pltpu.make_async_remote_copy(
            src_ref=kv_ref.at[c], dst_ref=kv2_ref.at[c], send_sem=send_sem.at[c],
            recv_sem=recv_sem.at[c], device_id=other, device_id_type=MESH,
        )

    live_copy = pltpu.make_async_remote_copy(
        src_ref=live_ref, dst_ref=live2_ref, send_sem=send_sem.at[CL_DEV],
        recv_sem=recv_sem.at[CL_DEV], device_id=other, device_id_type=MESH,
    )
    live_copy.start()
    for c in range(CL_DEV):
        copy_of(c).start()
    live_copy.wait()

    for c in range(CL_DEV):
        copy_of(c).wait()
        queries = qg_ref[c, :, :HD] * BF16(HD**-0.5)
        grads = qg_ref[c, :, HD:]
        keys = jnp.concatenate([kv_ref[c, :, :HD], kv2_ref[c, :, :HD]], axis=0)
        values = jnp.concatenate([kv_ref[c, :, HD:], kv2_ref[c, :, HD:]], axis=0)
        alive = jnp.concatenate(
            [ref[c, r : r + 1, :] for ref in (live_ref, live2_ref) for r in range(4)], axis=1
        )
        bias = jnp.where(alive > 0.5, 0.0, -1e30)
        s_ref[...] = dot_t(queries, keys)
        d_ref[...] = dot_t(grads, values)

        def rows(r, carry, bias=bias):
            at = pl.ds(pl.multiple_of(r * 32, 32), 32)
            scores = s_ref[at, :] + bias
            weights = jnp.exp(scores - jnp.max(scores, axis=1, keepdims=True))
            inverse = 1.0 / jnp.sum(weights, axis=1, keepdims=True)
            prob_grad = d_ref[at, :]
            row_dot = jnp.sum(weights * prob_grad, axis=1, keepdims=True) * inverse
            w_ref[at, :] = (
                weights * (prob_grad - row_dot) * (inverse * (HD**-0.5))
            ).astype(BF16)
            return carry

        lax.fori_loop(0, HALF // 32, rows, 0)
        place = slice((c % 2) * HALF, (c % 2 + 1) * HALF)
        column = slice((c // 2) * HD, (c // 2 + 1) * HD)
        grads_ref[place, column] = dot(w_ref[...], keys).astype(BF16)

    width = PER * BOUND
    for k in range(CHUNKS):
        labels = jnp.broadcast_to(lane_ref[k : k + 1, :], (128, width)).T
        low = labels & 1023
        hot = jnp.concatenate(
            [one_hot(low == iota((width, 128), 1) + 128 * b) for b in range(8)], axis=1
        )
        found = dot(hot, grads_ref[...])
        high = lax.shift_right_arithmetic(labels[:, :HD], 10)
        row = jnp.zeros((width, HD), F32)
        for a in range(4):
            row = row + jnp.where(high == a, found[:, a * HD : (a + 1) * HD], 0.0)
        row = row.reshape(PER, BOUND, HD)
        back_ref[k * PER : (k + 1) * PER] = jnp.concatenate(
            [row[:, : BOUND // 2], row[:, BOUND // 2 :]], axis=2
        ).astype(BF16)


def attend(qg, kv, live, lane):
    return pl.pallas_call(
        attend_kernel,
        out_shape=jax.ShapeDtypeStruct((GROUPS, BOUND // 2, 2 * HD), BF16),
        in_specs=[VMEM] * 4,
        out_specs=VMEM,
        scratch_shapes=[
            pltpu.VMEM((CL_DEV, HALF, 2 * HD), BF16),
            pltpu.VMEM((CL_DEV, 4, 128), F32),
            pltpu.VMEM((HALF, 2 * HALF), F32),
            pltpu.VMEM((HALF, 2 * HALF), F32),
            pltpu.VMEM((HALF, 2 * HALF), BF16),
            pltpu.VMEM((2 * HALF, 4 * HD), BF16),
            pltpu.SemaphoreType.DMA((CL_DEV + 1,)),
            pltpu.SemaphoreType.DMA((CL_DEV + 1,)),
        ],
        compiler_params=params(1),
    )(qg, kv, live, lane)


def reduce_kernel(
    back_ref, cell_ref, x_ref, out_ref, got_ref, xp_ref, g_ref, xo_ref, go_ref, part_ref, plane_ref,
    line_ref, lined_ref, send_sem, recv_sem, own_sem, psend_sem, precv_sem, ysend_sem, yrecv_sem,
    zsend_sem, zrecv_sem,
):
    seq, pair = lax.axis_index("seq"), lax.axis_index("pair")
    other = (seq, 1 - pair)
    yx, z = seq // DEPTH, lax.rem(seq, DEPTH)
    barrier = greet_all(seq, pair)
    pl.semaphore_signal(barrier, inc=1, device_id=other, device_id_type=MESH)
    own = pltpu.make_async_copy(back_ref.at[0], got_ref.at[0], own_sem)
    own.start()
    pl.semaphore_wait(barrier, GROUPS)

    def send(i, carry):
        to = lax.rem(seq + (GROUPS - i), GROUPS)
        pltpu.make_async_remote_copy(
            src_ref=back_ref.at[i], dst_ref=got_ref.at[i], send_sem=send_sem, recv_sem=recv_sem,
            device_id=(to, pair), device_id_type=MESH,
        ).start()
        return carry

    lax.fori_loop(1, GROUPS, send, 0)
    position = iota((1024, 512), 1)
    for p in range(2):
        column = lax.shift_right_logical(position, 2) * 8 + 4 * p + (position & 3)
        xp_ref[p] = dot(x_ref[...], one_hot(iota((1024, 512), 0) == column)).astype(BF16)
    x_copy = pltpu.make_async_remote_copy(
        src_ref=xp_ref.at[1 - pair], dst_ref=xo_ref, send_sem=psend_sem.at[0],
        recv_sem=precv_sem.at[0], device_id=other, device_id_type=MESH,
    )
    x_copy.start()
    own.wait()
    rest = pl.ds(1, GROUPS - 1)
    pltpu.make_async_remote_copy(
        src_ref=back_ref.at[rest], dst_ref=got_ref.at[rest], send_sem=send_sem, recv_sem=recv_sem,
        device_id=other, device_id_type=MESH,
    ).wait()
    got = got_ref[...].reshape(GROUPS * BOUND // 2, 2 * HD)
    for h in range(0, H, 2):
        pieces = []
        for e in range(2):
            cell = cell_ref[0:1, (h + e) * TOK : (h + e + 1) * TOK]
            cell = jnp.broadcast_to(cell, (TOK, TOK)).T
            offset = lax.rem(lax.shift_right_logical(cell, 5) + (GROUPS - seq), GROUPS)
            target = offset * (BOUND // 2) + (cell & (BOUND // 2 - 1))
            hot = jnp.concatenate(
                [one_hot(target == iota((TOK, 128), 1) + 128 * b) for b in range(16)], axis=1
            )
            found = dot(hot, got)
            upper = (cell[:, :HD] & (BOUND // 2)) > 0
            pieces.append(jnp.where(upper, found[:, HD:], found[:, :HD]))
        g_ref[:, h * HD : (h + 2) * HD] = jnp.concatenate(pieces, axis=1).astype(BF16)
    g_copy = pltpu.make_async_remote_copy(
        src_ref=g_ref, dst_ref=go_ref, send_sem=psend_sem.at[1], recv_sem=precv_sem.at[1],
        device_id=other, device_id_type=MESH,
    )
    g_copy.start()
    x_copy.wait()
    g_copy.wait()
    left, right = xp_ref[pair], xo_ref[...]
    for b in range(4):
        cut = slice(b * 128, (b + 1) * 128)
        term = t_dot(left[:, cut], g_ref[...]) + t_dot(right[:, cut], go_ref[...])
        part_ref[b * 4 : (b + 1) * 4] = term.astype(BF16).reshape(4, 32, 1024)

    def plane_copy(i):
        to = lax.rem(yx + i, PLANE)
        return pltpu.make_async_remote_copy(
            src_ref=part_ref.at[to], dst_ref=plane_ref.at[i - 1], send_sem=ysend_sem.at[i - 1],
            recv_sem=yrecv_sem.at[i - 1], device_id=(to * DEPTH + z, pair), device_id_type=MESH,
        )

    for i in range(1, PLANE):
        plane_copy(i).start()
    total = part_ref[yx].astype(F32)
    for i in range(1, PLANE):
        plane_copy(i).wait_recv()
        total = total + plane_ref[i - 1].astype(F32)
    for i in range(DEPTH):
        rows = total[4 * i : 4 * i + 4, :]
        line_ref[i] = jnp.concatenate([rows[:, :512], rows[:, 512:]], axis=0)

    def line_copy(i):
        to = lax.rem(z + i, DEPTH)
        return pltpu.make_async_remote_copy(
            src_ref=line_ref.at[to], dst_ref=lined_ref.at[i - 1], send_sem=zsend_sem.at[i - 1],
            recv_sem=zrecv_sem.at[i - 1], device_id=(yx * DEPTH + to, pair), device_id_type=MESH,
        )

    for i in range(1, DEPTH):
        line_copy(i).start()
    result = line_ref[z]
    for i in range(1, DEPTH):
        line_copy(i).wait_recv()
        result = result + lined_ref[i - 1]
    out_ref[...] = jnp.concatenate([result[:4], result[4:]], axis=1)
    for i in range(1, PLANE):
        plane_copy(i).wait_send()
    for i in range(1, DEPTH):
        line_copy(i).wait_send()


def reduce(back, cell, tokens_in):
    return pl.pallas_call(
        reduce_kernel,
        out_shape=jax.ShapeDtypeStruct((4, 1024), F32),
        in_specs=[VMEM] * 3,
        out_specs=VMEM,
        scratch_shapes=[
            pltpu.VMEM((GROUPS, BOUND // 2, 2 * HD), BF16),
            pltpu.VMEM((2, TOK, 512), BF16),
            pltpu.VMEM((TOK, 1024), BF16),
            pltpu.VMEM((TOK, 512), BF16),
            pltpu.VMEM((TOK, 1024), BF16),
            pltpu.VMEM((PLANE, 32, 1024), BF16),
            pltpu.VMEM((PLANE - 1, 32, 1024), BF16),
            pltpu.VMEM((DEPTH, 8, 512), F32),
            pltpu.VMEM((DEPTH - 1, 8, 512), F32),
            pltpu.SemaphoreType.DMA,
            pltpu.SemaphoreType.DMA,
            pltpu.SemaphoreType.DMA,
            pltpu.SemaphoreType.DMA((2,)),
            pltpu.SemaphoreType.DMA((2,)),
            pltpu.SemaphoreType.DMA((PLANE - 1,)),
            pltpu.SemaphoreType.DMA((PLANE - 1,)),
            pltpu.SemaphoreType.DMA((DEPTH - 1,)),
            pltpu.SemaphoreType.DMA((DEPTH - 1,)),
        ],
        compiler_params=params(2),
    )(back, cell, tokens_in)


def on_device(tokens_in, queries, key_value, out_grad, cluster_of, slot_of):
    idx = jnp.stack([cluster_of.T.reshape(ROWS), slot_of.T.reshape(ROWS)])
    outgoing, labels, cell = pack(idx, queries, out_grad, key_value)
    qg, kv, live, lane = forward(outgoing, labels)
    back = attend(qg, kv, live, lane)
    return reduce(back, cell, tokens_in)


def solution(mesh):
    spec = P(("seq", "pair"), None)
    return jax.shard_map(
        on_device, mesh=mesh, in_specs=(spec,) * 6, out_specs=spec, check_vma=False
    )
```

```python
import functools

import jax
import jax.numpy as jnp
from jax import lax
from jax.experimental import pallas as pl
from jax.experimental.pallas import tpu as pltpu
from jax.sharding import PartitionSpec as P

H = 16
HD = 64
HALF = 512
CL_DEV = 8
TOK = 128
ROWS = TOK * H
SLOTS = CL_DEV * HALF
GROUPS = 128
BOUND = 32
PLANE = 16
DEPTH = 8
ORDER = [0, 1, 7, 2, 6, 3, 5, 4]
LAG = 2
MESH = pl.DeviceIdType.MESH
F32 = jnp.float32
BF16 = jnp.bfloat16
VMEM = pl.BlockSpec(memory_space=pltpu.VMEM)


def params(collective=None):
    if collective is None:
        return pltpu.CompilerParams(vmem_limit_bytes=56 * 2**20)
    return pltpu.CompilerParams(
        vmem_limit_bytes=56 * 2**20, collective_id=collective, has_side_effects=True
    )


def iota(shape, dim):
    return lax.broadcasted_iota(jnp.int32, shape, dim)


def one_hot(mask):
    return jnp.where(mask, 1.0, 0.0).astype(BF16)


def dot(a, b):
    return jnp.dot(a, b, preferred_element_type=F32)


def dot_t(a, b):
    return lax.dot_general(a, b, (((1,), (1,)), ((), ())), preferred_element_type=F32)


def t_dot(a, b):
    return lax.dot_general(a, b, (((0,), (0,)), ((), ())), preferred_element_type=F32)


def neighbours(seq, pair, with_other):
    yx, z = seq // DEPTH, lax.rem(seq, DEPTH)
    barrier = pltpu.get_barrier_semaphore()
    for i in range(1, DEPTH):
        to = yx * DEPTH + lax.rem(z + i, DEPTH)
        pl.semaphore_signal(barrier, inc=1, device_id=(to, pair), device_id_type=MESH)
    for m in range(1, PLANE):
        to = lax.rem(yx + m, PLANE) * DEPTH + z
        pl.semaphore_signal(barrier, inc=1, device_id=(to, pair), device_id_type=MESH)
    if with_other:
        pl.semaphore_signal(barrier, inc=1, device_id=(seq, 1 - pair), device_id_type=MESH)
    return barrier, DEPTH - 1 + PLANE - 1 + with_other


def forward_kernel(
    idx_ref, q_ref, g_ref, kvin_ref, qg_ref, kv_ref, live_ref, lane_ref, cell_ref,
    flat_ref, pick_ref, zsend_ref, zgot_ref, zkv_ref, zlab_ref, zlabgot_ref, group_ref, plab_ref,
    fwd_ref, rows_ref, total_ref, zsend_sem, zrecv_sem, lsend_sem, lrecv_sem, psend_sem, precv_sem,
):
    seq, pair = lax.axis_index("seq"), lax.axis_index("pair")
    yx, z = seq // DEPTH, lax.rem(seq, DEPTH)
    barrier, answers = neighbours(seq, pair, 0)

    cluster = idx_ref[0:1, :]
    slot = idx_ref[1:2, :]
    owner = lax.shift_right_logical(cluster, 3)
    local = (cluster & (CL_DEV - 1)) * HALF + (slot & (HALF - 1))
    pick_ref[...] = jnp.where(iota((GROUPS, ROWS), 0) == owner, 1.0, 0.0)
    before = one_hot(iota((TOK, TOK), 0) < iota((TOK, TOK), 1))
    base = jnp.zeros((GROUPS, 1), F32)
    ranks = []
    for h in range(H):
        pick = pick_ref[:, h * TOK : (h + 1) * TOK]
        count = dot(pick.astype(BF16), before) + base
        ranks.append(jnp.sum(pick * count, axis=0, keepdims=True))
        base = base + jnp.sum(pick, axis=1, keepdims=True)
    rank = jnp.concatenate(ranks, axis=1).astype(jnp.int32)
    cell_ref[0:1, :] = owner * BOUND + rank
    place = (owner & (DEPTH - 1)) * (PLANE * BOUND) + lax.shift_right_logical(owner, 3) * BOUND + rank
    in_row = jnp.where(iota((32, ROWS), 0) == lax.shift_right_logical(place, 7), 1.0, 0.0)
    in_lane = one_hot(iota((128, ROWS), 0) == (place & 127))
    token = iota((1, ROWS), 1) & (TOK - 1)
    parts = [lax.shift_right_logical(local, 6), local & 63, token]
    stacked = [(in_row * part.astype(F32)).astype(BF16) for part in parts] + [in_row.astype(BF16)]
    found = dot_t(jnp.concatenate(stacked, axis=0), in_lane)
    label = jnp.where(
        found[96:128] > 0.5, (found[0:32] * 64.0 + found[32:64]) * 128.0 + found[64:96], -1.0
    ).astype(jnp.int32)
    for i in range(DEPTH):
        zlab_ref[i] = label[4 * i : 4 * i + 4, :]
    for h in range(H):
        cut = slice(h * HD, (h + 1) * HD)
        flat_ref[h * TOK : (h + 1) * TOK, :] = jnp.concatenate([q_ref[:, cut], g_ref[:, cut]], axis=1)

    def z_copy(i, kind):
        to = lax.rem(z + i, DEPTH)
        source, target = (
            (zlab_ref.at[to], zlabgot_ref.at[i]),
            (kvin_ref, zkv_ref.at[i]),
            (zsend_ref.at[i], zgot_ref.at[i]),
        )[kind]
        return pltpu.make_async_remote_copy(
            src_ref=source, dst_ref=target, send_sem=zsend_sem.at[i, kind],
            recv_sem=zrecv_sem.at[i, kind], device_id=(yx * DEPTH + to, pair), device_id_type=MESH,
        )

    pl.semaphore_wait(barrier, answers)
    for kind in range(2):
        for i in ORDER[1:]:
            z_copy(i, kind).start()
    for i in ORDER[1:] + ORDER[:1]:
        to = lax.rem(z + i, DEPTH)
        hot = one_hot(iota((PLANE * BOUND, ROWS), 0) == place - to * (PLANE * BOUND))
        zsend_ref[i] = dot(hot, flat_ref[...]).astype(BF16)
        if i:
            z_copy(i, 2).start()
    zlabgot_ref[0] = zlab_ref[z]
    for i in ORDER[1:]:
        z_copy(i, 0).wait_recv()
    for i in range(DEPTH):
        for g in range(4):
            group_ref[g, i : i + 1, :] = zlabgot_ref[i, g : g + 1, :]

    def label_copy(m):
        to = lax.rem(yx + m, PLANE)
        return pltpu.make_async_remote_copy(
            src_ref=group_ref.at[to // 4], dst_ref=plab_ref.at[m], send_sem=lsend_sem.at[m],
            recv_sem=lrecv_sem.at[m], device_id=(to * DEPTH + z, pair), device_id_type=MESH,
        )

    for m in range(1, PLANE):
        label_copy(m).start()
    plab_ref[0] = group_ref[yx // 4]

    def row_copy(i, m):
        to = lax.rem(yx + m, PLANE)
        return pltpu.make_async_remote_copy(
            src_ref=fwd_ref.at[i, to], dst_ref=rows_ref.at[i, m], send_sem=psend_sem.at[i],
            recv_sem=precv_sem.at[i], device_id=(to * DEPTH + z, pair), device_id_type=MESH,
        )

    def all_rows(i):
        rest = pl.ds(1, PLANE - 1)
        return pltpu.make_async_remote_copy(
            src_ref=fwd_ref.at[i, rest], dst_ref=rows_ref.at[i, rest], send_sem=psend_sem.at[i],
            recv_sem=precv_sem.at[i], device_id=(seq, pair), device_id_type=MESH,
        )

    width = PLANE * BOUND

    def pass_on(i):
        if i:
            z_copy(i, 1).wait_recv()
            z_copy(i, 2).wait_recv()
        labels = jnp.concatenate([zlabgot_ref[i, g : g + 1, :] for g in range(4)], axis=1)
        hot = one_hot(iota((TOK, width), 0) == (labels & (TOK - 1)))
        pairs = t_dot(hot, zkv_ref[i] if i else kvin_ref[...]).astype(BF16)
        rows = zgot_ref[i] if i else zsend_ref[0]
        fwd_ref[i] = jnp.concatenate([rows, pairs], axis=1).reshape(PLANE, BOUND, 4 * HD)

        def send(m, carry):
            row_copy(i, m).start()
            return carry

        lax.fori_loop(1, PLANE, send, 0)
        rows_ref[i, 0] = fwd_ref[i, yx]

    def arrange(i, first, last):
        if first:
            for m in range(1, PLANE):
                label_copy(m).wait_recv()
        given = plab_ref[:, i, :]
        quarter = lax.rem(yx, 4)
        mine = given[:, 3 * BOUND :]
        for g in range(3):
            mine = jnp.where(quarter == g, given[:, g * BOUND : (g + 1) * BOUND], mine)
        lane = jnp.concatenate([mine[m : m + 1, :] for m in range(PLANE)], axis=1)
        lane = lax.shift_right_arithmetic(lane, 7)
        lane_ref[i : i + 1, :] = lane
        live = dot_t(
            one_hot(iota((SLOTS // 128, width), 0) == lax.shift_right_arithmetic(lane, 7)),
            one_hot(iota((128, width), 0) == (lane & 127)),
        )
        all_rows(i).wait_recv()

        def add(b, carry):
            hot = one_hot(iota((HALF, width), 0) == lane - b * HALF)
            term = dot(hot, rows_ref[i].reshape(width, 4 * HD))
            if first:
                total_ref[b] = term
            elif not last:
                total_ref[b] += term
            else:
                done = (total_ref[b] + term).astype(BF16)
                qg_ref[b] = done[:, : 2 * HD]
                kv_ref[b] = done[:, 2 * HD :]
            return carry

        lax.fori_loop(0, CL_DEV, add, 0)
        return live

    live = jnp.zeros((SLOTS // 128, 128), F32)
    for n in range(DEPTH + LAG):
        if n < DEPTH:
            pass_on(ORDER[n])
        if n >= LAG:
            live = live + arrange(ORDER[n - LAG], n == LAG, n == DEPTH + LAG - 1)
    for c in range(CL_DEV):
        live_ref[c] = live[4 * c : 4 * c + 4, :]
    for i in range(DEPTH):
        all_rows(i).wait_send()
        if i:
            for kind in range(3):
                z_copy(i, kind).wait_send()
    for m in range(1, PLANE):
        label_copy(m).wait_send()


def forward(idx, queries, out_grad, key_value):
    width = PLANE * BOUND
    return pl.pallas_call(
        forward_kernel,
        out_shape=(
            jax.ShapeDtypeStruct((CL_DEV, HALF, 2 * HD), BF16),
            jax.ShapeDtypeStruct((CL_DEV, HALF, 2 * HD), BF16),
            jax.ShapeDtypeStruct((CL_DEV, 4, 128), F32),
            jax.ShapeDtypeStruct((DEPTH, width), jnp.int32),
            jax.ShapeDtypeStruct((1, ROWS), jnp.int32),
        ),
        in_specs=[VMEM] * 4,
        out_specs=(VMEM,) * 5,
        scratch_shapes=[
            pltpu.VMEM((ROWS, 2 * HD), BF16),
            pltpu.VMEM((GROUPS, ROWS), F32),
            pltpu.VMEM((DEPTH, width, 2 * HD), BF16),
            pltpu.VMEM((DEPTH, width, 2 * HD), BF16),
            pltpu.VMEM((DEPTH, TOK, 2 * HD), BF16),
            pltpu.VMEM((DEPTH, 4, 128), jnp.int32),
            pltpu.VMEM((DEPTH, 4, 128), jnp.int32),
            pltpu.VMEM((4, DEPTH, 128), jnp.int32),
            pltpu.VMEM((PLANE, DEPTH, 128), jnp.int32),
            pltpu.VMEM((DEPTH, PLANE, BOUND, 4 * HD), BF16),
            pltpu.VMEM((DEPTH, PLANE, BOUND, 4 * HD), BF16),
            pltpu.VMEM((CL_DEV, HALF, 4 * HD), F32),
            pltpu.SemaphoreType.DMA((DEPTH, 3)),
            pltpu.SemaphoreType.DMA((DEPTH, 3)),
            pltpu.SemaphoreType.DMA((PLANE,)),
            pltpu.SemaphoreType.DMA((PLANE,)),
            pltpu.SemaphoreType.DMA((DEPTH,)),
            pltpu.SemaphoreType.DMA((DEPTH,)),
        ],
        compiler_params=params(0),
    )(idx, queries, out_grad, key_value)


def backward_kernel(
    qg_ref, kv_ref, live_ref, lane_ref, cell_ref, x_ref, out_ref,
    kv2_ref, live2_ref, s_ref, d_ref, w_ref, grads_ref, back_ref, zback_ref, got_ref, hot_ref,
    xp_ref, g_ref, xo_ref, go_ref, part_ref, plane_ref, line_ref, lined_ref,
    ksend_sem, krecv_sem, bsend_sem, brecv_sem, rsend_sem, rrecv_sem, psend_sem, precv_sem,
    ysend_sem, yrecv_sem, zsend_sem, zrecv_sem,
):
    seq, pair = lax.axis_index("seq"), lax.axis_index("pair")
    other = (seq, 1 - pair)
    yx, z = seq // DEPTH, lax.rem(seq, DEPTH)
    barrier, answers = neighbours(seq, pair, 1)
    pl.semaphore_wait(barrier, answers)

    def key_copy(c):
        return pltpu.make_async_remote_copy(
            src_ref=kv_ref.at[c], dst_ref=kv2_ref.at[c], send_sem=ksend_sem.at[c],
            recv_sem=krecv_sem.at[c], device_id=other, device_id_type=MESH,
        )

    live_copy = pltpu.make_async_remote_copy(
        src_ref=live_ref, dst_ref=live2_ref, send_sem=ksend_sem.at[CL_DEV],
        recv_sem=krecv_sem.at[CL_DEV], device_id=other, device_id_type=MESH,
    )
    live_copy.start()
    for c in range(CL_DEV):
        key_copy(c).start()
    position = iota((1024, 512), 1)
    for p in range(2):
        column = lax.shift_right_logical(position, 2) * 8 + 4 * p + (position & 3)
        xp_ref[p] = dot(x_ref[...], one_hot(iota((1024, 512), 0) == column)).astype(BF16)
    x_copy = pltpu.make_async_remote_copy(
        src_ref=xp_ref.at[1 - pair], dst_ref=xo_ref, send_sem=psend_sem.at[0],
        recv_sem=precv_sem.at[0], device_id=other, device_id_type=MESH,
    )
    x_copy.start()
    live_copy.wait()

    for c in range(CL_DEV):
        key_copy(c).wait()
        queries = qg_ref[c, :, :HD] * BF16(HD**-0.5)
        grads = qg_ref[c, :, HD:]
        keys = jnp.concatenate([kv_ref[c, :, :HD], kv2_ref[c, :, :HD]], axis=0)
        values = jnp.concatenate([kv_ref[c, :, HD:], kv2_ref[c, :, HD:]], axis=0)
        alive = jnp.concatenate(
            [ref[c, r : r + 1, :] for ref in (live_ref, live2_ref) for r in range(4)], axis=1
        )
        bias = jnp.where(alive > 0.5, 0.0, -1e30)
        s_ref[...] = dot_t(queries, keys)
        d_ref[...] = dot_t(grads, values)

        def rows(r, carry, bias=bias):
            at = pl.ds(pl.multiple_of(r * 32, 32), 32)
            scores = s_ref[at, :] + bias
            weights = jnp.exp(scores - jnp.max(scores, axis=1, keepdims=True))
            inverse = 1.0 / jnp.sum(weights, axis=1, keepdims=True)
            prob_grad = d_ref[at, :]
            row_dot = jnp.sum(weights * prob_grad, axis=1, keepdims=True) * inverse
            w_ref[at, :] = (
                weights * (prob_grad - row_dot) * (inverse * (HD**-0.5))
            ).astype(BF16)
            return carry

        lax.fori_loop(0, HALF // 32, rows, 0)
        place = slice((c % 2) * HALF, (c % 2 + 1) * HALF)
        column = slice((c // 2) * HD, (c // 2 + 1) * HD)
        grads_ref[place, column] = dot(w_ref[...], keys).astype(BF16)

    def back_copy(i):
        to = lax.rem(z + (DEPTH - i), DEPTH)
        return pltpu.make_async_remote_copy(
            src_ref=back_ref.at[i], dst_ref=zback_ref.at[i], send_sem=bsend_sem.at[i],
            recv_sem=brecv_sem.at[i], device_id=(yx * DEPTH + to, pair), device_id_type=MESH,
        )

    width = PLANE * BOUND
    for i in ORDER[1:] + ORDER[:1]:
        labels = jnp.broadcast_to(lane_ref[i : i + 1, :], (128, width)).T
        low = labels & 1023
        hot = jnp.concatenate(
            [one_hot(low == iota((width, 128), 1) + 128 * b) for b in range(8)], axis=1
        )
        found = dot(hot, grads_ref[...])
        high = lax.shift_right_arithmetic(labels[:, :HD], 10)
        row = jnp.zeros((width, HD), F32)
        for a in range(4):
            row = row + jnp.where(high == a, found[:, a * HD : (a + 1) * HD], 0.0)
        row = row.reshape(PLANE, BOUND, HD)
        row = jnp.concatenate([row[:, : BOUND // 2], row[:, BOUND // 2 :]], axis=2).astype(BF16)
        if i:
            back_ref[i] = row
            back_copy(i).start()
        else:
            zback_ref[0] = row

    def return_copy(i, m):
        to = lax.rem(yx + (PLANE - m), PLANE)
        return pltpu.make_async_remote_copy(
            src_ref=zback_ref.at[i, m], dst_ref=got_ref.at[i, m], send_sem=rsend_sem.at[i],
            recv_sem=rrecv_sem.at[i], device_id=(to * DEPTH + z, pair), device_id_type=MESH,
        )

    def all_returns(i):
        rest = pl.ds(1, PLANE - 1)
        return pltpu.make_async_remote_copy(
            src_ref=zback_ref.at[i, rest], dst_ref=got_ref.at[i, rest], send_sem=rsend_sem.at[i],
            recv_sem=rrecv_sem.at[i], device_id=other, device_id_type=MESH,
        )

    for n, i in enumerate(ORDER):
        if i:
            back_copy(i).wait_recv()

        def send(m, carry, i=i):
            return_copy(i, m).start()
            return carry

        lax.fori_loop(1, PLANE, send, 0)
        got_ref[i, 0] = zback_ref[i, 0]
        for h in (2 * n, 2 * n + 1):
            cell = cell_ref[0:1, h * TOK : (h + 1) * TOK]
            line = lax.shift_right_logical(cell, 5) + (DEPTH - z)
            plane = lax.shift_right_logical(cell, 8) + (PLANE - yx)
            target = (line & (DEPTH - 1)) * (PLANE * BOUND // 2) + (plane & (PLANE - 1)) * (BOUND // 2)
            target = jnp.broadcast_to(target + (cell & (BOUND // 2 - 1)), (TOK, TOK)).T
            for b in range(16):
                hot_ref[h * TOK : (h + 1) * TOK, b * 128 : (b + 1) * 128] = one_hot(
                    target == iota((TOK, 128), 1) + 128 * b
                )
    for i in ORDER:
        all_returns(i).wait_recv()
    got = got_ref[...].reshape(GROUPS * BOUND // 2, 2 * HD)
    for h in range(0, H, 2):
        found = dot(hot_ref[h * TOK : (h + 2) * TOK, :], got)
        pieces = []
        for e in range(2):
            cell = cell_ref[0:1, (h + e) * TOK : (h + e + 1) * TOK]
            upper = (jnp.broadcast_to(cell, (TOK, TOK)).T[:, :HD] & (BOUND // 2)) > 0
            piece = found[e * TOK : (e + 1) * TOK]
            pieces.append(jnp.where(upper, piece[:, HD:], piece[:, :HD]))
        g_ref[:, h * HD : (h + 2) * HD] = jnp.concatenate(pieces, axis=1).astype(BF16)
    g_copy = pltpu.make_async_remote_copy(
        src_ref=g_ref, dst_ref=go_ref, send_sem=psend_sem.at[1], recv_sem=precv_sem.at[1],
        device_id=other, device_id_type=MESH,
    )
    g_copy.start()
    x_copy.wait()
    g_copy.wait()
    left, right = xp_ref[pair], xo_ref[...]
    for b in range(4):
        cut = slice(b * 128, (b + 1) * 128)
        term = t_dot(left[:, cut], g_ref[...]) + t_dot(right[:, cut], go_ref[...])
        part_ref[b * 4 : (b + 1) * 4] = term.astype(BF16).reshape(4, 32, 1024)

    def plane_copy(i):
        to = lax.rem(yx + i, PLANE)
        return pltpu.make_async_remote_copy(
            src_ref=part_ref.at[to], dst_ref=plane_ref.at[i - 1], send_sem=ysend_sem.at[i - 1],
            recv_sem=yrecv_sem.at[i - 1], device_id=(to * DEPTH + z, pair), device_id_type=MESH,
        )

    for i in range(1, PLANE):
        plane_copy(i).start()
    total = part_ref[yx].astype(F32)
    for i in range(1, PLANE):
        plane_copy(i).wait_recv()
        total = total + plane_ref[i - 1].astype(F32)
    for i in range(DEPTH):
        rows = total[4 * i : 4 * i + 4, :]
        line_ref[i] = jnp.concatenate([rows[:, :512], rows[:, 512:]], axis=0)

    def line_copy(i):
        to = lax.rem(z + i, DEPTH)
        return pltpu.make_async_remote_copy(
            src_ref=line_ref.at[to], dst_ref=lined_ref.at[i - 1], send_sem=zsend_sem.at[i - 1],
            recv_sem=zrecv_sem.at[i - 1], device_id=(yx * DEPTH + to, pair), device_id_type=MESH,
        )

    for i in range(1, DEPTH):
        line_copy(i).start()
    result = line_ref[z]
    for i in range(1, DEPTH):
        line_copy(i).wait_recv()
        result = result + lined_ref[i - 1]
    out_ref[...] = jnp.concatenate([result[:4], result[4:]], axis=1)
    for i in range(1, DEPTH):
        back_copy(i).wait_send()
    for i in range(DEPTH):
        all_returns(i).wait_send()
    for i in range(1, PLANE):
        plane_copy(i).wait_send()
    for i in range(1, DEPTH):
        line_copy(i).wait_send()


def backward(qg, kv, live, lane, cell, tokens_in):
    return pl.pallas_call(
        backward_kernel,
        out_shape=jax.ShapeDtypeStruct((4, 1024), F32),
        in_specs=[VMEM] * 6,
        out_specs=VMEM,
        scratch_shapes=[
            pltpu.VMEM((CL_DEV, HALF, 2 * HD), BF16),
            pltpu.VMEM((CL_DEV, 4, 128), F32),
            pltpu.VMEM((HALF, 2 * HALF), F32),
            pltpu.VMEM((HALF, 2 * HALF), F32),
            pltpu.VMEM((HALF, 2 * HALF), BF16),
            pltpu.VMEM((2 * HALF, 4 * HD), BF16),
            pltpu.VMEM((DEPTH, PLANE, BOUND // 2, 2 * HD), BF16),
            pltpu.VMEM((DEPTH, PLANE, BOUND // 2, 2 * HD), BF16),
            pltpu.VMEM((DEPTH, PLANE, BOUND // 2, 2 * HD), BF16),
            pltpu.VMEM((ROWS, GROUPS * BOUND // 2), BF16),
            pltpu.VMEM((2, TOK, 512), BF16),
            pltpu.VMEM((TOK, 1024), BF16),
            pltpu.VMEM((TOK, 512), BF16),
            pltpu.VMEM((TOK, 1024), BF16),
            pltpu.VMEM((PLANE, 32, 1024), BF16),
            pltpu.VMEM((PLANE - 1, 32, 1024), BF16),
            pltpu.VMEM((DEPTH, 8, 512), F32),
            pltpu.VMEM((DEPTH - 1, 8, 512), F32),
            pltpu.SemaphoreType.DMA((CL_DEV + 1,)),
            pltpu.SemaphoreType.DMA((CL_DEV + 1,)),
            pltpu.SemaphoreType.DMA((DEPTH,)),
            pltpu.SemaphoreType.DMA((DEPTH,)),
            pltpu.SemaphoreType.DMA((DEPTH,)),
            pltpu.SemaphoreType.DMA((DEPTH,)),
            pltpu.SemaphoreType.DMA((2,)),
            pltpu.SemaphoreType.DMA((2,)),
            pltpu.SemaphoreType.DMA((PLANE - 1,)),
            pltpu.SemaphoreType.DMA((PLANE - 1,)),
            pltpu.SemaphoreType.DMA((DEPTH - 1,)),
            pltpu.SemaphoreType.DMA((DEPTH - 1,)),
        ],
        compiler_params=params(1),
    )(qg, kv, live, lane, cell, tokens_in)


def on_device(tokens_in, queries, key_value, out_grad, cluster_of, slot_of):
    idx = jnp.stack([cluster_of.T.reshape(ROWS), slot_of.T.reshape(ROWS)])
    qg, kv, live, lane, cell = forward(idx, queries, out_grad, key_value)
    return backward(qg, kv, live, lane, cell, tokens_in)


def solution(mesh):
    spec = P(("seq", "pair"), None)
    return jax.shard_map(
        on_device, mesh=mesh, in_specs=(spec,) * 6, out_specs=spec, check_vma=False
    )
```

```python
import jax
import jax.numpy as jnp
from jax import lax
from jax.experimental import pallas as pl
from jax.experimental.pallas import tpu as pltpu
from jax.sharding import PartitionSpec as P

H = 16
HD = 64
HALF = 512
CL_DEV = 8
TOK = 128
ROWS = TOK * H
SLOTS = CL_DEV * HALF
GROUPS = 128
BOUND = 32
PLANE = 16
DEPTH = 8
ORDER = [0, 1, 7, 2, 6, 3, 5, 4]
LAG = 2
MESH = pl.DeviceIdType.MESH
F32 = jnp.float32
BF16 = jnp.bfloat16
VMEM = pl.BlockSpec(memory_space=pltpu.VMEM)


def params(collective=None):
    if collective is None:
        return pltpu.CompilerParams(vmem_limit_bytes=56 * 2**20)
    return pltpu.CompilerParams(
        vmem_limit_bytes=56 * 2**20, collective_id=collective, has_side_effects=True
    )


def iota(shape, dim):
    return lax.broadcasted_iota(jnp.int32, shape, dim)


def one_hot(mask):
    return jnp.where(mask, 1.0, 0.0).astype(BF16)


def dot(a, b):
    return jnp.dot(a, b, preferred_element_type=F32)


def dot_t(a, b):
    return lax.dot_general(a, b, (((1,), (1,)), ((), ())), preferred_element_type=F32)


def t_dot(a, b):
    return lax.dot_general(a, b, (((0,), (0,)), ((), ())), preferred_element_type=F32)


def whole_kernel(
    cluster_ref, slot_ref, q_ref, g_ref, kvin_ref, x_ref, out_ref,
    flat_ref, zsend_ref, zgot_ref, zkv_ref, zlab_ref, zlabgot_ref, group_ref, plab_ref,
    fwd_ref, rows_ref, total_ref, qg_ref, kv_ref, live_ref, kv2_ref, live2_ref, grads_ref,
    back_ref, zback_ref, got_ref, hot_ref, found_ref, xt_ref, xo_ref, wide_ref, part_ref,
    plane_ref, line_ref, lined_ref,
    fsend_sem, frecv_sem, lsend_sem, lrecv_sem, wsend_sem, wrecv_sem, ksend_sem, krecv_sem,
    bsend_sem, brecv_sem, rsend_sem, rrecv_sem, psend_sem, precv_sem, ysend_sem, yrecv_sem,
    zsend_sem, zrecv_sem,
):
    seq, pair = lax.axis_index("seq"), lax.axis_index("pair")
    other = (seq, 1 - pair)
    yx, z = seq // DEPTH, lax.rem(seq, DEPTH)
    width = PLANE * BOUND
    rest = pl.ds(1, PLANE - 1)

    def on_line(i):
        return (yx * DEPTH + lax.rem(z + i, DEPTH), pair)

    def in_plane(m):
        return (lax.rem(yx + m, PLANE) * DEPTH + z, pair)

    def remote(source, target, send_sem, recv_sem, to):
        return pltpu.make_async_remote_copy(
            src_ref=source, dst_ref=target, send_sem=send_sem, recv_sem=recv_sem,
            device_id=to, device_id_type=MESH,
        )

    barrier = pltpu.get_barrier_semaphore()
    for i in range(1, DEPTH):
        pl.semaphore_signal(barrier, inc=1, device_id=on_line(i), device_id_type=MESH)
    for m in range(1, PLANE):
        pl.semaphore_signal(barrier, inc=1, device_id=in_plane(m), device_id_type=MESH)
    pl.semaphore_signal(barrier, inc=1, device_id=other, device_id_type=MESH)

    def in_lanes(ref):
        turned = ref[...].T
        return jnp.concatenate([turned[h : h + 1, :] for h in range(H)], axis=1)

    cluster = in_lanes(cluster_ref)
    slot = in_lanes(slot_ref)
    owner = lax.shift_right_logical(cluster, 3)
    local = (cluster & (CL_DEV - 1)) * HALF + (slot & (HALF - 1))
    before = one_hot(iota((TOK, TOK), 0) < iota((TOK, TOK), 1))
    base = jnp.zeros((GROUPS, 1), F32)
    ranks = []
    for h in range(H):
        mine = owner[:, h * TOK : (h + 1) * TOK]
        pick = jnp.where(iota((GROUPS, TOK), 0) == mine, 1.0, 0.0)
        count = dot(pick.astype(BF16), before) + base
        ranks.append(jnp.sum(pick * count, axis=0, keepdims=True))
        base = base + jnp.sum(pick, axis=1, keepdims=True)
    rank = jnp.concatenate(ranks, axis=1).astype(jnp.int32)
    place = (owner & (DEPTH - 1)) * width + lax.shift_right_logical(owner, 3) * BOUND + rank
    in_row = jnp.where(iota((32, ROWS), 0) == lax.shift_right_logical(place, 7), 1.0, 0.0)
    in_lane = one_hot(iota((128, ROWS), 0) == (place & 127))
    token = iota((1, ROWS), 1) & (TOK - 1)
    parts = [lax.shift_right_logical(local, 6), local & 63, token]
    stacked = [(in_row * part.astype(F32)).astype(BF16) for part in parts] + [in_row.astype(BF16)]
    found = dot_t(jnp.concatenate(stacked, axis=0), in_lane)
    label = jnp.where(
        found[96:128] > 0.5, (found[0:32] * 64.0 + found[32:64]) * 128.0 + found[64:96], -1.0
    ).astype(jnp.int32)
    for i in range(DEPTH):
        zlab_ref[i] = label[4 * i : 4 * i + 4, :]
    for h in range(H):
        cut = slice(h * HD, (h + 1) * HD)
        flat_ref[h * TOK : (h + 1) * TOK, :] = jnp.concatenate([q_ref[:, cut], g_ref[:, cut]], axis=1)
    for i in ORDER[1:] + ORDER[:1]:
        to = lax.rem(z + i, DEPTH)
        hot = one_hot(iota((width, ROWS), 0) == place - to * width)
        zsend_ref[i] = dot(hot, flat_ref[...]).astype(BF16)
    position = iota((512, 1024), 0)
    for p in range(2):
        column = lax.shift_right_logical(position, 2) * 8 + 4 * p + (position & 3)
        xt_ref[p] = dot_t(one_hot(iota((512, 1024), 1) == column), x_ref[...]).astype(BF16)

    def z_copy(i, kind):
        to = lax.rem(z + i, DEPTH)
        source, target = (
            (zlab_ref.at[to], zlabgot_ref.at[i]),
            (kvin_ref, zkv_ref.at[i]),
            (zsend_ref.at[i], zgot_ref.at[i]),
        )[kind]
        return remote(source, target, fsend_sem.at[i, kind], frecv_sem.at[i, kind], on_line(i))

    pl.semaphore_wait(barrier, DEPTH - 1 + PLANE - 1 + 1)
    for i in ORDER[1:]:
        z_copy(i, 0).start()
    for i in ORDER[1:]:
        z_copy(i, 1).start()
        z_copy(i, 2).start()
    x_copy = remote(xt_ref.at[1 - pair], xo_ref, psend_sem.at[0], precv_sem.at[0], other)
    x_copy.start()

    def row_copy(i, m):
        to = lax.rem(yx + m, PLANE)
        return remote(
            fwd_ref.at[i, to], rows_ref.at[i, m], wsend_sem.at[i], wrecv_sem.at[i], in_plane(m)
        )

    def all_rows(i):
        return remote(
            fwd_ref.at[i, rest], rows_ref.at[i, rest], wsend_sem.at[i], wrecv_sem.at[i], other
        )

    def pass_on(i):
        if i:
            z_copy(i, 1).wait_recv()
            z_copy(i, 2).wait_recv()
        labels = jnp.concatenate([zlabgot_ref[i, g : g + 1, :] for g in range(4)], axis=1)
        hot = one_hot(iota((TOK, width), 0) == (labels & (TOK - 1)))
        pairs = t_dot(hot, zkv_ref[i] if i else kvin_ref[...]).astype(BF16)
        rows = zgot_ref[i] if i else zsend_ref[0]
        fwd_ref[i] = jnp.concatenate([rows, pairs], axis=1).reshape(PLANE, BOUND, 4 * HD)

        def send(m, carry):
            row_copy(i, m).start()
            return carry

        lax.fori_loop(1, PLANE, send, 0)
        rows_ref[i, 0] = fwd_ref[i, yx]

    zlabgot_ref[0] = zlab_ref[z]
    pass_on(0)
    for i in ORDER[1:]:
        z_copy(i, 0).wait_recv()
    for i in range(DEPTH):
        for g in range(4):
            group_ref[g, i : i + 1, :] = zlabgot_ref[i, g : g + 1, :]

    def label_copy(m):
        to = lax.rem(yx + m, PLANE)
        return remote(
            group_ref.at[to // 4], plab_ref.at[m], lsend_sem.at[m], lrecv_sem.at[m], in_plane(m)
        )

    for m in range(1, PLANE):
        label_copy(m).start()
    plab_ref[0] = group_ref[yx // 4]

    for h in range(H):
        cut = slice(h * TOK, (h + 1) * TOK)
        to = owner[:, cut]
        line = (to + (DEPTH - z)) & (DEPTH - 1)
        plane = (lax.shift_right_logical(to, 3) + (PLANE - yx)) & (PLANE - 1)
        target = line * (width // 2) + plane * (BOUND // 2) + (rank[:, cut] & (BOUND // 2 - 1))
        target = jnp.broadcast_to(target, (TOK, TOK)).T
        for b in range(16):
            hot_ref[cut, b * 128 : (b + 1) * 128] = one_hot(target == iota((TOK, 128), 1) + 128 * b)

    for m in range(1, PLANE):
        label_copy(m).wait_recv()
    quarter = lax.rem(yx, 4)
    lanes = []
    live = jnp.zeros((SLOTS // 128, 128), F32)
    for i in range(DEPTH):
        given = plab_ref[:, i, :]
        mine = given[:, 3 * BOUND :]
        for g in range(3):
            mine = jnp.where(quarter == g, given[:, g * BOUND : (g + 1) * BOUND], mine)
        lane = jnp.concatenate([mine[m : m + 1, :] for m in range(PLANE)], axis=1)
        lane = lax.shift_right_arithmetic(lane, 7)
        lanes.append(lane)
        live = live + dot_t(
            one_hot(iota((SLOTS // 128, width), 0) == lax.shift_right_arithmetic(lane, 7)),
            one_hot(iota((128, width), 0) == (lane & 127)),
        )
    for c in range(CL_DEV):
        live_ref[c] = live[4 * c : 4 * c + 4, :]
    live_copy = remote(
        live_ref, live2_ref, ksend_sem.at[CL_DEV], krecv_sem.at[CL_DEV], other
    )
    live_copy.start()

    def key_copy(c):
        return remote(kv_ref.at[c], kv2_ref.at[c], ksend_sem.at[c], krecv_sem.at[c], other)

    def arrange(i, first, last):
        all_rows(i).wait_recv()
        lane = lanes[i]
        for b in range(CL_DEV):
            hot = one_hot(iota((HALF, width), 0) == lane - b * HALF)
            term = dot(hot, rows_ref[i].reshape(width, 4 * HD))
            if first:
                total_ref[b] = term
            elif not last:
                total_ref[b] += term
            else:
                done = (total_ref[b] + term).astype(BF16)
                qg_ref[b] = done[:, : 2 * HD]
                kv_ref[b] = done[:, 2 * HD :]
                key_copy(b).start()

    for n in range(1, DEPTH + LAG):
        if n < DEPTH:
            pass_on(ORDER[n])
        if n >= LAG:
            arrange(ORDER[n - LAG], n == LAG, n == DEPTH + LAG - 1)

    live_copy.wait()
    for c in range(CL_DEV):
        if c % 4 == 0:
            for e in range(c, c + 4):
                key_copy(e).wait_recv()
        queries = qg_ref[c, :, :HD] * BF16(HD**-0.5)
        grads = qg_ref[c, :, HD:]
        keys = jnp.concatenate([kv_ref[c, :, :HD], kv2_ref[c, :, :HD]], axis=0)
        values = jnp.concatenate([kv_ref[c, :, HD:], kv2_ref[c, :, HD:]], axis=0)
        alive = jnp.concatenate(
            [ref[c, r : r + 1, :] for ref in (live_ref, live2_ref) for r in range(4)], axis=1
        )
        scores = dot_t(queries, keys) + jnp.where(alive > 0.5, 0.0, -1e30)
        prob_grad = dot_t(grads, values)
        weights = jnp.exp(scores - jnp.max(scores, axis=1, keepdims=True))
        inverse = 1.0 / jnp.sum(weights, axis=1, keepdims=True)
        row_dot = jnp.sum(weights * prob_grad, axis=1, keepdims=True) * inverse
        score_grad = (weights * (prob_grad - row_dot) * (inverse * (HD**-0.5))).astype(BF16)
        grads_ref[
            (c % 2) * HALF : (c % 2 + 1) * HALF, (c // 2) * HD : (c // 2 + 1) * HD
        ] = dot(score_grad, keys).astype(BF16)

    def back_copy(i):
        return remote(
            back_ref.at[i], zback_ref.at[i], bsend_sem.at[i], brecv_sem.at[i], on_line(DEPTH - i)
        )

    for i in ORDER[1:] + ORDER[:1]:
        labels = jnp.broadcast_to(lanes[i], (128, width)).T
        low = labels & 1023
        hot = jnp.concatenate(
            [one_hot(low == iota((width, 128), 1) + 128 * b) for b in range(8)], axis=1
        )
        found = dot(hot, grads_ref[...])
        high = lax.shift_right_arithmetic(labels[:, :HD], 10)
        row = jnp.zeros((width, HD), F32)
        for a in range(4):
            row = row + jnp.where(high == a, found[:, a * HD : (a + 1) * HD], 0.0)
        row = row.reshape(PLANE, BOUND, HD)
        row = jnp.concatenate([row[:, : BOUND // 2], row[:, BOUND // 2 :]], axis=2).astype(BF16)
        if i:
            back_ref[i] = row
            back_copy(i).start()
        else:
            zback_ref[0] = row

    def return_copy(i, m):
        return remote(
            zback_ref.at[i, m], got_ref.at[i, m], rsend_sem.at[i], rrecv_sem.at[i],
            in_plane(PLANE - m),
        )

    def all_returns(i):
        return remote(
            zback_ref.at[i, rest], got_ref.at[i, rest], rsend_sem.at[i], rrecv_sem.at[i], other
        )

    def take(i, first):
        all_returns(i).wait_recv()
        half = width // 2
        term = dot(
            hot_ref[:, i * half : (i + 1) * half], got_ref[i].reshape(half, 2 * HD)
        )
        if first:
            found_ref[...] = term
        else:
            found_ref[...] += term

    for n in range(DEPTH + LAG):
        if n < DEPTH:
            i = ORDER[n]
            if i:
                back_copy(i).wait_recv()

            def send(m, carry, i=i):
                return_copy(i, m).start()
                return carry

            lax.fori_loop(1, PLANE, send, 0)
            got_ref[i, 0] = zback_ref[i, 0]
        if n >= LAG:
            take(ORDER[n - LAG], n == LAG)
    for h in range(0, H, 2):
        pieces = []
        for e in range(2):
            cut = slice((h + e) * TOK, (h + e + 1) * TOK)
            upper = (jnp.broadcast_to(rank[:, cut], (TOK, TOK)).T[:, :HD] & (BOUND // 2)) > 0
            piece = found_ref[cut, :]
            pieces.append(jnp.where(upper, piece[:, HD:], piece[:, :HD]))
        wide_ref[0, :, h * HD : (h + 2) * HD] = jnp.concatenate(pieces, axis=1).astype(BF16)
    g_copy = remote(wide_ref.at[0], wide_ref.at[1], psend_sem.at[1], precv_sem.at[1], other)
    g_copy.start()
    x_copy.wait()
    g_copy.wait()

    def plane_copy(i):
        return remote(
            part_ref.at[lax.rem(yx + i, PLANE)], plane_ref.at[i - 1], ysend_sem.at[i - 1],
            yrecv_sem.at[i - 1], in_plane(i),
        )

    xt = jnp.concatenate([xt_ref[pair], xo_ref[...]], axis=1)
    part_ref[...] = dot(xt, wide_ref[...].reshape(2 * TOK, 1024)).astype(BF16).reshape(PLANE, 32, 1024)
    for i in range(1, PLANE):
        plane_copy(i).start()
    total = part_ref[yx].astype(F32)
    for i in range(1, PLANE):
        plane_copy(i).wait_recv()
        total = total + plane_ref[i - 1].astype(F32)
    for i in range(DEPTH):
        rows = total[4 * i : 4 * i + 4, :]
        line_ref[i] = jnp.concatenate([rows[:, :512], rows[:, 512:]], axis=0)

    def line_copy(i):
        return remote(
            line_ref.at[lax.rem(z + i, DEPTH)], lined_ref.at[i - 1], zsend_sem.at[i - 1],
            zrecv_sem.at[i - 1], on_line(i),
        )

    for i in range(1, DEPTH):
        line_copy(i).start()
    result = line_ref[z]
    for i in range(1, DEPTH):
        line_copy(i).wait_recv()
        result = result + lined_ref[i - 1]
    out_ref[...] = jnp.concatenate([result[:4], result[4:]], axis=1)

    for i in range(1, DEPTH):
        for kind in range(3):
            z_copy(i, kind).wait_send()
        back_copy(i).wait_send()
        line_copy(i).wait_send()
    for i in range(DEPTH):
        all_rows(i).wait_send()
        key_copy(i).wait_send()
        all_returns(i).wait_send()
    for m in range(1, PLANE):
        label_copy(m).wait_send()
        plane_copy(m).wait_send()


def whole(cluster_of, slot_of, queries, out_grad, key_value, tokens_in):
    width = PLANE * BOUND
    dma = pltpu.SemaphoreType.DMA
    return pl.pallas_call(
        whole_kernel,
        out_shape=jax.ShapeDtypeStruct((4, 1024), F32),
        in_specs=[VMEM] * 6,
        out_specs=VMEM,
        scratch_shapes=[
            pltpu.VMEM((ROWS, 2 * HD), BF16),
            pltpu.VMEM((DEPTH, width, 2 * HD), BF16),
            pltpu.VMEM((DEPTH, width, 2 * HD), BF16),
            pltpu.VMEM((DEPTH, TOK, 2 * HD), BF16),
            pltpu.VMEM((DEPTH, 4, 128), jnp.int32),
            pltpu.VMEM((DEPTH, 4, 128), jnp.int32),
            pltpu.VMEM((4, DEPTH, 128), jnp.int32),
            pltpu.VMEM((PLANE, DEPTH, 128), jnp.int32),
            pltpu.VMEM((DEPTH, PLANE, BOUND, 4 * HD), BF16),
            pltpu.VMEM((DEPTH, PLANE, BOUND, 4 * HD), BF16),
            pltpu.VMEM((CL_DEV, HALF, 4 * HD), F32),
            pltpu.VMEM((CL_DEV, HALF, 2 * HD), BF16),
            pltpu.VMEM((CL_DEV, HALF, 2 * HD), BF16),
            pltpu.VMEM((CL_DEV, 4, 128), F32),
            pltpu.VMEM((CL_DEV, HALF, 2 * HD), BF16),
            pltpu.VMEM((CL_DEV, 4, 128), F32),
            pltpu.VMEM((2 * HALF, 4 * HD), BF16),
            pltpu.VMEM((DEPTH, PLANE, BOUND // 2, 2 * HD), BF16),
            pltpu.VMEM((DEPTH, PLANE, BOUND // 2, 2 * HD), BF16),
            pltpu.VMEM((DEPTH, PLANE, BOUND // 2, 2 * HD), BF16),
            pltpu.VMEM((ROWS, GROUPS * BOUND // 2), BF16),
            pltpu.VMEM((ROWS, 2 * HD), F32),
            pltpu.VMEM((2, 512, TOK), BF16),
            pltpu.VMEM((512, TOK), BF16),
            pltpu.VMEM((2, TOK, 1024), BF16),
            pltpu.VMEM((PLANE, 32, 1024), BF16),
            pltpu.VMEM((PLANE - 1, 32, 1024), BF16),
            pltpu.VMEM((DEPTH, 8, 512), F32),
            pltpu.VMEM((DEPTH - 1, 8, 512), F32),
            dma((DEPTH, 3)),
            dma((DEPTH, 3)),
            dma((PLANE,)),
            dma((PLANE,)),
            dma((DEPTH,)),
            dma((DEPTH,)),
            dma((CL_DEV + 1,)),
            dma((CL_DEV + 1,)),
            dma((DEPTH,)),
            dma((DEPTH,)),
            dma((DEPTH,)),
            dma((DEPTH,)),
            dma((2,)),
            dma((2,)),
            dma((PLANE - 1,)),
            dma((PLANE - 1,)),
            dma((DEPTH - 1,)),
            dma((DEPTH - 1,)),
        ],
        compiler_params=params(0),
    )(cluster_of, slot_of, queries, out_grad, key_value, tokens_in)


def on_device(tokens_in, queries, key_value, out_grad, cluster_of, slot_of):
    return whole(cluster_of, slot_of, queries, out_grad, key_value, tokens_in)


def solution(mesh):
    spec = P(("seq", "pair"), None)
    return jax.shard_map(
        on_device, mesh=mesh, in_specs=(spec,) * 6, out_specs=spec, check_vma=False
    )
```

```python
import jax
import jax.numpy as jnp
from jax import lax
from jax.experimental import pallas as pl
from jax.experimental.pallas import tpu as pltpu
from jax.sharding import PartitionSpec as P

H = 16
HD = 64
HALF = 512
CL_DEV = 8
TOK = 128
ROWS = TOK * H
SLOTS = CL_DEV * HALF
GROUPS = 128
BOUND = 32
PLANE = 16
DEPTH = 8
ORDER = [0, 1, 7, 2, 6, 3, 5, 4]
LAG = 2
EARLY = 3
JOINT = 2
PIECE = 256
MESH = pl.DeviceIdType.MESH
F32 = jnp.float32
BF16 = jnp.bfloat16
VMEM = pl.BlockSpec(memory_space=pltpu.VMEM)


def params(collective=None):
    if collective is None:
        return pltpu.CompilerParams(vmem_limit_bytes=56 * 2**20)
    return pltpu.CompilerParams(
        vmem_limit_bytes=56 * 2**20, collective_id=collective, has_side_effects=True
    )


def iota(shape, dim):
    return lax.broadcasted_iota(jnp.int32, shape, dim)


def one_hot(mask):
    return jnp.where(mask, 1.0, 0.0).astype(BF16)


def dot(a, b):
    return jnp.dot(a, b, preferred_element_type=F32)


def dot_t(a, b):
    return lax.dot_general(a, b, (((1,), (1,)), ((), ())), preferred_element_type=F32)


def t_dot(a, b):
    return lax.dot_general(a, b, (((0,), (0,)), ((), ())), preferred_element_type=F32)


def whole_kernel(
    cluster_in, slot_in, q_in, g_in, kv_in, x_in, out_ref,
    cluster_ref, slot_ref, q_ref, g_ref, kvin_ref, x_ref, flat_ref, zsend_ref, zgot_ref, zkv_ref, zlab_ref, zlabgot_ref, group_ref, plab_ref,
    fwd_ref, rows_ref, total_ref, qg_ref, kv_ref, live_ref, kv2_ref, live2_ref, grads_ref,
    back_ref, zback_ref, got_ref, hot_ref, found_ref, xt_ref, xo_ref, xall_ref, wide_ref,
    fline_ref, flined_ref, fplane_ref, fplaned_ref, part_ref, plane_ref, line_ref, lined_ref,
    fsend_sem, frecv_sem, lsend_sem, lrecv_sem, wsend_sem, wrecv_sem, ksend_sem, krecv_sem,
    bsend_sem, brecv_sem, rsend_sem, rrecv_sem, psend_sem, precv_sem, ysend_sem, yrecv_sem,
    zsend_sem, zrecv_sem, fysend_sem, fyrecv_sem, fzsend_sem, fzrecv_sem, in_sem,
):
    seq, pair = lax.axis_index("seq"), lax.axis_index("pair")
    other = (seq, 1 - pair)
    yx, z = seq // DEPTH, lax.rem(seq, DEPTH)
    width = PLANE * BOUND
    rest = pl.ds(1, PLANE - 1)

    def on_line(i):
        return (yx * DEPTH + lax.rem(z + i, DEPTH), pair)

    def in_plane(m):
        return (lax.rem(yx + m, PLANE) * DEPTH + z, pair)

    def remote(source, target, send_sem, recv_sem, to):
        return pltpu.make_async_remote_copy(
            src_ref=source, dst_ref=target, send_sem=send_sem, recv_sem=recv_sem,
            device_id=to, device_id_type=MESH,
        )

    barrier = pltpu.get_barrier_semaphore()
    for i in range(1, DEPTH):
        pl.semaphore_signal(barrier, inc=1, device_id=on_line(i), device_id_type=MESH)
    for m in range(1, PLANE):
        pl.semaphore_signal(barrier, inc=1, device_id=in_plane(m), device_id_type=MESH)
    pl.semaphore_signal(barrier, inc=1, device_id=other, device_id_type=MESH)

    loads = [
        pltpu.make_async_copy(source, target, in_sem.at[n])
        for n, (source, target) in enumerate(
            (
                (cluster_in, cluster_ref), (slot_in, slot_ref), (q_in, q_ref), (g_in, g_ref),
                (kv_in, kvin_ref), (x_in, x_ref),
            )
        )
    ]
    for load in loads:
        load.start()
    for load in loads[:2]:
        load.wait()

    def in_lanes(ref):
        turned = ref[...].T
        return jnp.concatenate([turned[h : h + 1, :] for h in range(H)], axis=1)

    cluster = in_lanes(cluster_ref)
    slot = in_lanes(slot_ref)
    owner = lax.shift_right_logical(cluster, 3)
    local = (cluster & (CL_DEV - 1)) * HALF + (slot & (HALF - 1))
    before = one_hot(iota((TOK, TOK), 0) < iota((TOK, TOK), 1))
    base = jnp.zeros((GROUPS, 1), F32)
    ranks = []
    for h in range(H):
        mine = owner[:, h * TOK : (h + 1) * TOK]
        pick = jnp.where(iota((GROUPS, TOK), 0) == mine, 1.0, 0.0)
        count = dot(pick.astype(BF16), before) + base
        ranks.append(jnp.sum(pick * count, axis=0, keepdims=True))
        base = base + jnp.sum(pick, axis=1, keepdims=True)
    rank = jnp.concatenate(ranks, axis=1).astype(jnp.int32)
    place = (owner & (DEPTH - 1)) * width + lax.shift_right_logical(owner, 3) * BOUND + rank
    in_row = jnp.where(iota((32, ROWS), 0) == lax.shift_right_logical(place, 7), 1.0, 0.0)
    in_lane = one_hot(iota((128, ROWS), 0) == (place & 127))
    token = iota((1, ROWS), 1) & (TOK - 1)
    parts = [lax.shift_right_logical(local, 6), local & 63, token]
    stacked = [(in_row * part.astype(F32)).astype(BF16) for part in parts] + [in_row.astype(BF16)]
    found = dot_t(jnp.concatenate(stacked, axis=0), in_lane)
    label = jnp.where(
        found[96:128] > 0.5, (found[0:32] * 64.0 + found[32:64]) * 128.0 + found[64:96], -1.0
    ).astype(jnp.int32)
    for i in range(DEPTH):
        zlab_ref[i] = label[4 * i : 4 * i + 4, :]
    for load in loads[2:]:
        load.wait()
    for h in range(H):
        cut = slice(h * HD, (h + 1) * HD)
        flat_ref[h * TOK : (h + 1) * TOK, :] = jnp.concatenate([q_ref[:, cut], g_ref[:, cut]], axis=1)
    def pack(i):
        to = lax.rem(z + i, DEPTH)
        hot = one_hot(iota((width, ROWS), 0) == place - to * width)
        zsend_ref[i] = dot(hot, flat_ref[...]).astype(BF16)

    for i in ORDER[1:EARLY]:
        pack(i)

    def z_copy(i, kind):
        to = lax.rem(z + i, DEPTH)
        source, target = (
            (zlab_ref.at[to], zlabgot_ref.at[i]),
            (kvin_ref, zkv_ref.at[i]),
            (zsend_ref.at[i], zgot_ref.at[i]),
        )[kind]
        return remote(source, target, fsend_sem.at[i, kind], frecv_sem.at[i, kind], on_line(i))

    pl.semaphore_wait(barrier, DEPTH - 1 + PLANE - 1 + 1)
    for i in ORDER[1:]:
        z_copy(i, 0).start()
    for n, i in enumerate(ORDER[1:], 1):
        if n >= EARLY:
            pack(i)
        z_copy(i, 1).start()
        z_copy(i, 2).start()
    pack(0)

    def row_copy(i, m):
        to = lax.rem(yx + m, PLANE)
        return remote(
            fwd_ref.at[i, to], rows_ref.at[i, m], wsend_sem.at[i], wrecv_sem.at[i], in_plane(m)
        )

    def all_rows(i):
        return remote(
            fwd_ref.at[i, rest], rows_ref.at[i, rest], wsend_sem.at[i], wrecv_sem.at[i], other
        )

    def pass_on(i):
        if i:
            z_copy(i, 1).wait_recv()
            z_copy(i, 2).wait_recv()
        labels = jnp.concatenate([zlabgot_ref[i, g : g + 1, :] for g in range(4)], axis=1)
        hot = one_hot(iota((TOK, width), 0) == (labels & (TOK - 1)))
        pairs = t_dot(hot, zkv_ref[i] if i else kvin_ref[...]).astype(BF16)
        rows = zgot_ref[i] if i else zsend_ref[0]
        fwd_ref[i] = jnp.concatenate([rows, pairs], axis=1).reshape(PLANE, BOUND, 4 * HD)

        def send(m, carry):
            row_copy(i, m).start()
            return carry

        lax.fori_loop(1, PLANE, send, 0)
        rows_ref[i, 0] = fwd_ref[i, yx]

    zlabgot_ref[0] = zlab_ref[z]
    pass_on(0)

    position = iota((512, 1024), 0)
    for p in range(2):
        column = lax.shift_right_logical(position, 2) * 8 + 4 * p + (position & 3)
        xt_ref[p] = dot_t(one_hot(iota((512, 1024), 1) == column), x_ref[...]).astype(BF16)
    x_copy = remote(xt_ref.at[1 - pair], xo_ref, psend_sem.at[0], precv_sem.at[0], other)
    x_copy.start()
    for i in ORDER[1:]:
        z_copy(i, 0).wait_recv()
    for i in range(DEPTH):
        for g in range(4):
            group_ref[g, i : i + 1, :] = zlabgot_ref[i, g : g + 1, :]

    def label_copy(m):
        to = lax.rem(yx + m, PLANE)
        return remote(
            group_ref.at[to // 4], plab_ref.at[m], lsend_sem.at[m], lrecv_sem.at[m], in_plane(m)
        )

    for m in range(1, PLANE):
        label_copy(m).start()
    plab_ref[0] = group_ref[yx // 4]

    for h in range(H):
        cut = slice(h * TOK, (h + 1) * TOK)
        to = owner[:, cut]
        line = (to + (DEPTH - z)) & (DEPTH - 1)
        plane = (lax.shift_right_logical(to, 3) + (PLANE - yx)) & (PLANE - 1)
        target = line * (width // 2) + plane * (BOUND // 2) + (rank[:, cut] & (BOUND // 2 - 1))
        target = jnp.broadcast_to(target, (TOK, TOK)).T
        for b in range(16):
            hot_ref[cut, b * 128 : (b + 1) * 128] = one_hot(target == iota((TOK, 128), 1) + 128 * b)

    x_copy.wait()
    both = jnp.concatenate([xt_ref[pair], xo_ref[...]], axis=1)
    xall_ref[0] = both
    position = iota((512, 512), 0)
    row = (lax.shift_right_logical(position, 2) & (PLANE - 1)) * 32
    row = row + lax.shift_right_logical(position, 6) * 4 + (position & 3)
    xall_ref[1] = dot(one_hot(iota((512, 512), 1) == row), both).astype(BF16)

    for m in range(1, PLANE):
        label_copy(m).wait_recv()
    quarter = lax.rem(yx, 4)
    lanes = []
    live = jnp.zeros((SLOTS // 128, 128), F32)
    for i in range(DEPTH):
        given = plab_ref[:, i, :]
        mine = given[:, 3 * BOUND :]
        for g in range(3):
            mine = jnp.where(quarter == g, given[:, g * BOUND : (g + 1) * BOUND], mine)
        lane = jnp.concatenate([mine[m : m + 1, :] for m in range(PLANE)], axis=1)
        lane = lax.shift_right_arithmetic(lane, 7)
        lanes.append(lane)
        live = live + dot_t(
            one_hot(iota((SLOTS // 128, width), 0) == lax.shift_right_arithmetic(lane, 7)),
            one_hot(iota((128, width), 0) == (lane & 127)),
        )
    for c in range(CL_DEV):
        live_ref[c] = live[4 * c : 4 * c + 4, :]
    live_copy = remote(
        live_ref, live2_ref, ksend_sem.at[CL_DEV], krecv_sem.at[CL_DEV], other
    )
    live_copy.start()

    def key_copy(c):
        return remote(kv_ref.at[c], kv2_ref.at[c], ksend_sem.at[c], krecv_sem.at[c], other)

    def arrange(i, first, last):
        all_rows(i).wait_recv()
        lane = lanes[i]
        for b in range(CL_DEV):
            hot = one_hot(iota((HALF, width), 0) == lane - b * HALF)
            term = dot(hot, rows_ref[i].reshape(width, 4 * HD))
            if first:
                total_ref[b] = term
            elif not last:
                total_ref[b] += term
            else:
                done = (total_ref[b] + term).astype(BF16)
                qg_ref[b] = done[:, : 2 * HD]
                kv_ref[b] = done[:, 2 * HD :]
                key_copy(b).start()

    for n in range(1, DEPTH + LAG):
        if n < DEPTH:
            pass_on(ORDER[n])
        if n >= LAG:
            arrange(ORDER[n - LAG], n == LAG, n == DEPTH + LAG - 1)

    live_copy.wait()
    for c in range(CL_DEV):
        if c % JOINT == 0:
            for e in range(c, c + JOINT):
                key_copy(e).wait_recv()
        queries = qg_ref[c, :, :HD] * BF16(HD**-0.5)
        grads = qg_ref[c, :, HD:]
        keys = jnp.concatenate([kv_ref[c, :, :HD], kv2_ref[c, :, :HD]], axis=0)
        values = jnp.concatenate([kv_ref[c, :, HD:], kv2_ref[c, :, HD:]], axis=0)
        alive = jnp.concatenate(
            [ref[c, r : r + 1, :] for ref in (live_ref, live2_ref) for r in range(4)], axis=1
        )
        scores = dot_t(queries, keys) + jnp.where(alive > 0.5, 0.0, -1e30)
        prob_grad = dot_t(grads, values)
        weights = jnp.exp(scores - jnp.max(scores, axis=1, keepdims=True))
        inverse = 1.0 / jnp.sum(weights, axis=1, keepdims=True)
        row_dot = jnp.sum(weights * prob_grad, axis=1, keepdims=True) * inverse
        score_grad = (weights * (prob_grad - row_dot) * (inverse * (HD**-0.5))).astype(BF16)
        grads_ref[
            (c % 2) * HALF : (c % 2 + 1) * HALF, (c // 2) * HD : (c // 2 + 1) * HD
        ] = dot(score_grad, keys).astype(BF16)

    def back_copy(i):
        return remote(
            back_ref.at[i], zback_ref.at[i], bsend_sem.at[i], brecv_sem.at[i], on_line(DEPTH - i)
        )

    for i in ORDER[1:] + ORDER[:1]:
        labels = jnp.broadcast_to(lanes[i], (128, width)).T
        low = labels & 1023
        hot = jnp.concatenate(
            [one_hot(low == iota((width, 128), 1) + 128 * b) for b in range(8)], axis=1
        )
        found = dot(hot, grads_ref[...])
        high = lax.shift_right_arithmetic(labels[:, :HD], 10)
        row = jnp.zeros((width, HD), F32)
        for a in range(4):
            row = row + jnp.where(high == a, found[:, a * HD : (a + 1) * HD], 0.0)
        row = row.reshape(PLANE, BOUND, HD)
        row = jnp.concatenate([row[:, : BOUND // 2], row[:, BOUND // 2 :]], axis=2).astype(BF16)
        if i:
            back_ref[i] = row
            back_copy(i).start()
        else:
            zback_ref[0] = row

    def return_copy(i, m):
        return remote(
            zback_ref.at[i, m], got_ref.at[i, m], rsend_sem.at[i], rrecv_sem.at[i],
            in_plane(PLANE - m),
        )

    def all_returns(i):
        return remote(
            zback_ref.at[i, rest], got_ref.at[i, rest], rsend_sem.at[i], rrecv_sem.at[i], other
        )

    def take(i, first):
        all_returns(i).wait_recv()
        half = width // 2
        term = dot(
            hot_ref[:, i * half : (i + 1) * half], got_ref[i].reshape(half, 2 * HD)
        )
        if first:
            found_ref[...] = term
        else:
            found_ref[...] += term

    for n in range(DEPTH + LAG):
        if n < DEPTH:
            i = ORDER[n]
            if i:
                back_copy(i).wait_recv()

            def send(m, carry, i=i):
                return_copy(i, m).start()
                return carry

            lax.fori_loop(1, PLANE, send, 0)
            got_ref[i, 0] = zback_ref[i, 0]
        if n >= LAG:
            take(ORDER[n - LAG], n == LAG)
    def g_copy(n):
        cut = pl.ds(n * PIECE, PIECE)
        return remote(
            wide_ref.at[0, :, cut], wide_ref.at[1, :, cut], psend_sem.at[1 + n],
            precv_sem.at[1 + n], other,
        )

    for h in range(0, H, 2):
        pieces = []
        for e in range(2):
            cut = slice((h + e) * TOK, (h + e + 1) * TOK)
            upper = (jnp.broadcast_to(rank[:, cut], (TOK, TOK)).T[:, :HD] & (BOUND // 2)) > 0
            piece = found_ref[cut, :]
            pieces.append(jnp.where(upper, piece[:, HD:], piece[:, :HD]))
        wide_ref[0, :, h * HD : (h + 2) * HD] = jnp.concatenate(pieces, axis=1).astype(BF16)
        if (h + 2) * HD % PIECE == 0:
            g_copy(h * HD // PIECE).start()

    def first_line(i):
        return remote(
            fline_ref.at[lax.rem(z + i, DEPTH)], flined_ref.at[i - 1], fzsend_sem.at[i - 1],
            fzrecv_sem.at[i - 1], on_line(i),
        )

    def first_plane(m):
        return remote(
            fplane_ref.at[lax.rem(yx + m, PLANE)], fplaned_ref.at[m - 1], fysend_sem.at[m - 1],
            fyrecv_sem.at[m - 1], in_plane(m),
        )

    def plane_copy(i):
        return remote(
            part_ref.at[lax.rem(yx + i, PLANE)], plane_ref.at[i - 1], ysend_sem.at[i - 1],
            yrecv_sem.at[i - 1], in_plane(i),
        )

    def line_copy(i):
        return remote(
            line_ref.at[lax.rem(z + i, DEPTH)], lined_ref.at[i - 1], zsend_sem.at[i - 1],
            zrecv_sem.at[i - 1], on_line(i),
        )

    def summed(n, order):
        g_copy(n).wait()
        columns = wide_ref[:, :, n * PIECE : (n + 1) * PIECE].reshape(2 * TOK, PIECE)
        return dot(xall_ref[order], columns).astype(BF16)

    fline_ref[...] = summed(0, 1).reshape(DEPTH, 4 * PLANE, PIECE)
    for i in range(1, DEPTH):
        first_line(i).start()
    for n in range(1, 1024 // PIECE):
        part_ref[:, :, (n - 1) * PIECE : n * PIECE] = summed(n, 0).reshape(PLANE, 32, PIECE)
    for i in range(1, PLANE):
        plane_copy(i).start()
    total = fline_ref[z].astype(F32)
    for i in range(1, DEPTH):
        first_line(i).wait_recv()
        total = total + flined_ref[i - 1].astype(F32)
    for m in range(PLANE):
        rows = total[4 * m : 4 * m + 4, :]
        fplane_ref[m] = jnp.concatenate([rows[:, : PIECE // 2], rows[:, PIECE // 2 :]], axis=0)
    for m in range(1, PLANE):
        first_plane(m).start()
    half = (1024 - PIECE) // 2
    total = part_ref[yx].astype(F32)
    for i in range(1, PLANE):
        plane_copy(i).wait_recv()
        total = total + plane_ref[i - 1].astype(F32)
    for i in range(DEPTH):
        rows = total[4 * i : 4 * i + 4, :]
        line_ref[i] = jnp.concatenate([rows[:, :half], rows[:, half:]], axis=0)
    for i in range(1, DEPTH):
        line_copy(i).start()
    result = fplane_ref[yx]
    for m in range(1, PLANE):
        first_plane(m).wait_recv()
        result = result + fplaned_ref[m - 1]
    out_ref[:, :PIECE] = jnp.concatenate([result[:4], result[4:]], axis=1)
    result = line_ref[z]
    for i in range(1, DEPTH):
        line_copy(i).wait_recv()
        result = result + lined_ref[i - 1]
    out_ref[:, PIECE:] = jnp.concatenate([result[:4], result[4:]], axis=1)

    for i in range(1, DEPTH):
        for kind in range(3):
            z_copy(i, kind).wait_send()
        back_copy(i).wait_send()
        line_copy(i).wait_send()
        first_line(i).wait_send()
    for i in range(DEPTH):
        all_rows(i).wait_send()
        key_copy(i).wait_send()
        all_returns(i).wait_send()
    for m in range(1, PLANE):
        label_copy(m).wait_send()
        plane_copy(m).wait_send()
        first_plane(m).wait_send()


def whole(cluster_of, slot_of, queries, out_grad, key_value, tokens_in):
    width = PLANE * BOUND
    dma = pltpu.SemaphoreType.DMA
    return pl.pallas_call(
        whole_kernel,
        out_shape=jax.ShapeDtypeStruct((4, 1024), F32),
        in_specs=[pl.BlockSpec(memory_space=pl.ANY)] * 6,
        out_specs=VMEM,
        scratch_shapes=[
            pltpu.VMEM((TOK, H), jnp.int32),
            pltpu.VMEM((TOK, H), jnp.int32),
            pltpu.VMEM((TOK, H * HD), BF16),
            pltpu.VMEM((TOK, H * HD), BF16),
            pltpu.VMEM((TOK, 2 * HD), BF16),
            pltpu.VMEM((TOK, 1024), BF16),
            pltpu.VMEM((ROWS, 2 * HD), BF16),
            pltpu.VMEM((DEPTH, width, 2 * HD), BF16),
            pltpu.VMEM((DEPTH, width, 2 * HD), BF16),
            pltpu.VMEM((DEPTH, TOK, 2 * HD), BF16),
            pltpu.VMEM((DEPTH, 4, 128), jnp.int32),
            pltpu.VMEM((DEPTH, 4, 128), jnp.int32),
            pltpu.VMEM((4, DEPTH, 128), jnp.int32),
            pltpu.VMEM((PLANE, DEPTH, 128), jnp.int32),
            pltpu.VMEM((DEPTH, PLANE, BOUND, 4 * HD), BF16),
            pltpu.VMEM((DEPTH, PLANE, BOUND, 4 * HD), BF16),
            pltpu.VMEM((CL_DEV, HALF, 4 * HD), F32),
            pltpu.VMEM((CL_DEV, HALF, 2 * HD), BF16),
            pltpu.VMEM((CL_DEV, HALF, 2 * HD), BF16),
            pltpu.VMEM((CL_DEV, 4, 128), F32),
            pltpu.VMEM((CL_DEV, HALF, 2 * HD), BF16),
            pltpu.VMEM((CL_DEV, 4, 128), F32),
            pltpu.VMEM((2 * HALF, 4 * HD), BF16),
            pltpu.VMEM((DEPTH, PLANE, BOUND // 2, 2 * HD), BF16),
            pltpu.VMEM((DEPTH, PLANE, BOUND // 2, 2 * HD), BF16),
            pltpu.VMEM((DEPTH, PLANE, BOUND // 2, 2 * HD), BF16),
            pltpu.VMEM((ROWS, GROUPS * BOUND // 2), BF16),
            pltpu.VMEM((ROWS, 2 * HD), F32),
            pltpu.VMEM((2, 512, TOK), BF16),
            pltpu.VMEM((512, TOK), BF16),
            pltpu.VMEM((2, 512, 2 * TOK), BF16),
            pltpu.VMEM((2, TOK, 1024), BF16),
            pltpu.VMEM((DEPTH, 4 * PLANE, PIECE), BF16),
            pltpu.VMEM((DEPTH - 1, 4 * PLANE, PIECE), BF16),
            pltpu.VMEM((PLANE, 8, PIECE // 2), F32),
            pltpu.VMEM((PLANE - 1, 8, PIECE // 2), F32),
            pltpu.VMEM((PLANE, 32, 1024 - PIECE), BF16),
            pltpu.VMEM((PLANE - 1, 32, 1024 - PIECE), BF16),
            pltpu.VMEM((DEPTH, 8, (1024 - PIECE) // 2), F32),
            pltpu.VMEM((DEPTH - 1, 8, (1024 - PIECE) // 2), F32),
            dma((DEPTH, 3)),
            dma((DEPTH, 3)),
            dma((PLANE,)),
            dma((PLANE,)),
            dma((DEPTH,)),
            dma((DEPTH,)),
            dma((CL_DEV + 1,)),
            dma((CL_DEV + 1,)),
            dma((DEPTH,)),
            dma((DEPTH,)),
            dma((DEPTH,)),
            dma((DEPTH,)),
            dma((1 + 1024 // PIECE,)),
            dma((1 + 1024 // PIECE,)),
            dma((PLANE - 1,)),
            dma((PLANE - 1,)),
            dma((DEPTH - 1,)),
            dma((DEPTH - 1,)),
            dma((PLANE - 1,)),
            dma((PLANE - 1,)),
            dma((DEPTH - 1,)),
            dma((DEPTH - 1,)),
            dma((6,)),
        ],
        compiler_params=params(0),
    )(cluster_of, slot_of, queries, out_grad, key_value, tokens_in)


def on_device(tokens_in, queries, key_value, out_grad, cluster_of, slot_of):
    return whole(cluster_of, slot_of, queries, out_grad, key_value, tokens_in)


def solution(mesh):
    spec = P(("seq", "pair"), None)
    return jax.shard_map(
        on_device, mesh=mesh, in_specs=(spec,) * 6, out_specs=spec, check_vma=False
    )
```

```python
import jax
import jax.numpy as jnp
from jax import lax
from jax.experimental import pallas as pl
from jax.experimental.pallas import tpu as pltpu
from jax.sharding import PartitionSpec as P

H = 16
HD = 64
HALF = 512
CL_DEV = 8
TOK = 128
ROWS = TOK * H
SLOTS = CL_DEV * HALF
GROUPS = 128
BOUND = 32
PLANE = 16
DEPTH = 8
ORDER = [0, 1, 7, 2, 6, 3, 5, 4]
LAG = 2
EARLY = 3
JOINT = 4
PIECE = 256
MESH = pl.DeviceIdType.MESH
F32 = jnp.float32
BF16 = jnp.bfloat16
VMEM = pl.BlockSpec(memory_space=pltpu.VMEM)


def params(collective=None):
    if collective is None:
        return pltpu.CompilerParams(vmem_limit_bytes=56 * 2**20)
    return pltpu.CompilerParams(
        vmem_limit_bytes=56 * 2**20, collective_id=collective, has_side_effects=True
    )


def iota(shape, dim):
    return lax.broadcasted_iota(jnp.int32, shape, dim)


def one_hot(mask):
    return jnp.where(mask, 1.0, 0.0).astype(BF16)


def dot(a, b):
    return jnp.dot(a, b, preferred_element_type=F32)


def dot_t(a, b):
    return lax.dot_general(a, b, (((1,), (1,)), ((), ())), preferred_element_type=F32)


def t_dot(a, b):
    return lax.dot_general(a, b, (((0,), (0,)), ((), ())), preferred_element_type=F32)


def whole_kernel(
    cluster_in, slot_in, q_in, g_in, kv_in, x_in, out_ref,
    cluster_ref, slot_ref, q_ref, g_ref, kvin_ref, x_ref, flat_ref, zsend_ref, zgot_ref, zkv_ref, zlab_ref, zlabgot_ref, group_ref, plab_ref,
    fwd_ref, rows_ref, total_ref, qg_ref, kv_ref, live_ref, kv2_ref, live2_ref, grads_ref,
    back_ref, zback_ref, got_ref, hot_ref, target_ref, found_ref, xt_ref, xo_ref, xall_ref, wide_ref,
    fline_ref, flined_ref, fplane_ref, fplaned_ref, part_ref, plane_ref, line_ref, lined_ref,
    fsend_sem, frecv_sem, lsend_sem, lrecv_sem, wsend_sem, wrecv_sem, ksend_sem, krecv_sem,
    bsend_sem, brecv_sem, rsend_sem, rrecv_sem, psend_sem, precv_sem, ysend_sem, yrecv_sem,
    zsend_sem, zrecv_sem, fysend_sem, fyrecv_sem, fzsend_sem, fzrecv_sem, in_sem,
):
    seq, pair = lax.axis_index("seq"), lax.axis_index("pair")
    other = (seq, 1 - pair)
    yx, z = seq // DEPTH, lax.rem(seq, DEPTH)
    width = PLANE * BOUND
    rest = pl.ds(1, PLANE - 1)

    def on_line(i):
        return (yx * DEPTH + lax.rem(z + i, DEPTH), pair)

    def in_plane(m):
        return (lax.rem(yx + m, PLANE) * DEPTH + z, pair)

    def remote(source, target, send_sem, recv_sem, to):
        return pltpu.make_async_remote_copy(
            src_ref=source, dst_ref=target, send_sem=send_sem, recv_sem=recv_sem,
            device_id=to, device_id_type=MESH,
        )

    barrier = pltpu.get_barrier_semaphore()
    for i in range(1, DEPTH):
        pl.semaphore_signal(barrier, inc=1, device_id=on_line(i), device_id_type=MESH)
    for m in range(1, PLANE):
        pl.semaphore_signal(barrier, inc=1, device_id=in_plane(m), device_id_type=MESH)
    pl.semaphore_signal(barrier, inc=1, device_id=other, device_id_type=MESH)

    loads = [
        pltpu.make_async_copy(source, target, in_sem.at[n])
        for n, (source, target) in enumerate(
            (
                (cluster_in, cluster_ref), (slot_in, slot_ref), (q_in, q_ref), (g_in, g_ref),
                (kv_in, kvin_ref), (x_in, x_ref),
            )
        )
    ]
    for load in loads:
        load.start()
    for load in loads[:2]:
        load.wait()

    def in_lanes(ref):
        return jnp.concatenate([ref[h : h + 1, :] for h in range(H)], axis=1)

    cluster = in_lanes(cluster_ref)
    slot = in_lanes(slot_ref)
    owner = lax.shift_right_logical(cluster, 3)
    local = (cluster & (CL_DEV - 1)) * HALF + (slot & (HALF - 1))
    before = one_hot(iota((TOK, TOK), 0) < iota((TOK, TOK), 1))
    base = jnp.zeros((GROUPS, 1), F32)
    ranks = []
    for h in range(H):
        mine = owner[:, h * TOK : (h + 1) * TOK]
        pick = jnp.where(iota((GROUPS, TOK), 0) == mine, 1.0, 0.0)
        count = dot(pick.astype(BF16), before) + base
        ranks.append(jnp.sum(pick * count, axis=0, keepdims=True))
        base = base + jnp.sum(pick, axis=1, keepdims=True)
    rank = jnp.concatenate(ranks, axis=1).astype(jnp.int32)
    place = (owner & (DEPTH - 1)) * width + lax.shift_right_logical(owner, 3) * BOUND + rank
    in_row = jnp.where(iota((32, ROWS), 0) == lax.shift_right_logical(place, 7), 1.0, 0.0)
    in_lane = one_hot(iota((128, ROWS), 0) == (place & 127))
    token = iota((1, ROWS), 1) & (TOK - 1)
    parts = [lax.shift_right_logical(local, 6), local & 63, token]
    stacked = [(in_row * part.astype(F32)).astype(BF16) for part in parts] + [in_row.astype(BF16)]
    found = dot_t(jnp.concatenate(stacked, axis=0), in_lane)
    label = jnp.where(
        found[96:128] > 0.5, (found[0:32] * 64.0 + found[32:64]) * 128.0 + found[64:96], -1.0
    ).astype(jnp.int32)
    for i in range(DEPTH):
        zlab_ref[i] = label[4 * i : 4 * i + 4, :]
    for load in loads[2:]:
        load.wait()
    for h in range(H):
        cut = slice(h * HD, (h + 1) * HD)
        flat_ref[h * TOK : (h + 1) * TOK, :] = jnp.concatenate([q_ref[:, cut], g_ref[:, cut]], axis=1)
    def pack(i):
        to = lax.rem(z + i, DEPTH)
        hot = one_hot(iota((width, ROWS), 0) == place - to * width)
        zsend_ref[i] = dot(hot, flat_ref[...]).astype(BF16)

    for i in ORDER[1:EARLY]:
        pack(i)

    def z_copy(i, kind):
        to = lax.rem(z + i, DEPTH)
        source, target = (
            (zlab_ref.at[to], zlabgot_ref.at[i]),
            (kvin_ref, zkv_ref.at[i]),
            (zsend_ref.at[i], zgot_ref.at[i]),
        )[kind]
        return remote(source, target, fsend_sem.at[i, kind], frecv_sem.at[i, kind], on_line(i))

    pl.semaphore_wait(barrier, DEPTH - 1 + PLANE - 1 + 1)
    for i in ORDER[1:]:
        z_copy(i, 0).start()
    for n, i in enumerate(ORDER[1:], 1):
        if n >= EARLY:
            pack(i)
        z_copy(i, 1).start()
        z_copy(i, 2).start()
    pack(0)

    def row_copy(i, m):
        to = lax.rem(yx + m, PLANE)
        return remote(
            fwd_ref.at[i, to], rows_ref.at[i, m], wsend_sem.at[i], wrecv_sem.at[i], in_plane(m)
        )

    def all_rows(i):
        return remote(
            fwd_ref.at[i, rest], rows_ref.at[i, rest], wsend_sem.at[i], wrecv_sem.at[i], other
        )

    def pass_on(i):
        if i:
            z_copy(i, 1).wait_recv()
            z_copy(i, 2).wait_recv()
        labels = jnp.concatenate([zlabgot_ref[i, g : g + 1, :] for g in range(4)], axis=1)
        hot = one_hot(iota((TOK, width), 0) == (labels & (TOK - 1)))
        pairs = t_dot(hot, zkv_ref[i] if i else kvin_ref[...]).astype(BF16)
        rows = zgot_ref[i] if i else zsend_ref[0]
        fwd_ref[i] = jnp.concatenate([rows, pairs], axis=1).reshape(PLANE, BOUND, 4 * HD)

        def send(m, carry):
            row_copy(i, m).start()
            return carry

        lax.fori_loop(1, PLANE, send, 0)
        rows_ref[i, 0] = fwd_ref[i, yx]

    zlabgot_ref[0] = zlab_ref[z]
    pass_on(0)

    for i in ORDER[1:]:
        z_copy(i, 0).wait_recv()
    for i in range(DEPTH):
        for g in range(4):
            group_ref[g, i : i + 1, :] = zlabgot_ref[i, g : g + 1, :]

    def label_copy(m):
        to = lax.rem(yx + m, PLANE)
        return remote(
            group_ref.at[to // 4], plab_ref.at[m], lsend_sem.at[m], lrecv_sem.at[m], in_plane(m)
        )

    for m in range(1, PLANE):
        label_copy(m).start()
    plab_ref[0] = group_ref[yx // 4]

    pass_on(ORDER[1])
    for m in range(1, PLANE):
        label_copy(m).wait_recv()
    quarter = lax.rem(yx, 4)
    lanes = []
    live = jnp.zeros((SLOTS // 128, 128), F32)
    for i in range(DEPTH):
        given = plab_ref[:, i, :]
        mine = given[:, 3 * BOUND :]
        for g in range(3):
            mine = jnp.where(quarter == g, given[:, g * BOUND : (g + 1) * BOUND], mine)
        lane = jnp.concatenate([mine[m : m + 1, :] for m in range(PLANE)], axis=1)
        lane = lax.shift_right_arithmetic(lane, 7)
        lanes.append(lane)
        live = live + dot_t(
            one_hot(iota((SLOTS // 128, width), 0) == lax.shift_right_arithmetic(lane, 7)),
            one_hot(iota((128, width), 0) == (lane & 127)),
        )
    for c in range(CL_DEV):
        live_ref[c] = live[4 * c : 4 * c + 4, :]
    live_copy = remote(
        live_ref, live2_ref, ksend_sem.at[CL_DEV], krecv_sem.at[CL_DEV], other
    )
    live_copy.start()

    def key_copy(c):
        return remote(kv_ref.at[c], kv2_ref.at[c], ksend_sem.at[c], krecv_sem.at[c], other)

    def arrange(i, first, last):
        all_rows(i).wait_recv()
        lane = lanes[i]
        for b in range(CL_DEV):
            hot = one_hot(iota((HALF, width), 0) == lane - b * HALF)
            term = dot(hot, rows_ref[i].reshape(width, 4 * HD))
            if first:
                total_ref[b] = term
            elif not last:
                total_ref[b] += term
            else:
                done = (total_ref[b] + term).astype(BF16)
                qg_ref[b] = done[:, : 2 * HD]
                kv_ref[b] = done[:, 2 * HD :]
                key_copy(b).start()

    x_copy = remote(xt_ref.at[1 - pair], xo_ref, psend_sem.at[0], precv_sem.at[0], other)

    def turn_x():
        position = iota((512, 1024), 0)
        for p in range(2):
            column = lax.shift_right_logical(position, 2) * 8 + 4 * p + (position & 3)
            xt_ref[p] = dot_t(one_hot(iota((512, 1024), 1) == column), x_ref[...]).astype(BF16)
        x_copy.start()

    def join_x():
        x_copy.wait()
        both = jnp.concatenate([xt_ref[pair], xo_ref[...]], axis=1)
        xall_ref[0] = both
        position = iota((512, 512), 0)
        row = (lax.shift_right_logical(position, 2) & (PLANE - 1)) * 32
        row = row + lax.shift_right_logical(position, 6) * 4 + (position & 3)
        xall_ref[1] = dot(one_hot(iota((512, 512), 1) == row), both).astype(BF16)

    def find_targets():
        for h in range(H):
            cut = slice(h * TOK, (h + 1) * TOK)
            to = owner[:, cut]
            line = (to + (DEPTH - z)) & (DEPTH - 1)
            plane = (lax.shift_right_logical(to, 3) + (PLANE - yx)) & (PLANE - 1)
            target = line * (width // 2) + plane * (BOUND // 2) + (rank[:, cut] & (BOUND // 2 - 1))
            target = jnp.broadcast_to(target, (TOK, TOK)).T
            target_ref[cut, :] = target

    for n in range(2, DEPTH + LAG):
        if n < DEPTH:
            pass_on(ORDER[n])
        if n >= LAG:
            arrange(ORDER[n - LAG], n == LAG, n == DEPTH + LAG - 1)
        if n == 3:
            turn_x()
        if n == 4:
            find_targets()
        if n == 5:
            join_x()

    live_copy.wait()
    for c in range(CL_DEV):
        if c % JOINT == 0:
            for e in range(c, c + JOINT):
                key_copy(e).wait_recv()
        queries = qg_ref[c, :, :HD] * BF16(HD**-0.5)
        grads = qg_ref[c, :, HD:]
        keys = jnp.concatenate([kv_ref[c, :, :HD], kv2_ref[c, :, :HD]], axis=0)
        values = jnp.concatenate([kv_ref[c, :, HD:], kv2_ref[c, :, HD:]], axis=0)
        alive = jnp.concatenate(
            [ref[c, r : r + 1, :] for ref in (live_ref, live2_ref) for r in range(4)], axis=1
        )
        scores = dot_t(queries, keys) + jnp.where(alive > 0.5, 0.0, -1e30)
        prob_grad = dot_t(grads, values)
        weights = jnp.exp(scores - jnp.max(scores, axis=1, keepdims=True))
        inverse = 1.0 / jnp.sum(weights, axis=1, keepdims=True)
        row_dot = jnp.sum(weights * prob_grad, axis=1, keepdims=True) * inverse
        score_grad = (weights * (prob_grad - row_dot) * (inverse * (HD**-0.5))).astype(BF16)
        grads_ref[
            (c % 2) * HALF : (c % 2 + 1) * HALF, (c // 2) * HD : (c // 2 + 1) * HD
        ] = dot(score_grad, keys).astype(BF16)

    def back_copy(i):
        return remote(
            back_ref.at[i], zback_ref.at[i], bsend_sem.at[i], brecv_sem.at[i], on_line(DEPTH - i)
        )

    for i in ORDER[1:] + ORDER[:1]:
        labels = jnp.broadcast_to(lanes[i], (128, width)).T
        low = labels & 1023
        hot = jnp.concatenate(
            [one_hot(low == iota((width, 128), 1) + 128 * b) for b in range(8)], axis=1
        )
        found = dot(hot, grads_ref[...])
        high = lax.shift_right_arithmetic(labels[:, :HD], 10)
        row = jnp.zeros((width, HD), F32)
        for a in range(4):
            row = row + jnp.where(high == a, found[:, a * HD : (a + 1) * HD], 0.0)
        row = row.reshape(PLANE, BOUND, HD)
        row = jnp.concatenate([row[:, : BOUND // 2], row[:, BOUND // 2 :]], axis=2).astype(BF16)
        if i:
            back_ref[i] = row
            back_copy(i).start()
        else:
            zback_ref[0] = row

    def return_copy(i, m):
        return remote(
            zback_ref.at[i, m], got_ref.at[i, m], rsend_sem.at[i], rrecv_sem.at[i],
            in_plane(PLANE - m),
        )

    def all_returns(i):
        return remote(
            zback_ref.at[i, rest], got_ref.at[i, rest], rsend_sem.at[i], rrecv_sem.at[i], other
        )

    def take(i, first):
        all_returns(i).wait_recv()
        half = width // 2
        term = dot(
            hot_ref[:, i * half : (i + 1) * half], got_ref[i].reshape(half, 2 * HD)
        )
        if first:
            found_ref[...] = term
        else:
            found_ref[...] += term

    for n in range(DEPTH + LAG):
        if n < DEPTH:
            i = ORDER[n]
            if i:
                back_copy(i).wait_recv()

            def send(m, carry, i=i):
                return_copy(i, m).start()
                return carry

            lax.fori_loop(1, PLANE, send, 0)
            got_ref[i, 0] = zback_ref[i, 0]
            for b in range(i * width // 2, (i + 1) * width // 2, 128):
                hot_ref[:, b : b + 128] = one_hot(target_ref[...] == iota((ROWS, 128), 1) + b)
        if n >= LAG:
            take(ORDER[n - LAG], n == LAG)
    def g_copy(n):
        cut = pl.ds(n * PIECE, PIECE)
        return remote(
            wide_ref.at[0, :, cut], wide_ref.at[1, :, cut], psend_sem.at[1 + n],
            precv_sem.at[1 + n], other,
        )

    for h in range(0, H, 2):
        pieces = []
        for e in range(2):
            cut = slice((h + e) * TOK, (h + e + 1) * TOK)
            upper = (jnp.broadcast_to(rank[:, cut], (TOK, TOK)).T[:, :HD] & (BOUND // 2)) > 0
            piece = found_ref[cut, :]
            pieces.append(jnp.where(upper, piece[:, HD:], piece[:, :HD]))
        wide_ref[0, :, h * HD : (h + 2) * HD] = jnp.concatenate(pieces, axis=1).astype(BF16)
        if (h + 2) * HD % PIECE == 0:
            g_copy(h * HD // PIECE).start()

    def first_line(i):
        return remote(
            fline_ref.at[lax.rem(z + i, DEPTH)], flined_ref.at[i - 1], fzsend_sem.at[i - 1],
            fzrecv_sem.at[i - 1], on_line(i),
        )

    def first_plane(m):
        return remote(
            fplane_ref.at[lax.rem(yx + m, PLANE)], fplaned_ref.at[m - 1], fysend_sem.at[m - 1],
            fyrecv_sem.at[m - 1], in_plane(m),
        )

    def plane_copy(i):
        return remote(
            part_ref.at[lax.rem(yx + i, PLANE)], plane_ref.at[i - 1], ysend_sem.at[i - 1],
            yrecv_sem.at[i - 1], in_plane(i),
        )

    def line_copy(i):
        return remote(
            line_ref.at[lax.rem(z + i, DEPTH)], lined_ref.at[i - 1], zsend_sem.at[i - 1],
            zrecv_sem.at[i - 1], on_line(i),
        )

    def summed(n, order):
        g_copy(n).wait()
        columns = wide_ref[:, :, n * PIECE : (n + 1) * PIECE].reshape(2 * TOK, PIECE)
        return dot(xall_ref[order], columns).astype(BF16)

    fline_ref[...] = summed(0, 1).reshape(DEPTH, 4 * PLANE, PIECE)
    for i in range(1, DEPTH):
        first_line(i).start()
    for n in range(1, 1024 // PIECE):
        part_ref[:, :, (n - 1) * PIECE : n * PIECE] = summed(n, 0).reshape(PLANE, 32, PIECE)
    for i in range(1, PLANE):
        plane_copy(i).start()
    total = fline_ref[z].astype(F32)
    for i in range(1, DEPTH):
        first_line(i).wait_recv()
        total = total + flined_ref[i - 1].astype(F32)
    for m in range(PLANE):
        rows = total[4 * m : 4 * m + 4, :]
        fplane_ref[m] = jnp.concatenate([rows[:, : PIECE // 2], rows[:, PIECE // 2 :]], axis=0)
    for m in range(1, PLANE):
        first_plane(m).start()
    half = (1024 - PIECE) // 2
    total = part_ref[yx].astype(F32)
    for i in range(1, PLANE):
        plane_copy(i).wait_recv()
        total = total + plane_ref[i - 1].astype(F32)
    for i in range(DEPTH):
        rows = total[4 * i : 4 * i + 4, :]
        line_ref[i] = jnp.concatenate([rows[:, :half], rows[:, half:]], axis=0)
    for i in range(1, DEPTH):
        line_copy(i).start()
    result = fplane_ref[yx]
    for m in range(1, PLANE):
        first_plane(m).wait_recv()
        result = result + fplaned_ref[m - 1]
    out_ref[:, :PIECE] = jnp.concatenate([result[:4], result[4:]], axis=1)
    result = line_ref[z]
    for i in range(1, DEPTH):
        line_copy(i).wait_recv()
        result = result + lined_ref[i - 1]
    out_ref[:, PIECE:] = jnp.concatenate([result[:4], result[4:]], axis=1)

    for i in range(1, DEPTH):
        for kind in range(3):
            z_copy(i, kind).wait_send()
        back_copy(i).wait_send()
        line_copy(i).wait_send()
        first_line(i).wait_send()
    for i in range(DEPTH):
        all_rows(i).wait_send()
        key_copy(i).wait_send()
        all_returns(i).wait_send()
    for m in range(1, PLANE):
        label_copy(m).wait_send()
        plane_copy(m).wait_send()
        first_plane(m).wait_send()


def whole(cluster_of, slot_of, queries, out_grad, key_value, tokens_in):
    width = PLANE * BOUND
    dma = pltpu.SemaphoreType.DMA
    return pl.pallas_call(
        whole_kernel,
        out_shape=jax.ShapeDtypeStruct((4, 1024), F32),
        in_specs=[pl.BlockSpec(memory_space=pl.ANY)] * 6,
        out_specs=VMEM,
        scratch_shapes=[
            pltpu.VMEM((H, TOK), jnp.int32),
            pltpu.VMEM((H, TOK), jnp.int32),
            pltpu.VMEM((TOK, H * HD), BF16),
            pltpu.VMEM((TOK, H * HD), BF16),
            pltpu.VMEM((TOK, 2 * HD), BF16),
            pltpu.VMEM((TOK, 1024), BF16),
            pltpu.VMEM((ROWS, 2 * HD), BF16),
            pltpu.VMEM((DEPTH, width, 2 * HD), BF16),
            pltpu.VMEM((DEPTH, width, 2 * HD), BF16),
            pltpu.VMEM((DEPTH, TOK, 2 * HD), BF16),
            pltpu.VMEM((DEPTH, 4, 128), jnp.int32),
            pltpu.VMEM((DEPTH, 4, 128), jnp.int32),
            pltpu.VMEM((4, DEPTH, 128), jnp.int32),
            pltpu.VMEM((PLANE, DEPTH, 128), jnp.int32),
            pltpu.VMEM((DEPTH, PLANE, BOUND, 4 * HD), BF16),
            pltpu.VMEM((DEPTH, PLANE, BOUND, 4 * HD), BF16),
            pltpu.VMEM((CL_DEV, HALF, 4 * HD), F32),
            pltpu.VMEM((CL_DEV, HALF, 2 * HD), BF16),
            pltpu.VMEM((CL_DEV, HALF, 2 * HD), BF16),
            pltpu.VMEM((CL_DEV, 4, 128), F32),
            pltpu.VMEM((CL_DEV, HALF, 2 * HD), BF16),
            pltpu.VMEM((CL_DEV, 4, 128), F32),
            pltpu.VMEM((2 * HALF, 4 * HD), BF16),
            pltpu.VMEM((DEPTH, PLANE, BOUND // 2, 2 * HD), BF16),
            pltpu.VMEM((DEPTH, PLANE, BOUND // 2, 2 * HD), BF16),
            pltpu.VMEM((DEPTH, PLANE, BOUND // 2, 2 * HD), BF16),
            pltpu.VMEM((ROWS, GROUPS * BOUND // 2), BF16),
            pltpu.VMEM((ROWS, 128), jnp.int32),
            pltpu.VMEM((ROWS, 2 * HD), F32),
            pltpu.VMEM((2, 512, TOK), BF16),
            pltpu.VMEM((512, TOK), BF16),
            pltpu.VMEM((2, 512, 2 * TOK), BF16),
            pltpu.VMEM((2, TOK, 1024), BF16),
            pltpu.VMEM((DEPTH, 4 * PLANE, PIECE), BF16),
            pltpu.VMEM((DEPTH - 1, 4 * PLANE, PIECE), BF16),
            pltpu.VMEM((PLANE, 8, PIECE // 2), F32),
            pltpu.VMEM((PLANE - 1, 8, PIECE // 2), F32),
            pltpu.VMEM((PLANE, 32, 1024 - PIECE), BF16),
            pltpu.VMEM((PLANE - 1, 32, 1024 - PIECE), BF16),
            pltpu.VMEM((DEPTH, 8, (1024 - PIECE) // 2), F32),
            pltpu.VMEM((DEPTH - 1, 8, (1024 - PIECE) // 2), F32),
            dma((DEPTH, 3)),
            dma((DEPTH, 3)),
            dma((PLANE,)),
            dma((PLANE,)),
            dma((DEPTH,)),
            dma((DEPTH,)),
            dma((CL_DEV + 1,)),
            dma((CL_DEV + 1,)),
            dma((DEPTH,)),
            dma((DEPTH,)),
            dma((DEPTH,)),
            dma((DEPTH,)),
            dma((1 + 1024 // PIECE,)),
            dma((1 + 1024 // PIECE,)),
            dma((PLANE - 1,)),
            dma((PLANE - 1,)),
            dma((DEPTH - 1,)),
            dma((DEPTH - 1,)),
            dma((PLANE - 1,)),
            dma((PLANE - 1,)),
            dma((DEPTH - 1,)),
            dma((DEPTH - 1,)),
            dma((6,)),
        ],
        compiler_params=params(0),
    )(cluster_of, slot_of, queries, out_grad, key_value, tokens_in)


def on_device(tokens_in, queries, key_value, out_grad, cluster_of, slot_of):
    return whole(cluster_of.T, slot_of.T, queries, out_grad, key_value, tokens_in)


def solution(mesh):
    spec = P(("seq", "pair"), None)
    return jax.shard_map(
        on_device, mesh=mesh, in_specs=(spec,) * 6, out_specs=spec, check_vma=False
    )
```

```python
import jax
import jax.numpy as jnp
from jax import lax
from jax.experimental import pallas as pl
from jax.experimental.pallas import tpu as pltpu
from jax.sharding import PartitionSpec as P

H = 16
HD = 64
HALF = 512
CL_DEV = 8
TOK = 128
ROWS = TOK * H
SLOTS = CL_DEV * HALF
GROUPS = 128
BOUND = 32
PLANE = 16
DEPTH = 8
ORDER = [0, 1, 7, 2, 6, 3, 5, 4]
LAG = 2
EARLY = 3
JOINT = 4
PIECE = 256
Z_FIRST = (4, 2, 6)
RETURN = [4, 3, 2, 5, 6, 1, 7, 0]
RELAY = [3, 2, 5, 6, 1, 4, 7]
TAKE = [0, 2, 6, 4, 3, 5, 1, 7]
MESH = pl.DeviceIdType.MESH
F32 = jnp.float32
BF16 = jnp.bfloat16
VMEM = pl.BlockSpec(memory_space=pltpu.VMEM)


def params(collective=None):
    if collective is None:
        return pltpu.CompilerParams(vmem_limit_bytes=56 * 2**20)
    return pltpu.CompilerParams(
        vmem_limit_bytes=56 * 2**20, collective_id=collective, has_side_effects=True
    )


def iota(shape, dim):
    return lax.broadcasted_iota(jnp.int32, shape, dim)


def one_hot(mask):
    return jnp.where(mask, 1.0, 0.0).astype(BF16)


def dot(a, b):
    return jnp.dot(a, b, preferred_element_type=F32)


def dot_t(a, b):
    return lax.dot_general(a, b, (((1,), (1,)), ((), ())), preferred_element_type=F32)


def t_dot(a, b):
    return lax.dot_general(a, b, (((0,), (0,)), ((), ())), preferred_element_type=F32)


def whole_kernel(
    cluster_in, slot_in, q_in, g_in, kv_in, x_in, out_ref,
    cluster_ref, slot_ref, q_ref, g_ref, kvin_ref, x_ref, flat_ref, zsend_ref, zgot_ref, zkv_ref, zlab_ref, zlabgot_ref, group_ref, plab_ref,
    fwd_ref, rows_ref, total_ref, qg_ref, kv_ref, live_ref, kv2_ref, live2_ref, grads_ref,
    back_ref, zback_ref, got_ref, hot_ref, target_ref, found_ref, xt_ref, xo_ref, xall_ref, wide_ref,
    fline_ref, flined_ref, fplane_ref, fplaned_ref, part_ref, plane_ref, line_ref, lined_ref,
    fsend_sem, frecv_sem, lsend_sem, lrecv_sem, wsend_sem, wrecv_sem, ksend_sem, krecv_sem,
    bsend_sem, brecv_sem, rsend_sem, rrecv_sem, psend_sem, precv_sem, ysend_sem, yrecv_sem,
    zsend_sem, zrecv_sem, fysend_sem, fyrecv_sem, fzsend_sem, fzrecv_sem, in_sem,
):
    seq, pair = lax.axis_index("seq"), lax.axis_index("pair")
    other = (seq, 1 - pair)
    yx, z = seq // DEPTH, lax.rem(seq, DEPTH)
    width = PLANE * BOUND
    rest = pl.ds(1, PLANE - 1)

    def on_line(i):
        return (yx * DEPTH + lax.rem(z + i, DEPTH), pair)

    def in_plane(m):
        return (lax.rem(yx + m, PLANE) * DEPTH + z, pair)

    def remote(source, target, send_sem, recv_sem, to):
        return pltpu.make_async_remote_copy(
            src_ref=source, dst_ref=target, send_sem=send_sem, recv_sem=recv_sem,
            device_id=to, device_id_type=MESH,
        )

    barrier = pltpu.get_barrier_semaphore()
    for i in range(1, DEPTH):
        pl.semaphore_signal(barrier, inc=1, device_id=on_line(i), device_id_type=MESH)
    for m in range(1, PLANE):
        pl.semaphore_signal(barrier, inc=1, device_id=in_plane(m), device_id_type=MESH)
    pl.semaphore_signal(barrier, inc=1, device_id=other, device_id_type=MESH)

    loads = [
        pltpu.make_async_copy(source, target, in_sem.at[n])
        for n, (source, target) in enumerate(
            (
                (cluster_in, cluster_ref), (slot_in, slot_ref), (q_in, q_ref), (g_in, g_ref),
                (kv_in, kvin_ref), (x_in, x_ref),
            )
        )
    ]
    for load in loads:
        load.start()
    for load in loads[:2]:
        load.wait()

    def in_lanes(ref):
        return jnp.concatenate([ref[h : h + 1, :] for h in range(H)], axis=1)

    cluster = in_lanes(cluster_ref)
    slot = in_lanes(slot_ref)
    owner = lax.shift_right_logical(cluster, 3)
    local = (cluster & (CL_DEV - 1)) * HALF + (slot & (HALF - 1))
    before = one_hot(iota((TOK, TOK), 0) < iota((TOK, TOK), 1))
    base = jnp.zeros((GROUPS, 1), F32)
    ranks = []
    for h in range(H):
        mine = owner[:, h * TOK : (h + 1) * TOK]
        pick = jnp.where(iota((GROUPS, TOK), 0) == mine, 1.0, 0.0)
        count = dot(pick.astype(BF16), before) + base
        ranks.append(jnp.sum(pick * count, axis=0, keepdims=True))
        base = base + jnp.sum(pick, axis=1, keepdims=True)
    rank = jnp.concatenate(ranks, axis=1).astype(jnp.int32)
    place = (owner & (DEPTH - 1)) * width + lax.shift_right_logical(owner, 3) * BOUND + rank
    in_row = jnp.where(iota((32, ROWS), 0) == lax.shift_right_logical(place, 7), 1.0, 0.0)
    in_lane = one_hot(iota((128, ROWS), 0) == (place & 127))
    token = iota((1, ROWS), 1) & (TOK - 1)
    parts = [lax.shift_right_logical(local, 6), local & 63, token]
    stacked = [(in_row * part.astype(F32)).astype(BF16) for part in parts] + [in_row.astype(BF16)]
    found = dot_t(jnp.concatenate(stacked, axis=0), in_lane)
    label = jnp.where(
        found[96:128] > 0.5, (found[0:32] * 64.0 + found[32:64]) * 128.0 + found[64:96], -1.0
    ).astype(jnp.int32)
    for i in range(DEPTH):
        zlab_ref[i] = label[4 * i : 4 * i + 4, :]
    for load in loads[2:]:
        load.wait()
    for h in range(H):
        cut = slice(h * HD, (h + 1) * HD)
        flat_ref[h * TOK : (h + 1) * TOK, :] = jnp.concatenate([q_ref[:, cut], g_ref[:, cut]], axis=1)
    def pack(i):
        to = lax.rem(z + i, DEPTH)
        hot = one_hot(iota((width, ROWS), 0) == place - to * width)
        zsend_ref[i] = dot(hot, flat_ref[...]).astype(BF16)

    for i in ORDER[1:EARLY]:
        pack(i)

    def z_copy(i, kind):
        to = lax.rem(z + i, DEPTH)
        source, target = (
            (zlab_ref.at[to], zlabgot_ref.at[i]),
            (kvin_ref, zkv_ref.at[i]),
            (zsend_ref.at[i], zgot_ref.at[i]),
        )[kind]
        return remote(source, target, fsend_sem.at[i, kind], frecv_sem.at[i, kind], on_line(i))

    pl.semaphore_wait(barrier, DEPTH - 1 + PLANE - 1 + 1)
    for i in ORDER[1:]:
        z_copy(i, 0).start()
    for n, i in enumerate(ORDER[1:], 1):
        if n >= EARLY:
            pack(i)
        z_copy(i, 1).start()
        z_copy(i, 2).start()
    pack(0)

    def row_copy(i, m):
        to = lax.rem(yx + m, PLANE)
        return remote(
            fwd_ref.at[i, to], rows_ref.at[i, m], wsend_sem.at[i], wrecv_sem.at[i], in_plane(m)
        )

    def all_rows(i):
        return remote(
            fwd_ref.at[i, rest], rows_ref.at[i, rest], wsend_sem.at[i], wrecv_sem.at[i], other
        )

    def pass_on(i):
        if i:
            z_copy(i, 1).wait_recv()
            z_copy(i, 2).wait_recv()
        labels = jnp.concatenate([zlabgot_ref[i, g : g + 1, :] for g in range(4)], axis=1)
        hot = one_hot(iota((TOK, width), 0) == (labels & (TOK - 1)))
        pairs = t_dot(hot, zkv_ref[i] if i else kvin_ref[...]).astype(BF16)
        rows = zgot_ref[i] if i else zsend_ref[0]
        fwd_ref[i] = jnp.concatenate([rows, pairs], axis=1).reshape(PLANE, BOUND, 4 * HD)

        def send(m, carry):
            row_copy(i, m).start()
            return carry

        lax.fori_loop(1, PLANE, send, 0)
        rows_ref[i, 0] = fwd_ref[i, yx]

    zlabgot_ref[0] = zlab_ref[z]
    pass_on(0)

    for i in ORDER[1:]:
        z_copy(i, 0).wait_recv()
    for i in range(DEPTH):
        for g in range(4):
            group_ref[g, i : i + 1, :] = zlabgot_ref[i, g : g + 1, :]

    def label_copy(m):
        to = lax.rem(yx + m, PLANE)
        return remote(
            group_ref.at[to // 4], plab_ref.at[m], lsend_sem.at[m], lrecv_sem.at[m], in_plane(m)
        )

    for m in range(1, PLANE):
        label_copy(m).start()
    plab_ref[0] = group_ref[yx // 4]

    pass_on(ORDER[1])
    for m in range(1, PLANE):
        label_copy(m).wait_recv()
    quarter = lax.rem(yx, 4)
    lanes = []
    live = jnp.zeros((SLOTS // 128, 128), F32)
    for i in range(DEPTH):
        given = plab_ref[:, i, :]
        mine = given[:, 3 * BOUND :]
        for g in range(3):
            mine = jnp.where(quarter == g, given[:, g * BOUND : (g + 1) * BOUND], mine)
        lane = jnp.concatenate([mine[m : m + 1, :] for m in range(PLANE)], axis=1)
        lane = lax.shift_right_arithmetic(lane, 7)
        lanes.append(lane)
        live = live + dot_t(
            one_hot(iota((SLOTS // 128, width), 0) == lax.shift_right_arithmetic(lane, 7)),
            one_hot(iota((128, width), 0) == (lane & 127)),
        )
    for c in range(CL_DEV):
        live_ref[c] = live[4 * c : 4 * c + 4, :]
    live_copy = remote(
        live_ref, live2_ref, ksend_sem.at[CL_DEV], krecv_sem.at[CL_DEV], other
    )
    live_copy.start()

    def key_copy(c):
        return remote(kv_ref.at[c], kv2_ref.at[c], ksend_sem.at[c], krecv_sem.at[c], other)

    def arrange(i, first, last):
        all_rows(i).wait_recv()
        lane = lanes[i]
        for b in range(CL_DEV):
            hot = one_hot(iota((HALF, width), 0) == lane - b * HALF)
            term = dot(hot, rows_ref[i].reshape(width, 4 * HD))
            if first:
                total_ref[b] = term
            elif not last:
                total_ref[b] += term
            else:
                done = (total_ref[b] + term).astype(BF16)
                qg_ref[b] = done[:, : 2 * HD]
                kv_ref[b] = done[:, 2 * HD :]
                key_copy(b).start()

    x_copy = remote(xt_ref.at[1 - pair], xo_ref, psend_sem.at[0], precv_sem.at[0], other)

    def turn_x():
        position = iota((512, 1024), 0)
        for p in range(2):
            column = lax.shift_right_logical(position, 2) * 8 + 4 * p + (position & 3)
            xt_ref[p] = dot_t(one_hot(iota((512, 1024), 1) == column), x_ref[...]).astype(BF16)
        x_copy.start()

    def join_x():
        x_copy.wait()
        both = jnp.concatenate([xt_ref[pair], xo_ref[...]], axis=1)
        xall_ref[0] = both
        position = iota((512, 512), 0)
        row = (lax.shift_right_logical(position, 2) & (PLANE - 1)) * 32
        row = row + lax.shift_right_logical(position, 6) * 4 + (position & 3)
        xall_ref[1] = dot(one_hot(iota((512, 512), 1) == row), both).astype(BF16)

    def find_targets():
        for h in range(H):
            cut = slice(h * TOK, (h + 1) * TOK)
            to = owner[:, cut]
            line = (to + (DEPTH - z)) & (DEPTH - 1)
            plane = (lax.shift_right_logical(to, 3) + (PLANE - yx)) & (PLANE - 1)
            target = line * (width // 2) + plane * (BOUND // 2) + (rank[:, cut] & (BOUND // 2 - 1))
            target = jnp.broadcast_to(target, (TOK, TOK)).T
            target_ref[cut, :] = target

    for n in range(2, DEPTH + LAG):
        if n < DEPTH:
            pass_on(ORDER[n])
        if n >= LAG:
            arrange(ORDER[n - LAG], n == LAG, n == DEPTH + LAG - 1)
        if n == 3:
            turn_x()
        if n == 4:
            find_targets()
        if n == 5:
            join_x()

    live_copy.wait()
    for c in range(CL_DEV):
        if c % JOINT == 0:
            for e in range(c, c + JOINT):
                key_copy(e).wait_recv()
        queries = qg_ref[c, :, :HD] * BF16(HD**-0.5)
        grads = qg_ref[c, :, HD:]
        keys = jnp.concatenate([kv_ref[c, :, :HD], kv2_ref[c, :, :HD]], axis=0)
        values = jnp.concatenate([kv_ref[c, :, HD:], kv2_ref[c, :, HD:]], axis=0)
        alive = jnp.concatenate(
            [ref[c, r : r + 1, :] for ref in (live_ref, live2_ref) for r in range(4)], axis=1
        )
        scores = dot_t(queries, keys) + jnp.where(alive > 0.5, 0.0, -1e30)
        prob_grad = dot_t(grads, values)
        weights = jnp.exp(scores - jnp.max(scores, axis=1, keepdims=True))
        inverse = 1.0 / jnp.sum(weights, axis=1, keepdims=True)
        row_dot = jnp.sum(weights * prob_grad, axis=1, keepdims=True) * inverse
        score_grad = (weights * (prob_grad - row_dot) * (inverse * (HD**-0.5))).astype(BF16)
        grads_ref[
            (c % 2) * HALF : (c % 2 + 1) * HALF, (c // 2) * HD : (c // 2 + 1) * HD
        ] = dot(score_grad, keys).astype(BF16)

    def back_copy(i):
        source, target = (back_ref, zback_ref) if i in Z_FIRST else (zback_ref, got_ref)
        return remote(
            source.at[i], target.at[i], bsend_sem.at[i], brecv_sem.at[i], on_line(DEPTH - i)
        )

    def return_copy(i, m):
        source, target = (zback_ref, got_ref) if i in Z_FIRST or not i else (back_ref, zback_ref)
        return remote(
            source.at[i, m], target.at[i, m], rsend_sem.at[i], rrecv_sem.at[i], in_plane(PLANE - m)
        )

    def all_returns(i):
        source, target = (zback_ref, got_ref) if i in Z_FIRST or not i else (back_ref, zback_ref)
        return remote(
            source.at[i, rest], target.at[i, rest], rsend_sem.at[i], rrecv_sem.at[i], other
        )

    def return_all(i):
        def send(m, carry):
            return_copy(i, m).start()
            return carry

        lax.fori_loop(1, PLANE, send, 0)

    for i in RETURN:
        labels = jnp.broadcast_to(lanes[i], (128, width)).T
        low = labels & 1023
        hot = jnp.concatenate(
            [one_hot(low == iota((width, 128), 1) + 128 * b) for b in range(8)], axis=1
        )
        found = dot(hot, grads_ref[...])
        high = lax.shift_right_arithmetic(labels[:, :HD], 10)
        row = jnp.zeros((width, HD), F32)
        for a in range(4):
            row = row + jnp.where(high == a, found[:, a * HD : (a + 1) * HD], 0.0)
        row = row.reshape(PLANE, BOUND, HD)
        row = jnp.concatenate([row[:, : BOUND // 2], row[:, BOUND // 2 :]], axis=2).astype(BF16)
        if i == 0:
            zback_ref[0] = row
            return_all(0)
            got_ref[0, 0] = row[0]
        elif i in Z_FIRST:
            back_ref[i] = row
            back_copy(i).start()
        else:
            back_ref[i] = row
            return_all(i)
            zback_ref[i, 0] = row[0]

    def take(i, first):
        if i in Z_FIRST or not i:
            all_returns(i).wait_recv()
        else:
            back_copy(i).wait_recv()
        half = width // 2
        term = dot(
            hot_ref[:, i * half : (i + 1) * half], got_ref[i].reshape(half, 2 * HD)
        )
        if first:
            found_ref[...] = term
        else:
            found_ref[...] += term

    def mark(i):
        for b in range(i * width // 2, (i + 1) * width // 2, 128):
            hot_ref[:, b : b + 128] = one_hot(target_ref[...] == iota((ROWS, 128), 1) + b)

    mark(0)
    for i in RELAY:
        if i in Z_FIRST:
            back_copy(i).wait_recv()
            return_all(i)
            got_ref[i, 0] = zback_ref[i, 0]
        else:
            all_returns(i).wait_recv()
            back_copy(i).start()
        mark(i)
    for n, i in enumerate(TAKE):
        take(i, n == 0)

    def g_copy(n):
        cut = pl.ds(n * PIECE, PIECE)
        return remote(
            wide_ref.at[0, :, cut], wide_ref.at[1, :, cut], psend_sem.at[1 + n],
            precv_sem.at[1 + n], other,
        )

    for h in range(0, H, 2):
        pieces = []
        for e in range(2):
            cut = slice((h + e) * TOK, (h + e + 1) * TOK)
            upper = (jnp.broadcast_to(rank[:, cut], (TOK, TOK)).T[:, :HD] & (BOUND // 2)) > 0
            piece = found_ref[cut, :]
            pieces.append(jnp.where(upper, piece[:, HD:], piece[:, :HD]))
        wide_ref[0, :, h * HD : (h + 2) * HD] = jnp.concatenate(pieces, axis=1).astype(BF16)
        if (h + 2) * HD % PIECE == 0:
            g_copy(h * HD // PIECE).start()

    def first_line(i):
        return remote(
            fline_ref.at[lax.rem(z + i, DEPTH)], flined_ref.at[i - 1], fzsend_sem.at[i - 1],
            fzrecv_sem.at[i - 1], on_line(i),
        )

    def first_plane(m):
        return remote(
            fplane_ref.at[lax.rem(yx + m, PLANE)], fplaned_ref.at[m - 1], fysend_sem.at[m - 1],
            fyrecv_sem.at[m - 1], in_plane(m),
        )

    def plane_copy(i):
        return remote(
            part_ref.at[lax.rem(yx + i, PLANE)], plane_ref.at[i - 1], ysend_sem.at[i - 1],
            yrecv_sem.at[i - 1], in_plane(i),
        )

    def line_copy(i):
        return remote(
            line_ref.at[lax.rem(z + i, DEPTH)], lined_ref.at[i - 1], zsend_sem.at[i - 1],
            zrecv_sem.at[i - 1], on_line(i),
        )

    def summed(n, order):
        g_copy(n).wait()
        columns = wide_ref[:, :, n * PIECE : (n + 1) * PIECE].reshape(2 * TOK, PIECE)
        return dot(xall_ref[order], columns).astype(BF16)

    fline_ref[...] = summed(0, 1).reshape(DEPTH, 4 * PLANE, PIECE)
    for i in range(1, DEPTH):
        first_line(i).start()
    for n in range(1, 1024 // PIECE):
        part_ref[:, :, (n - 1) * PIECE : n * PIECE] = summed(n, 0).reshape(PLANE, 32, PIECE)
    for i in range(1, PLANE):
        plane_copy(i).start()
    total = fline_ref[z].astype(F32)
    for i in range(1, DEPTH):
        first_line(i).wait_recv()
        total = total + flined_ref[i - 1].astype(F32)
    for m in range(PLANE):
        rows = total[4 * m : 4 * m + 4, :]
        fplane_ref[m] = jnp.concatenate([rows[:, : PIECE // 2], rows[:, PIECE // 2 :]], axis=0)
    for m in range(1, PLANE):
        first_plane(m).start()
    half = (1024 - PIECE) // 2
    total = part_ref[yx].astype(F32)
    for i in range(1, PLANE):
        plane_copy(i).wait_recv()
        total = total + plane_ref[i - 1].astype(F32)
    for i in range(DEPTH):
        rows = total[4 * i : 4 * i + 4, :]
        line_ref[i] = jnp.concatenate([rows[:, :half], rows[:, half:]], axis=0)
    for i in range(1, DEPTH):
        line_copy(i).start()
    result = fplane_ref[yx]
    for m in range(1, PLANE):
        first_plane(m).wait_recv()
        result = result + fplaned_ref[m - 1]
    out_ref[:, :PIECE] = jnp.concatenate([result[:4], result[4:]], axis=1)
    result = line_ref[z]
    for i in range(1, DEPTH):
        line_copy(i).wait_recv()
        result = result + lined_ref[i - 1]
    out_ref[:, PIECE:] = jnp.concatenate([result[:4], result[4:]], axis=1)

    for i in range(1, DEPTH):
        for kind in range(3):
            z_copy(i, kind).wait_send()
        back_copy(i).wait_send()
        line_copy(i).wait_send()
        first_line(i).wait_send()
    for i in range(DEPTH):
        all_rows(i).wait_send()
        key_copy(i).wait_send()
        all_returns(i).wait_send()
    for m in range(1, PLANE):
        label_copy(m).wait_send()
        plane_copy(m).wait_send()
        first_plane(m).wait_send()


def whole(cluster_of, slot_of, queries, out_grad, key_value, tokens_in):
    width = PLANE * BOUND
    dma = pltpu.SemaphoreType.DMA
    return pl.pallas_call(
        whole_kernel,
        out_shape=jax.ShapeDtypeStruct((4, 1024), F32),
        in_specs=[pl.BlockSpec(memory_space=pl.ANY)] * 6,
        out_specs=VMEM,
        scratch_shapes=[
            pltpu.VMEM((H, TOK), jnp.int32),
            pltpu.VMEM((H, TOK), jnp.int32),
            pltpu.VMEM((TOK, H * HD), BF16),
            pltpu.VMEM((TOK, H * HD), BF16),
            pltpu.VMEM((TOK, 2 * HD), BF16),
            pltpu.VMEM((TOK, 1024), BF16),
            pltpu.VMEM((ROWS, 2 * HD), BF16),
            pltpu.VMEM((DEPTH, width, 2 * HD), BF16),
            pltpu.VMEM((DEPTH, width, 2 * HD), BF16),
            pltpu.VMEM((DEPTH, TOK, 2 * HD), BF16),
            pltpu.VMEM((DEPTH, 4, 128), jnp.int32),
            pltpu.VMEM((DEPTH, 4, 128), jnp.int32),
            pltpu.VMEM((4, DEPTH, 128), jnp.int32),
            pltpu.VMEM((PLANE, DEPTH, 128), jnp.int32),
            pltpu.VMEM((DEPTH, PLANE, BOUND, 4 * HD), BF16),
            pltpu.VMEM((DEPTH, PLANE, BOUND, 4 * HD), BF16),
            pltpu.VMEM((CL_DEV, HALF, 4 * HD), F32),
            pltpu.VMEM((CL_DEV, HALF, 2 * HD), BF16),
            pltpu.VMEM((CL_DEV, HALF, 2 * HD), BF16),
            pltpu.VMEM((CL_DEV, 4, 128), F32),
            pltpu.VMEM((CL_DEV, HALF, 2 * HD), BF16),
            pltpu.VMEM((CL_DEV, 4, 128), F32),
            pltpu.VMEM((2 * HALF, 4 * HD), BF16),
            pltpu.VMEM((DEPTH, PLANE, BOUND // 2, 2 * HD), BF16),
            pltpu.VMEM((DEPTH, PLANE, BOUND // 2, 2 * HD), BF16),
            pltpu.VMEM((DEPTH, PLANE, BOUND // 2, 2 * HD), BF16),
            pltpu.VMEM((ROWS, GROUPS * BOUND // 2), BF16),
            pltpu.VMEM((ROWS, 128), jnp.int32),
            pltpu.VMEM((ROWS, 2 * HD), F32),
            pltpu.VMEM((2, 512, TOK), BF16),
            pltpu.VMEM((512, TOK), BF16),
            pltpu.VMEM((2, 512, 2 * TOK), BF16),
            pltpu.VMEM((2, TOK, 1024), BF16),
            pltpu.VMEM((DEPTH, 4 * PLANE, PIECE), BF16),
            pltpu.VMEM((DEPTH - 1, 4 * PLANE, PIECE), BF16),
            pltpu.VMEM((PLANE, 8, PIECE // 2), F32),
            pltpu.VMEM((PLANE - 1, 8, PIECE // 2), F32),
            pltpu.VMEM((PLANE, 32, 1024 - PIECE), BF16),
            pltpu.VMEM((PLANE - 1, 32, 1024 - PIECE), BF16),
            pltpu.VMEM((DEPTH, 8, (1024 - PIECE) // 2), F32),
            pltpu.VMEM((DEPTH - 1, 8, (1024 - PIECE) // 2), F32),
            dma((DEPTH, 3)),
            dma((DEPTH, 3)),
            dma((PLANE,)),
            dma((PLANE,)),
            dma((DEPTH,)),
            dma((DEPTH,)),
            dma((CL_DEV + 1,)),
            dma((CL_DEV + 1,)),
            dma((DEPTH,)),
            dma((DEPTH,)),
            dma((DEPTH,)),
            dma((DEPTH,)),
            dma((1 + 1024 // PIECE,)),
            dma((1 + 1024 // PIECE,)),
            dma((PLANE - 1,)),
            dma((PLANE - 1,)),
            dma((DEPTH - 1,)),
            dma((DEPTH - 1,)),
            dma((PLANE - 1,)),
            dma((PLANE - 1,)),
            dma((DEPTH - 1,)),
            dma((DEPTH - 1,)),
            dma((6,)),
        ],
        compiler_params=params(0),
    )(cluster_of, slot_of, queries, out_grad, key_value, tokens_in)


def on_device(tokens_in, queries, key_value, out_grad, cluster_of, slot_of):
    return whole(cluster_of.T, slot_of.T, queries, out_grad, key_value, tokens_in)


def solution(mesh):
    spec = P(("seq", "pair"), None)
    return jax.shard_map(
        on_device, mesh=mesh, in_specs=(spec,) * 6, out_specs=spec, check_vma=False
    )
```

```python
import jax
import jax.numpy as jnp
from jax import lax
from jax.experimental import pallas as pl
from jax.experimental.pallas import tpu as pltpu
from jax.sharding import PartitionSpec as P

H = 16
HD = 64
HALF = 512
CL_DEV = 8
TOK = 128
ROWS = TOK * H
SLOTS = CL_DEV * HALF
GROUPS = 128
BOUND = 32
PLANE = 16
DEPTH = 8
ORDER = [0, 1, 7, 2, 6, 3, 5, 4]
LAG = 2
EARLY = 3
JOINT = 4
PIECE = 256
Z_FIRST = (4, 2, 6)
RETURN = [4, 3, 2, 5, 6, 1, 7, 0]
RELAY = [3, 2, 5, 6, 1, 4, 7]
TAKE = [0, 2, 6, 4, 3, 5, 1, 7]
MESH = pl.DeviceIdType.MESH
F32 = jnp.float32
BF16 = jnp.bfloat16
VMEM = pl.BlockSpec(memory_space=pltpu.VMEM)


def params(collective=None):
    if collective is None:
        return pltpu.CompilerParams(vmem_limit_bytes=56 * 2**20)
    return pltpu.CompilerParams(
        vmem_limit_bytes=56 * 2**20, collective_id=collective, has_side_effects=True
    )


def iota(shape, dim):
    return lax.broadcasted_iota(jnp.int32, shape, dim)


def one_hot(mask):
    return jnp.where(mask, 1.0, 0.0).astype(BF16)


def dot(a, b):
    return jnp.dot(a, b, preferred_element_type=F32)


def dot_t(a, b):
    return lax.dot_general(a, b, (((1,), (1,)), ((), ())), preferred_element_type=F32)


def t_dot(a, b):
    return lax.dot_general(a, b, (((0,), (0,)), ((), ())), preferred_element_type=F32)


def whole_kernel(
    cluster_in, slot_in, q_in, g_in, kv_in, x_in, out_ref,
    cluster_ref, slot_ref, q_ref, g_ref, kvin_ref, x_ref, flat_ref, zsend_ref, zgot_ref, zkv_ref, zlab_ref, zlabgot_ref, group_ref, plab_ref,
    fwd_ref, rows_ref, total_ref, qg_ref, kv_ref, live_ref, kv2_ref, live2_ref, grads_ref,
    back_ref, zback_ref, got_ref, hot_ref, target_ref, found_ref, xt_ref, xo_ref, xall_ref, wide_ref,
    fline_ref, flined_ref, fplane_ref, fplaned_ref, part_ref, plane_ref, line_ref, lined_ref,
    fsend_sem, frecv_sem, lsend_sem, lrecv_sem, wsend_sem, wrecv_sem, ksend_sem, krecv_sem,
    bsend_sem, brecv_sem, rsend_sem, rrecv_sem, psend_sem, precv_sem, ysend_sem, yrecv_sem,
    zsend_sem, zrecv_sem, fysend_sem, fyrecv_sem, fzsend_sem, fzrecv_sem, in_sem,
):
    seq, pair = lax.axis_index("seq"), lax.axis_index("pair")
    other = (seq, 1 - pair)
    yx, z = seq // DEPTH, lax.rem(seq, DEPTH)
    width = PLANE * BOUND
    rest = pl.ds(1, PLANE - 1)

    def on_line(i):
        return (yx * DEPTH + lax.rem(z + i, DEPTH), pair)

    def in_plane(m):
        return (lax.rem(yx + m, PLANE) * DEPTH + z, pair)

    def remote(source, target, send_sem, recv_sem, to):
        return pltpu.make_async_remote_copy(
            src_ref=source, dst_ref=target, send_sem=send_sem, recv_sem=recv_sem,
            device_id=to, device_id_type=MESH,
        )

    barrier = pltpu.get_barrier_semaphore()
    for i in range(1, DEPTH):
        pl.semaphore_signal(barrier, inc=1, device_id=on_line(i), device_id_type=MESH)
    for m in range(1, PLANE):
        pl.semaphore_signal(barrier, inc=1, device_id=in_plane(m), device_id_type=MESH)
    pl.semaphore_signal(barrier, inc=1, device_id=other, device_id_type=MESH)

    loads = [
        pltpu.make_async_copy(source, target, in_sem.at[n])
        for n, (source, target) in enumerate(
            (
                (cluster_in, cluster_ref), (slot_in, slot_ref), (q_in, q_ref), (g_in, g_ref),
                (kv_in, kvin_ref), (x_in, x_ref),
            )
        )
    ]
    for load in loads:
        load.start()
    for load in loads[:2]:
        load.wait()

    def in_lanes(ref):
        return jnp.concatenate([ref[h : h + 1, :] for h in range(H)], axis=1)

    cluster = in_lanes(cluster_ref)
    slot = in_lanes(slot_ref)
    owner = lax.shift_right_logical(cluster, 3)
    local = (cluster & (CL_DEV - 1)) * HALF + (slot & (HALF - 1))
    before = one_hot(iota((TOK, TOK), 0) < iota((TOK, TOK), 1))
    base = jnp.zeros((GROUPS, 1), F32)
    ranks = []
    for h in range(H):
        mine = owner[:, h * TOK : (h + 1) * TOK]
        pick = jnp.where(iota((GROUPS, TOK), 0) == mine, 1.0, 0.0)
        count = dot(pick.astype(BF16), before) + base
        ranks.append(jnp.sum(pick * count, axis=0, keepdims=True))
        base = base + jnp.sum(pick, axis=1, keepdims=True)
    rank = jnp.concatenate(ranks, axis=1).astype(jnp.int32)
    place = (owner & (DEPTH - 1)) * width + lax.shift_right_logical(owner, 3) * BOUND + rank
    in_row = jnp.where(iota((32, ROWS), 0) == lax.shift_right_logical(place, 7), 1.0, 0.0)
    in_lane = one_hot(iota((128, ROWS), 0) == (place & 127))
    token = iota((1, ROWS), 1) & (TOK - 1)
    parts = [lax.shift_right_logical(local, 6), local & 63, token]
    stacked = [(in_row * part.astype(F32)).astype(BF16) for part in parts] + [in_row.astype(BF16)]
    found = dot_t(jnp.concatenate(stacked, axis=0), in_lane)
    label = jnp.where(
        found[96:128] > 0.5, (found[0:32] * 64.0 + found[32:64]) * 128.0 + found[64:96], -1.0
    ).astype(jnp.int32)
    for i in range(DEPTH):
        zlab_ref[i] = label[4 * i : 4 * i + 4, :]
    for load in loads[2:]:
        load.wait()
    for h in range(H):
        cut = slice(h * HD, (h + 1) * HD)
        flat_ref[h * TOK : (h + 1) * TOK, :] = jnp.concatenate([q_ref[:, cut], g_ref[:, cut]], axis=1)
    def pack(i):
        to = lax.rem(z + i, DEPTH)
        hot = one_hot(iota((width, ROWS), 0) == place - to * width)
        zsend_ref[i] = dot(hot, flat_ref[...]).astype(BF16)

    for i in ORDER[1:EARLY]:
        pack(i)

    def z_copy(i, kind):
        to = lax.rem(z + i, DEPTH)
        source, target = (
            (zlab_ref.at[to], zlabgot_ref.at[i]),
            (kvin_ref, zkv_ref.at[i]),
            (zsend_ref.at[i], zgot_ref.at[i]),
        )[kind]
        return remote(source, target, fsend_sem.at[i, kind], frecv_sem.at[i, kind], on_line(i))

    pl.semaphore_wait(barrier, DEPTH - 1 + PLANE - 1 + 1)
    for i in ORDER[1:]:
        z_copy(i, 0).start()
    for n, i in enumerate(ORDER[1:], 1):
        if n >= EARLY:
            pack(i)
        z_copy(i, 1).start()
        z_copy(i, 2).start()
    pack(0)

    def row_copy(i, m):
        to = lax.rem(yx + m, PLANE)
        return remote(
            fwd_ref.at[i, to], rows_ref.at[i, m], wsend_sem.at[i], wrecv_sem.at[i], in_plane(m)
        )

    def all_rows(i):
        return remote(
            fwd_ref.at[i, rest], rows_ref.at[i, rest], wsend_sem.at[i], wrecv_sem.at[i], other
        )

    def pass_on(i):
        if i:
            z_copy(i, 1).wait_recv()
            z_copy(i, 2).wait_recv()
        labels = jnp.concatenate([zlabgot_ref[i, g : g + 1, :] for g in range(4)], axis=1)
        hot = one_hot(iota((TOK, width), 0) == (labels & (TOK - 1)))
        pairs = t_dot(hot, zkv_ref[i] if i else kvin_ref[...]).astype(BF16)
        rows = zgot_ref[i] if i else zsend_ref[0]
        fwd_ref[i] = jnp.concatenate([rows, pairs], axis=1).reshape(PLANE, BOUND, 4 * HD)

        def send(m, carry):
            row_copy(i, m).start()
            return carry

        lax.fori_loop(1, PLANE, send, 0)
        rows_ref[i, 0] = fwd_ref[i, yx]

    zlabgot_ref[0] = zlab_ref[z]
    pass_on(0)

    for i in ORDER[1:]:
        z_copy(i, 0).wait_recv()
    for i in range(DEPTH):
        for g in range(4):
            group_ref[g, i : i + 1, :] = zlabgot_ref[i, g : g + 1, :]

    def label_copy(m):
        to = lax.rem(yx + m, PLANE)
        return remote(
            group_ref.at[to // 4], plab_ref.at[m], lsend_sem.at[m], lrecv_sem.at[m], in_plane(m)
        )

    for m in range(1, PLANE):
        label_copy(m).start()
    plab_ref[0] = group_ref[yx // 4]

    pass_on(ORDER[1])
    for m in range(1, PLANE):
        label_copy(m).wait_recv()
    quarter = lax.rem(yx, 4)
    lanes = []
    live = jnp.zeros((SLOTS // 128, 128), F32)
    for i in range(DEPTH):
        given = plab_ref[:, i, :]
        mine = given[:, 3 * BOUND :]
        for g in range(3):
            mine = jnp.where(quarter == g, given[:, g * BOUND : (g + 1) * BOUND], mine)
        lane = jnp.concatenate([mine[m : m + 1, :] for m in range(PLANE)], axis=1)
        lane = lax.shift_right_arithmetic(lane, 7)
        lanes.append(lane)
        live = live + dot_t(
            one_hot(iota((SLOTS // 128, width), 0) == lax.shift_right_arithmetic(lane, 7)),
            one_hot(iota((128, width), 0) == (lane & 127)),
        )
    for c in range(CL_DEV):
        live_ref[c] = live[4 * c : 4 * c + 4, :]
    live_copy = remote(
        live_ref, live2_ref, ksend_sem.at[CL_DEV], krecv_sem.at[CL_DEV], other
    )
    live_copy.start()

    def key_copy(c):
        return remote(kv_ref.at[c], kv2_ref.at[c], ksend_sem.at[c], krecv_sem.at[c], other)

    def arrange(i, first, last):
        all_rows(i).wait_recv()
        lane = lanes[i]
        for b in range(CL_DEV):
            hot = one_hot(iota((HALF, width), 0) == lane - b * HALF)
            term = dot(hot, rows_ref[i].reshape(width, 4 * HD))
            if first:
                total_ref[b] = term
            elif not last:
                total_ref[b] += term
            else:
                done = (total_ref[b] + term).astype(BF16)
                qg_ref[b] = done[:, : 2 * HD]
                kv_ref[b] = done[:, 2 * HD :]
                key_copy(b).start()

    x_copy = remote(xt_ref.at[1 - pair], xo_ref, psend_sem.at[0], precv_sem.at[0], other)

    def turn_x():
        position = iota((512, 1024), 0)
        for p in range(2):
            column = lax.shift_right_logical(position, 2) * 8 + 4 * p + (position & 3)
            xt_ref[p] = dot_t(one_hot(iota((512, 1024), 1) == column), x_ref[...]).astype(BF16)
        x_copy.start()

    def join_x():
        x_copy.wait()
        both = jnp.concatenate([xt_ref[pair], xo_ref[...]], axis=1)
        xall_ref[0] = both
        position = iota((512, 512), 0)
        row = (lax.shift_right_logical(position, 2) & (PLANE - 1)) * 32
        row = row + lax.shift_right_logical(position, 6) * 4 + (position & 3)
        xall_ref[1] = dot(one_hot(iota((512, 512), 1) == row), both).astype(BF16)

    def find_targets():
        for h in range(H):
            cut = slice(h * TOK, (h + 1) * TOK)
            to = owner[:, cut]
            line = (to + (DEPTH - z)) & (DEPTH - 1)
            plane = (lax.shift_right_logical(to, 3) + (PLANE - yx)) & (PLANE - 1)
            target = line * (width // 2) + plane * (BOUND // 2) + (rank[:, cut] & (BOUND // 2 - 1))
            target = jnp.broadcast_to(target, (TOK, TOK)).T
            target_ref[cut, :] = target

    for n in range(2, DEPTH + LAG):
        if n < DEPTH:
            pass_on(ORDER[n])
        if n >= LAG:
            arrange(ORDER[n - LAG], n == LAG, n == DEPTH + LAG - 1)
        if n == 3:
            turn_x()
        if n == 4:
            find_targets()
        if n == 5:
            join_x()

    live_copy.wait()
    for c in range(CL_DEV):
        if c % JOINT == 0:
            for e in range(c, c + JOINT):
                key_copy(e).wait_recv()
        queries = qg_ref[c, :, :HD] * BF16(HD**-0.5)
        grads = qg_ref[c, :, HD:]
        keys = jnp.concatenate([kv_ref[c, :, :HD], kv2_ref[c, :, :HD]], axis=0)
        values = jnp.concatenate([kv_ref[c, :, HD:], kv2_ref[c, :, HD:]], axis=0)
        alive = jnp.concatenate(
            [ref[c, r : r + 1, :] for ref in (live_ref, live2_ref) for r in range(4)], axis=1
        )
        scores = dot_t(queries, keys) + jnp.where(alive > 0.5, 0.0, -1e30)
        prob_grad = dot_t(grads, values)
        weights = jnp.exp(scores - jnp.max(scores, axis=1, keepdims=True))
        inverse = 1.0 / jnp.sum(weights, axis=1, keepdims=True)
        row_dot = jnp.sum(weights * prob_grad, axis=1, keepdims=True) * inverse
        score_grad = (weights * (prob_grad - row_dot)).astype(BF16)
        grads_ref[
            (c % 2) * HALF : (c % 2 + 1) * HALF, (c // 2) * HD : (c // 2 + 1) * HD
        ] = (dot(score_grad, keys) * (inverse * (HD**-0.5))).astype(BF16)

    def back_copy(i):
        source, target = (back_ref, zback_ref) if i in Z_FIRST else (zback_ref, got_ref)
        return remote(
            source.at[i], target.at[i], bsend_sem.at[i], brecv_sem.at[i], on_line(DEPTH - i)
        )

    def return_copy(i, m):
        source, target = (zback_ref, got_ref) if i in Z_FIRST or not i else (back_ref, zback_ref)
        return remote(
            source.at[i, m], target.at[i, m], rsend_sem.at[i], rrecv_sem.at[i], in_plane(PLANE - m)
        )

    def all_returns(i):
        source, target = (zback_ref, got_ref) if i in Z_FIRST or not i else (back_ref, zback_ref)
        return remote(
            source.at[i, rest], target.at[i, rest], rsend_sem.at[i], rrecv_sem.at[i], other
        )

    def return_all(i):
        def send(m, carry):
            return_copy(i, m).start()
            return carry

        lax.fori_loop(1, PLANE, send, 0)

    for i in RETURN:
        labels = jnp.broadcast_to(lanes[i], (128, width)).T
        low = labels & 1023
        hot = jnp.concatenate(
            [one_hot(low == iota((width, 128), 1) + 128 * b) for b in range(8)], axis=1
        )
        found = dot(hot, grads_ref[...])
        high = lax.shift_right_arithmetic(labels[:, :HD], 10)
        row = jnp.zeros((width, HD), F32)
        for a in range(4):
            row = row + jnp.where(high == a, found[:, a * HD : (a + 1) * HD], 0.0)
        row = row.reshape(PLANE, BOUND, HD)
        row = jnp.concatenate([row[:, : BOUND // 2], row[:, BOUND // 2 :]], axis=2).astype(BF16)
        if i == 0:
            zback_ref[0] = row
            return_all(0)
            got_ref[0, 0] = row[0]
        elif i in Z_FIRST:
            back_ref[i] = row
            back_copy(i).start()
        else:
            back_ref[i] = row
            return_all(i)
            zback_ref[i, 0] = row[0]

    def take(i, first):
        if i in Z_FIRST or not i:
            all_returns(i).wait_recv()
        else:
            back_copy(i).wait_recv()
        half = width // 2
        term = dot(
            hot_ref[:, i * half : (i + 1) * half], got_ref[i].reshape(half, 2 * HD)
        )
        if first:
            found_ref[...] = term
        else:
            found_ref[...] += term

    def mark(i):
        for b in range(i * width // 2, (i + 1) * width // 2, 128):
            hot_ref[:, b : b + 128] = one_hot(target_ref[...] == iota((ROWS, 128), 1) + b)

    mark(0)
    for i in RELAY:
        if i in Z_FIRST:
            back_copy(i).wait_recv()
            return_all(i)
            got_ref[i, 0] = zback_ref[i, 0]
        else:
            all_returns(i).wait_recv()
            back_copy(i).start()
        mark(i)
    for n, i in enumerate(TAKE):
        take(i, n == 0)

    def g_copy(n):
        cut = pl.ds(n * PIECE, PIECE)
        return remote(
            wide_ref.at[0, :, cut], wide_ref.at[1, :, cut], psend_sem.at[1 + n],
            precv_sem.at[1 + n], other,
        )

    for h in range(0, H, 2):
        pieces = []
        for e in range(2):
            cut = slice((h + e) * TOK, (h + e + 1) * TOK)
            upper = (jnp.broadcast_to(rank[:, cut], (TOK, TOK)).T[:, :HD] & (BOUND // 2)) > 0
            piece = found_ref[cut, :]
            pieces.append(jnp.where(upper, piece[:, HD:], piece[:, :HD]))
        wide_ref[0, :, h * HD : (h + 2) * HD] = jnp.concatenate(pieces, axis=1).astype(BF16)
        if (h + 2) * HD % PIECE == 0:
            g_copy(h * HD // PIECE).start()

    def first_line(i):
        return remote(
            fline_ref.at[lax.rem(z + i, DEPTH)], flined_ref.at[i - 1], fzsend_sem.at[i - 1],
            fzrecv_sem.at[i - 1], on_line(i),
        )

    def first_plane(m):
        return remote(
            fplane_ref.at[lax.rem(yx + m, PLANE)], fplaned_ref.at[m - 1], fysend_sem.at[m - 1],
            fyrecv_sem.at[m - 1], in_plane(m),
        )

    def plane_copy(i):
        return remote(
            part_ref.at[lax.rem(yx + i, PLANE)], plane_ref.at[i - 1], ysend_sem.at[i - 1],
            yrecv_sem.at[i - 1], in_plane(i),
        )

    def line_copy(i):
        return remote(
            line_ref.at[lax.rem(z + i, DEPTH)], lined_ref.at[i - 1], zsend_sem.at[i - 1],
            zrecv_sem.at[i - 1], on_line(i),
        )

    def summed(n, order):
        g_copy(n).wait()
        columns = wide_ref[:, :, n * PIECE : (n + 1) * PIECE].reshape(2 * TOK, PIECE)
        return dot(xall_ref[order], columns).astype(BF16)

    fline_ref[...] = summed(0, 1).reshape(DEPTH, 4 * PLANE, PIECE)
    for i in range(1, DEPTH):
        first_line(i).start()
    for n in range(1, 1024 // PIECE):
        part_ref[:, :, (n - 1) * PIECE : n * PIECE] = summed(n, 0).reshape(PLANE, 32, PIECE)
    for i in range(1, PLANE):
        plane_copy(i).start()
    total = fline_ref[z].astype(F32)
    for i in range(1, DEPTH):
        first_line(i).wait_recv()
        total = total + flined_ref[i - 1].astype(F32)
    for m in range(PLANE):
        rows = total[4 * m : 4 * m + 4, :]
        fplane_ref[m] = jnp.concatenate([rows[:, : PIECE // 2], rows[:, PIECE // 2 :]], axis=0)
    for m in range(1, PLANE):
        first_plane(m).start()
    half = (1024 - PIECE) // 2
    total = part_ref[yx].astype(F32)
    for i in range(1, PLANE):
        plane_copy(i).wait_recv()
        total = total + plane_ref[i - 1].astype(F32)
    for i in range(DEPTH):
        rows = total[4 * i : 4 * i + 4, :]
        line_ref[i] = jnp.concatenate([rows[:, :half], rows[:, half:]], axis=0)
    for i in range(1, DEPTH):
        line_copy(i).start()
    result = fplane_ref[yx]
    for m in range(1, PLANE):
        first_plane(m).wait_recv()
        result = result + fplaned_ref[m - 1]
    out_ref[:, :PIECE] = jnp.concatenate([result[:4], result[4:]], axis=1)
    result = line_ref[z]
    for i in range(1, DEPTH):
        line_copy(i).wait_recv()
        result = result + lined_ref[i - 1]
    out_ref[:, PIECE:] = jnp.concatenate([result[:4], result[4:]], axis=1)

    for i in range(1, DEPTH):
        for kind in range(3):
            z_copy(i, kind).wait_send()
        back_copy(i).wait_send()
        line_copy(i).wait_send()
        first_line(i).wait_send()
    for i in range(DEPTH):
        all_rows(i).wait_send()
        key_copy(i).wait_send()
        all_returns(i).wait_send()
    for m in range(1, PLANE):
        label_copy(m).wait_send()
        plane_copy(m).wait_send()
        first_plane(m).wait_send()


def whole(cluster_of, slot_of, queries, out_grad, key_value, tokens_in):
    width = PLANE * BOUND
    dma = pltpu.SemaphoreType.DMA
    return pl.pallas_call(
        whole_kernel,
        out_shape=jax.ShapeDtypeStruct((4, 1024), F32),
        in_specs=[pl.BlockSpec(memory_space=pl.ANY)] * 6,
        out_specs=VMEM,
        scratch_shapes=[
            pltpu.VMEM((H, TOK), jnp.int32),
            pltpu.VMEM((H, TOK), jnp.int32),
            pltpu.VMEM((TOK, H * HD), BF16),
            pltpu.VMEM((TOK, H * HD), BF16),
            pltpu.VMEM((TOK, 2 * HD), BF16),
            pltpu.VMEM((TOK, 1024), BF16),
            pltpu.VMEM((ROWS, 2 * HD), BF16),
            pltpu.VMEM((DEPTH, width, 2 * HD), BF16),
            pltpu.VMEM((DEPTH, width, 2 * HD), BF16),
            pltpu.VMEM((DEPTH, TOK, 2 * HD), BF16),
            pltpu.VMEM((DEPTH, 4, 128), jnp.int32),
            pltpu.VMEM((DEPTH, 4, 128), jnp.int32),
            pltpu.VMEM((4, DEPTH, 128), jnp.int32),
            pltpu.VMEM((PLANE, DEPTH, 128), jnp.int32),
            pltpu.VMEM((DEPTH, PLANE, BOUND, 4 * HD), BF16),
            pltpu.VMEM((DEPTH, PLANE, BOUND, 4 * HD), BF16),
            pltpu.VMEM((CL_DEV, HALF, 4 * HD), F32),
            pltpu.VMEM((CL_DEV, HALF, 2 * HD), BF16),
            pltpu.VMEM((CL_DEV, HALF, 2 * HD), BF16),
            pltpu.VMEM((CL_DEV, 4, 128), F32),
            pltpu.VMEM((CL_DEV, HALF, 2 * HD), BF16),
            pltpu.VMEM((CL_DEV, 4, 128), F32),
            pltpu.VMEM((2 * HALF, 4 * HD), BF16),
            pltpu.VMEM((DEPTH, PLANE, BOUND // 2, 2 * HD), BF16),
            pltpu.VMEM((DEPTH, PLANE, BOUND // 2, 2 * HD), BF16),
            pltpu.VMEM((DEPTH, PLANE, BOUND // 2, 2 * HD), BF16),
            pltpu.VMEM((ROWS, GROUPS * BOUND // 2), BF16),
            pltpu.VMEM((ROWS, 128), jnp.int32),
            pltpu.VMEM((ROWS, 2 * HD), F32),
            pltpu.VMEM((2, 512, TOK), BF16),
            pltpu.VMEM((512, TOK), BF16),
            pltpu.VMEM((2, 512, 2 * TOK), BF16),
            pltpu.VMEM((2, TOK, 1024), BF16),
            pltpu.VMEM((DEPTH, 4 * PLANE, PIECE), BF16),
            pltpu.VMEM((DEPTH - 1, 4 * PLANE, PIECE), BF16),
            pltpu.VMEM((PLANE, 8, PIECE // 2), F32),
            pltpu.VMEM((PLANE - 1, 8, PIECE // 2), F32),
            pltpu.VMEM((PLANE, 32, 1024 - PIECE), BF16),
            pltpu.VMEM((PLANE - 1, 32, 1024 - PIECE), BF16),
            pltpu.VMEM((DEPTH, 8, (1024 - PIECE) // 2), F32),
            pltpu.VMEM((DEPTH - 1, 8, (1024 - PIECE) // 2), F32),
            dma((DEPTH, 3)),
            dma((DEPTH, 3)),
            dma((PLANE,)),
            dma((PLANE,)),
            dma((DEPTH,)),
            dma((DEPTH,)),
            dma((CL_DEV + 1,)),
            dma((CL_DEV + 1,)),
            dma((DEPTH,)),
            dma((DEPTH,)),
            dma((DEPTH,)),
            dma((DEPTH,)),
            dma((1 + 1024 // PIECE,)),
            dma((1 + 1024 // PIECE,)),
            dma((PLANE - 1,)),
            dma((PLANE - 1,)),
            dma((DEPTH - 1,)),
            dma((DEPTH - 1,)),
            dma((PLANE - 1,)),
            dma((PLANE - 1,)),
            dma((DEPTH - 1,)),
            dma((DEPTH - 1,)),
            dma((6,)),
        ],
        compiler_params=params(0),
    )(cluster_of, slot_of, queries, out_grad, key_value, tokens_in)


def on_device(tokens_in, queries, key_value, out_grad, cluster_of, slot_of):
    return whole(cluster_of.T, slot_of.T, queries, out_grad, key_value, tokens_in)


def solution(mesh):
    spec = P(("seq", "pair"), None)
    return jax.shard_map(
        on_device, mesh=mesh, in_specs=(spec,) * 6, out_specs=spec, check_vma=False
    )
```

```python
import jax
import jax.numpy as jnp
from jax import lax
from jax.experimental import pallas as pl
from jax.experimental.pallas import tpu as pltpu
from jax.sharding import PartitionSpec as P

H = 16
HD = 64
HALF = 512
CL_DEV = 8
TOK = 128
ROWS = TOK * H
SLOTS = CL_DEV * HALF
GROUPS = 128
BOUND = 32
PLANE = 16
DEPTH = 8
ORDER = [0, 1, 7, 2, 6, 3, 5, 4]
LAG = 2
EARLY = 3
JOINT = 4
PIECE = 256
Z_FIRST = (4, 2, 6)
RETURN = [4, 3, 2, 5, 6, 1, 7, 0]
RELAY = [3, 2, 5, 6, 1, 4, 7]
TAKE = [0, 2, 6, 4, 3, 5, 1, 7]
MESH = pl.DeviceIdType.MESH
F32 = jnp.float32
BF16 = jnp.bfloat16
VMEM = pl.BlockSpec(memory_space=pltpu.VMEM)


def params(collective=None):
    if collective is None:
        return pltpu.CompilerParams(vmem_limit_bytes=56 * 2**20)
    return pltpu.CompilerParams(
        vmem_limit_bytes=56 * 2**20, collective_id=collective, has_side_effects=True
    )


def iota(shape, dim):
    return lax.broadcasted_iota(jnp.int32, shape, dim)


def one_hot(mask):
    return jnp.where(mask, 1.0, 0.0).astype(BF16)


def dot(a, b):
    return jnp.dot(a, b, preferred_element_type=F32)


def dot_t(a, b):
    return lax.dot_general(a, b, (((1,), (1,)), ((), ())), preferred_element_type=F32)


def t_dot(a, b):
    return lax.dot_general(a, b, (((0,), (0,)), ((), ())), preferred_element_type=F32)


def whole_kernel(
    cluster_in, slot_in, q_in, g_in, kv_in, x_in, out_ref,
    cluster_ref, slot_ref, q_ref, g_ref, kvin_ref, x_ref, flat_ref, zsend_ref, zgot_ref, zkv_ref, zlab_ref, zlabgot_ref, group_ref, plab_ref,
    fwd_ref, rows_ref, total_ref, qg_ref, kv_ref, live_ref, kv2_ref, live2_ref, grads_ref,
    back_ref, zback_ref, got_ref, hot_ref, target_ref, found_ref, xt_ref, xo_ref, xall_ref, wide_ref,
    fline_ref, flined_ref, fplane_ref, fplaned_ref, part_ref, plane_ref, line_ref, lined_ref,
    fsend_sem, frecv_sem, lsend_sem, lrecv_sem, wsend_sem, wrecv_sem, ksend_sem, krecv_sem,
    bsend_sem, brecv_sem, rsend_sem, rrecv_sem, psend_sem, precv_sem, ysend_sem, yrecv_sem,
    zsend_sem, zrecv_sem, fysend_sem, fyrecv_sem, fzsend_sem, fzrecv_sem, in_sem,
):
    seq, pair = lax.axis_index("seq"), lax.axis_index("pair")
    other = (seq, 1 - pair)
    yx, z = seq // DEPTH, lax.rem(seq, DEPTH)
    width = PLANE * BOUND
    rest = pl.ds(1, PLANE - 1)

    def on_line(i):
        return (yx * DEPTH + lax.rem(z + i, DEPTH), pair)

    def in_plane(m):
        return (lax.rem(yx + m, PLANE) * DEPTH + z, pair)

    def remote(source, target, send_sem, recv_sem, to):
        return pltpu.make_async_remote_copy(
            src_ref=source, dst_ref=target, send_sem=send_sem, recv_sem=recv_sem,
            device_id=to, device_id_type=MESH,
        )

    barrier = pltpu.get_barrier_semaphore()
    for i in range(1, DEPTH):
        pl.semaphore_signal(barrier, inc=1, device_id=on_line(i), device_id_type=MESH)
    for m in range(1, PLANE):
        pl.semaphore_signal(barrier, inc=1, device_id=in_plane(m), device_id_type=MESH)
    pl.semaphore_signal(barrier, inc=1, device_id=other, device_id_type=MESH)

    loads = [
        pltpu.make_async_copy(source, target, in_sem.at[n])
        for n, (source, target) in enumerate(
            (
                (cluster_in, cluster_ref), (slot_in, slot_ref), (q_in, q_ref), (g_in, g_ref),
                (kv_in, kvin_ref), (x_in, x_ref),
            )
        )
    ]
    for load in loads:
        load.start()
    for load in loads[:2]:
        load.wait()

    def in_lanes(ref):
        return jnp.concatenate([ref[h : h + 1, :] for h in range(H)], axis=1)

    cluster = in_lanes(cluster_ref)
    slot = in_lanes(slot_ref)
    owner = lax.shift_right_logical(cluster, 3)
    local = (cluster & (CL_DEV - 1)) * HALF + (slot & (HALF - 1))
    before = one_hot(iota((TOK, TOK), 0) < iota((TOK, TOK), 1))
    base = jnp.zeros((GROUPS, 1), F32)
    ranks = []
    for h in range(H):
        mine = owner[:, h * TOK : (h + 1) * TOK]
        pick = jnp.where(iota((GROUPS, TOK), 0) == mine, 1.0, 0.0)
        count = dot(pick.astype(BF16), before) + base
        ranks.append(jnp.sum(pick * count, axis=0, keepdims=True))
        base = base + jnp.sum(pick, axis=1, keepdims=True)
    rank = jnp.concatenate(ranks, axis=1).astype(jnp.int32)
    place = (owner & (DEPTH - 1)) * width + lax.shift_right_logical(owner, 3) * BOUND + rank
    in_row = jnp.where(iota((32, ROWS), 0) == lax.shift_right_logical(place, 7), 1.0, 0.0)
    in_lane = one_hot(iota((128, ROWS), 0) == (place & 127))
    token = iota((1, ROWS), 1) & (TOK - 1)
    parts = [lax.shift_right_logical(local, 6), local & 63, token]
    stacked = [(in_row * part.astype(F32)).astype(BF16) for part in parts] + [in_row.astype(BF16)]
    found = dot_t(jnp.concatenate(stacked, axis=0), in_lane)
    label = jnp.where(
        found[96:128] > 0.5, (found[0:32] * 64.0 + found[32:64]) * 128.0 + found[64:96], -1.0
    ).astype(jnp.int32)
    for i in range(DEPTH):
        zlab_ref[i] = label[4 * i : 4 * i + 4, :]
    for load in loads[2:]:
        load.wait()
    for h in range(H):
        cut = slice(h * HD, (h + 1) * HD)
        flat_ref[h * TOK : (h + 1) * TOK, :] = jnp.concatenate([q_ref[:, cut], g_ref[:, cut]], axis=1)
    def pack(i):
        to = lax.rem(z + i, DEPTH)
        hot = one_hot(iota((width, ROWS), 0) == place - to * width)
        zsend_ref[i] = dot(hot, flat_ref[...]).astype(BF16)

    for i in ORDER[1:EARLY]:
        pack(i)

    def z_copy(i, kind):
        to = lax.rem(z + i, DEPTH)
        source, target = (
            (zlab_ref.at[to], zlabgot_ref.at[i]),
            (kvin_ref, zkv_ref.at[i]),
            (zsend_ref.at[i], zgot_ref.at[i]),
        )[kind]
        return remote(source, target, fsend_sem.at[i, kind], frecv_sem.at[i, kind], on_line(i))

    pl.semaphore_wait(barrier, DEPTH - 1 + PLANE - 1 + 1)
    for i in ORDER[1:]:
        z_copy(i, 0).start()
    for n, i in enumerate(ORDER[1:], 1):
        if n >= EARLY:
            pack(i)
        z_copy(i, 1).start()
        z_copy(i, 2).start()
    pack(0)

    def row_copy(i, m):
        to = lax.rem(yx + m, PLANE)
        return remote(
            fwd_ref.at[i, to], rows_ref.at[i, m], wsend_sem.at[i], wrecv_sem.at[i], in_plane(m)
        )

    def all_rows(i):
        return remote(
            fwd_ref.at[i, rest], rows_ref.at[i, rest], wsend_sem.at[i], wrecv_sem.at[i], other
        )

    def pass_on(i):
        if i:
            z_copy(i, 1).wait_recv()
            z_copy(i, 2).wait_recv()
        labels = jnp.concatenate([zlabgot_ref[i, g : g + 1, :] for g in range(4)], axis=1)
        hot = one_hot(iota((TOK, width), 0) == (labels & (TOK - 1)))
        pairs = t_dot(hot, zkv_ref[i] if i else kvin_ref[...]).astype(BF16)
        rows = zgot_ref[i] if i else zsend_ref[0]
        fwd_ref[i] = jnp.concatenate([rows, pairs], axis=1).reshape(PLANE, BOUND, 4 * HD)

        def send(m, carry):
            row_copy(i, m).start()
            return carry

        lax.fori_loop(1, PLANE, send, 0)
        rows_ref[i, 0] = fwd_ref[i, yx]

    zlabgot_ref[0] = zlab_ref[z]
    pass_on(0)

    for i in ORDER[1:]:
        z_copy(i, 0).wait_recv()
    for i in range(DEPTH):
        for g in range(4):
            group_ref[g, i : i + 1, :] = zlabgot_ref[i, g : g + 1, :]

    def label_copy(m):
        to = lax.rem(yx + m, PLANE)
        return remote(
            group_ref.at[to // 4], plab_ref.at[m], lsend_sem.at[m], lrecv_sem.at[m], in_plane(m)
        )

    for m in range(1, PLANE):
        label_copy(m).start()
    plab_ref[0] = group_ref[yx // 4]

    pass_on(ORDER[1])
    for m in range(1, PLANE):
        label_copy(m).wait_recv()
    quarter = lax.rem(yx, 4)
    lanes = []
    live = jnp.zeros((SLOTS // 128, 128), F32)
    for i in range(DEPTH):
        given = plab_ref[:, i, :]
        mine = given[:, 3 * BOUND :]
        for g in range(3):
            mine = jnp.where(quarter == g, given[:, g * BOUND : (g + 1) * BOUND], mine)
        lane = jnp.concatenate([mine[m : m + 1, :] for m in range(PLANE)], axis=1)
        lane = lax.shift_right_arithmetic(lane, 7)
        lanes.append(lane)
        live = live + dot_t(
            one_hot(iota((SLOTS // 128, width), 0) == lax.shift_right_arithmetic(lane, 7)),
            one_hot(iota((128, width), 0) == (lane & 127)),
        )
    for c in range(CL_DEV):
        live_ref[c] = live[4 * c : 4 * c + 4, :]
    live_copy = remote(
        live_ref, live2_ref, ksend_sem.at[CL_DEV], krecv_sem.at[CL_DEV], other
    )
    live_copy.start()

    def key_copy(c):
        return remote(kv_ref.at[c], kv2_ref.at[c], ksend_sem.at[c], krecv_sem.at[c], other)

    def arrange(i, first, last):
        all_rows(i).wait_recv()
        lane = lanes[i]
        for b in range(CL_DEV):
            hot = one_hot(iota((HALF, width), 0) == lane - b * HALF)
            term = dot(hot, rows_ref[i].reshape(width, 4 * HD))
            if first:
                total_ref[b] = term
            elif not last:
                total_ref[b] += term
            else:
                done = (total_ref[b] + term).astype(BF16)
                qg_ref[b] = done[:, : 2 * HD]
                kv_ref[b] = done[:, 2 * HD :]
                key_copy(b).start()

    x_copy = remote(xt_ref.at[1 - pair], xo_ref, psend_sem.at[0], precv_sem.at[0], other)

    def turn_x():
        position = iota((512, 1024), 0)
        for p in range(2):
            column = lax.shift_right_logical(position, 2) * 8 + 4 * p + (position & 3)
            xt_ref[p] = dot_t(one_hot(iota((512, 1024), 1) == column), x_ref[...]).astype(BF16)
        x_copy.start()

    def join_x():
        x_copy.wait()
        both = jnp.concatenate([xt_ref[pair], xo_ref[...]], axis=1)
        xall_ref[0] = both
        position = iota((512, 512), 0)
        row = (lax.shift_right_logical(position, 2) & (PLANE - 1)) * 32
        row = row + lax.shift_right_logical(position, 6) * 4 + (position & 3)
        xall_ref[1] = dot(one_hot(iota((512, 512), 1) == row), both).astype(BF16)

    def find_targets():
        for h in range(H):
            cut = slice(h * TOK, (h + 1) * TOK)
            to = owner[:, cut]
            line = (to + (DEPTH - z)) & (DEPTH - 1)
            plane = (lax.shift_right_logical(to, 3) + (PLANE - yx)) & (PLANE - 1)
            target = line * (width // 2) + plane * (BOUND // 2) + (rank[:, cut] & (BOUND // 2 - 1))
            target = jnp.broadcast_to(target, (TOK, TOK)).T
            target_ref[cut, :] = target

    for n in range(2, DEPTH + LAG):
        if n < DEPTH:
            pass_on(ORDER[n])
        if n >= LAG:
            arrange(ORDER[n - LAG], n == LAG, n == DEPTH + LAG - 1)
        if n == 3:
            turn_x()
        if n == 4:
            find_targets()
        if n == 5:
            join_x()

    live_copy.wait()
    for c in range(CL_DEV):
        if c % JOINT == 0:
            for e in range(c, c + JOINT):
                key_copy(e).wait_recv()
        queries = qg_ref[c, :, :HD] * BF16(HD**-0.5)
        grads = qg_ref[c, :, HD:]
        keys = jnp.concatenate([kv_ref[c, :, :HD], kv2_ref[c, :, :HD]], axis=0)
        values = jnp.concatenate([kv_ref[c, :, HD:], kv2_ref[c, :, HD:]], axis=0)
        alive = jnp.concatenate(
            [ref[c, r : r + 1, :] for ref in (live_ref, live2_ref) for r in range(4)], axis=1
        )
        scores = dot_t(queries, keys) + jnp.where(alive > 0.5, 0.0, -1e30)
        prob_grad = dot_t(grads, values)
        weights = jnp.exp(scores - jnp.max(scores, axis=1, keepdims=True))
        inverse = 1.0 / jnp.sum(weights, axis=1, keepdims=True)
        row_dot = jnp.sum(weights * prob_grad, axis=1, keepdims=True) * inverse
        score_grad = (weights * (prob_grad - row_dot) * (inverse * (HD**-0.5))).astype(BF16)
        grads_ref[
            (c % 2) * HALF : (c % 2 + 1) * HALF, (c // 2) * HD : (c // 2 + 1) * HD
        ] = dot(score_grad, keys).astype(BF16)

    def back_copy(i):
        source, target = (back_ref, zback_ref) if i in Z_FIRST else (zback_ref, got_ref)
        return remote(
            source.at[i], target.at[i], bsend_sem.at[i], brecv_sem.at[i], on_line(DEPTH - i)
        )

    def return_copy(i, m):
        source, target = (zback_ref, got_ref) if i in Z_FIRST or not i else (back_ref, zback_ref)
        return remote(
            source.at[i, m], target.at[i, m], rsend_sem.at[i], rrecv_sem.at[i], in_plane(PLANE - m)
        )

    def all_returns(i):
        source, target = (zback_ref, got_ref) if i in Z_FIRST or not i else (back_ref, zback_ref)
        return remote(
            source.at[i, rest], target.at[i, rest], rsend_sem.at[i], rrecv_sem.at[i], other
        )

    def return_all(i):
        def send(m, carry):
            return_copy(i, m).start()
            return carry

        lax.fori_loop(1, PLANE, send, 0)

    for i in RETURN:
        labels = jnp.broadcast_to(lanes[i], (128, width)).T
        low = labels & 1023
        hot = jnp.concatenate(
            [one_hot(low == iota((width, 128), 1) + 128 * b) for b in range(8)], axis=1
        )
        found = dot(hot, grads_ref[...])
        high = lax.shift_right_arithmetic(labels[:, :HD], 10)
        row = jnp.zeros((width, HD), F32)
        for a in range(4):
            row = row + jnp.where(high == a, found[:, a * HD : (a + 1) * HD], 0.0)
        row = row.reshape(PLANE, BOUND, HD)
        row = jnp.concatenate([row[:, : BOUND // 2], row[:, BOUND // 2 :]], axis=2).astype(BF16)
        if i == 0:
            zback_ref[0] = row
            return_all(0)
            got_ref[0, 0] = row[0]
        elif i in Z_FIRST:
            back_ref[i] = row
            back_copy(i).start()
        else:
            back_ref[i] = row
            return_all(i)
            zback_ref[i, 0] = row[0]

    def take(i, first):
        if i in Z_FIRST or not i:
            all_returns(i).wait_recv()
        else:
            back_copy(i).wait_recv()
        half = width // 2
        term = dot(
            hot_ref[:, i * half : (i + 1) * half], got_ref[i].reshape(half, 2 * HD)
        )
        if first:
            found_ref[...] = term
        else:
            found_ref[...] += term

    def mark(i):
        for b in range(i * width // 2, (i + 1) * width // 2, 128):
            hot_ref[:, b : b + 128] = one_hot(target_ref[...] == iota((ROWS, 128), 1) + b)

    mark(0)
    for i in RELAY:
        if i in Z_FIRST:
            back_copy(i).wait_recv()
            return_all(i)
            got_ref[i, 0] = zback_ref[i, 0]
        else:
            all_returns(i).wait_recv()
            back_copy(i).start()
        mark(i)
    for n, i in enumerate(TAKE):
        take(i, n == 0)

    def g_copy(n):
        cut = pl.ds(n * PIECE, PIECE)
        return remote(
            wide_ref.at[0, :, cut], wide_ref.at[1, :, cut], psend_sem.at[1 + n],
            precv_sem.at[1 + n], other,
        )

    for h in range(0, H, 2):
        pieces = []
        for e in range(2):
            cut = slice((h + e) * TOK, (h + e + 1) * TOK)
            upper = (jnp.broadcast_to(rank[:, cut], (TOK, TOK)).T[:, :HD] & (BOUND // 2)) > 0
            piece = found_ref[cut, :]
            pieces.append(jnp.where(upper, piece[:, HD:], piece[:, :HD]))
        wide_ref[0, :, h * HD : (h + 2) * HD] = jnp.concatenate(pieces, axis=1).astype(BF16)
        if (h + 2) * HD % PIECE == 0:
            g_copy(h * HD // PIECE).start()

    def first_line(i):
        return remote(
            fline_ref.at[lax.rem(z + i, DEPTH)], flined_ref.at[i - 1], fzsend_sem.at[i - 1],
            fzrecv_sem.at[i - 1], on_line(i),
        )

    def first_plane(m):
        return remote(
            fplane_ref.at[lax.rem(yx + m, PLANE)], fplaned_ref.at[m - 1], fysend_sem.at[m - 1],
            fyrecv_sem.at[m - 1], in_plane(m),
        )

    def plane_copy(i):
        return remote(
            part_ref.at[lax.rem(yx + i, PLANE)], plane_ref.at[i - 1], ysend_sem.at[i - 1],
            yrecv_sem.at[i - 1], in_plane(i),
        )

    def line_copy(i):
        return remote(
            line_ref.at[lax.rem(z + i, DEPTH)], lined_ref.at[i - 1], zsend_sem.at[i - 1],
            zrecv_sem.at[i - 1], on_line(i),
        )

    def summed(n, order):
        g_copy(n).wait()
        columns = wide_ref[:, :, n * PIECE : (n + 1) * PIECE].reshape(2 * TOK, PIECE)
        return dot(xall_ref[order], columns).astype(BF16)

    fline_ref[...] = summed(0, 1).reshape(DEPTH, 4 * PLANE, PIECE)
    for i in range(1, DEPTH):
        first_line(i).start()
    for n in range(1, 1024 // PIECE):
        part_ref[:, :, (n - 1) * PIECE : n * PIECE] = summed(n, 0).reshape(PLANE, 32, PIECE)
        cut = pl.ds((n - 1) * PIECE, PIECE)
        for i in range(1, PLANE):
            remote(
                part_ref.at[lax.rem(yx + i, PLANE), :, cut], plane_ref.at[i - 1, :, cut],
                ysend_sem.at[i - 1], yrecv_sem.at[i - 1], in_plane(i),
            ).start()
    total = fline_ref[z].astype(F32)
    for i in range(1, DEPTH):
        first_line(i).wait_recv()
        total = total + flined_ref[i - 1].astype(F32)
    for m in range(PLANE):
        rows = total[4 * m : 4 * m + 4, :]
        fplane_ref[m] = jnp.concatenate([rows[:, : PIECE // 2], rows[:, PIECE // 2 :]], axis=0)
    for m in range(1, PLANE):
        first_plane(m).start()
    half = (1024 - PIECE) // 2
    total = part_ref[yx].astype(F32)
    for i in range(1, PLANE):
        plane_copy(i).wait_recv()
        total = total + plane_ref[i - 1].astype(F32)
    for i in range(DEPTH):
        rows = total[4 * i : 4 * i + 4, :]
        line_ref[i] = jnp.concatenate([rows[:, :half], rows[:, half:]], axis=0)
    for i in range(1, DEPTH):
        line_copy(i).start()
    result = fplane_ref[yx]
    for m in range(1, PLANE):
        first_plane(m).wait_recv()
        result = result + fplaned_ref[m - 1]
    out_ref[:, :PIECE] = jnp.concatenate([result[:4], result[4:]], axis=1)
    result = line_ref[z]
    for i in range(1, DEPTH):
        line_copy(i).wait_recv()
        result = result + lined_ref[i - 1]
    out_ref[:, PIECE:] = jnp.concatenate([result[:4], result[4:]], axis=1)

    for i in range(1, DEPTH):
        for kind in range(3):
            z_copy(i, kind).wait_send()
        back_copy(i).wait_send()
        line_copy(i).wait_send()
        first_line(i).wait_send()
    for i in range(DEPTH):
        all_rows(i).wait_send()
        key_copy(i).wait_send()
        all_returns(i).wait_send()
    for m in range(1, PLANE):
        label_copy(m).wait_send()
        plane_copy(m).wait_send()
        first_plane(m).wait_send()


def whole(cluster_of, slot_of, queries, out_grad, key_value, tokens_in):
    width = PLANE * BOUND
    dma = pltpu.SemaphoreType.DMA
    return pl.pallas_call(
        whole_kernel,
        out_shape=jax.ShapeDtypeStruct((4, 1024), F32),
        in_specs=[pl.BlockSpec(memory_space=pl.ANY)] * 6,
        out_specs=VMEM,
        scratch_shapes=[
            pltpu.VMEM((H, TOK), jnp.int32),
            pltpu.VMEM((H, TOK), jnp.int32),
            pltpu.VMEM((TOK, H * HD), BF16),
            pltpu.VMEM((TOK, H * HD), BF16),
            pltpu.VMEM((TOK, 2 * HD), BF16),
            pltpu.VMEM((TOK, 1024), BF16),
            pltpu.VMEM((ROWS, 2 * HD), BF16),
            pltpu.VMEM((DEPTH, width, 2 * HD), BF16),
            pltpu.VMEM((DEPTH, width, 2 * HD), BF16),
            pltpu.VMEM((DEPTH, TOK, 2 * HD), BF16),
            pltpu.VMEM((DEPTH, 4, 128), jnp.int32),
            pltpu.VMEM((DEPTH, 4, 128), jnp.int32),
            pltpu.VMEM((4, DEPTH, 128), jnp.int32),
            pltpu.VMEM((PLANE, DEPTH, 128), jnp.int32),
            pltpu.VMEM((DEPTH, PLANE, BOUND, 4 * HD), BF16),
            pltpu.VMEM((DEPTH, PLANE, BOUND, 4 * HD), BF16),
            pltpu.VMEM((CL_DEV, HALF, 4 * HD), F32),
            pltpu.VMEM((CL_DEV, HALF, 2 * HD), BF16),
            pltpu.VMEM((CL_DEV, HALF, 2 * HD), BF16),
            pltpu.VMEM((CL_DEV, 4, 128), F32),
            pltpu.VMEM((CL_DEV, HALF, 2 * HD), BF16),
            pltpu.VMEM((CL_DEV, 4, 128), F32),
            pltpu.VMEM((2 * HALF, 4 * HD), BF16),
            pltpu.VMEM((DEPTH, PLANE, BOUND // 2, 2 * HD), BF16),
            pltpu.VMEM((DEPTH, PLANE, BOUND // 2, 2 * HD), BF16),
            pltpu.VMEM((DEPTH, PLANE, BOUND // 2, 2 * HD), BF16),
            pltpu.VMEM((ROWS, GROUPS * BOUND // 2), BF16),
            pltpu.VMEM((ROWS, 128), jnp.int32),
            pltpu.VMEM((ROWS, 2 * HD), F32),
            pltpu.VMEM((2, 512, TOK), BF16),
            pltpu.VMEM((512, TOK), BF16),
            pltpu.VMEM((2, 512, 2 * TOK), BF16),
            pltpu.VMEM((2, TOK, 1024), BF16),
            pltpu.VMEM((DEPTH, 4 * PLANE, PIECE), BF16),
            pltpu.VMEM((DEPTH - 1, 4 * PLANE, PIECE), BF16),
            pltpu.VMEM((PLANE, 8, PIECE // 2), F32),
            pltpu.VMEM((PLANE - 1, 8, PIECE // 2), F32),
            pltpu.VMEM((PLANE, 32, 1024 - PIECE), BF16),
            pltpu.VMEM((PLANE - 1, 32, 1024 - PIECE), BF16),
            pltpu.VMEM((DEPTH, 8, (1024 - PIECE) // 2), F32),
            pltpu.VMEM((DEPTH - 1, 8, (1024 - PIECE) // 2), F32),
            dma((DEPTH, 3)),
            dma((DEPTH, 3)),
            dma((PLANE,)),
            dma((PLANE,)),
            dma((DEPTH,)),
            dma((DEPTH,)),
            dma((CL_DEV + 1,)),
            dma((CL_DEV + 1,)),
            dma((DEPTH,)),
            dma((DEPTH,)),
            dma((DEPTH,)),
            dma((DEPTH,)),
            dma((1 + 1024 // PIECE,)),
            dma((1 + 1024 // PIECE,)),
            dma((PLANE - 1,)),
            dma((PLANE - 1,)),
            dma((DEPTH - 1,)),
            dma((DEPTH - 1,)),
            dma((PLANE - 1,)),
            dma((PLANE - 1,)),
            dma((DEPTH - 1,)),
            dma((DEPTH - 1,)),
            dma((6,)),
        ],
        compiler_params=params(0),
    )(cluster_of, slot_of, queries, out_grad, key_value, tokens_in)


def on_device(tokens_in, queries, key_value, out_grad, cluster_of, slot_of):
    return whole(cluster_of.T, slot_of.T, queries, out_grad, key_value, tokens_in)


def solution(mesh):
    spec = P(("seq", "pair"), None)
    return jax.shard_map(
        on_device, mesh=mesh, in_specs=(spec,) * 6, out_specs=spec, check_vma=False
    )
```
